32 devices in a mesh: wide: 16 (over z, y, core), narrow: 2 (over x).
Axes of the slice: x: 2, y: 2, z: 4, core: 2. Of those that a mesh axis runs over, the one named last changes fastest.
Arguments:
- inputs: bfloat16 [32, 1024, 768], P('wide', 'narrow'), may hold values from -6 to 6
- out_grad: bfloat16 [32, 1024, 768], P('wide', 'narrow'), may hold values from -6 to 6
- source_id: int32 [32], P('wide'), may hold values from 0 to 2
- source_weight: float32 [3], replicated, may hold values from 0.25 to 4
- gain_attn: bfloat16 [768], P(('wide', 'narrow')), may hold values from 0.5 to 1.5
- gain_mlp: bfloat16 [768], P(('wide', 'narrow')), may hold values from 0.5 to 1.5
- w_query: bfloat16 [768, 768], P(('wide', 'narrow')), may hold values from -0.3125 to 0.3125
- w_key: bfloat16 [768, 768], P(('wide', 'narrow')), may hold values from -0.21875 to 0.21875
- w_value: bfloat16 [768, 768], P(('wide', 'narrow')), may hold values from -0.21875 to 0.21875
- w_attn_out: bfloat16 [768, 768], P(('wide', 'narrow')), may hold values from -1.25 to 1.25
- w_gate: bfloat16 [768, 2048], P(('wide', 'narrow')), may hold values from -0.21875 to 0.21875
- w_up: bfloat16 [768, 2048], P(('wide', 'narrow')), may hold values from -0.21875 to 0.21875
- w_down: bfloat16 [2048, 768], P(('wide', 'narrow')), may hold values from -0.125 to 0.125
Outputs:
- activations: bfloat16 [32, 1024, 768], P('wide', 'narrow')
- input_grad: float32 [32, 1024, 768], P('wide', 'narrow')
- grad_gain_attn: float32 [768], P(('wide', 'narrow'))
- grad_gain_mlp: float32 [768], P(('wide', 'narrow'))
- grad_query: float32 [768, 768], P(('wide', 'narrow'))
- grad_key: float32 [768, 768], P(('wide', 'narrow'))
- grad_value: float32 [768, 768], P(('wide', 'narrow'))
- grad_attn_out: float32 [768, 768], P(('wide', 'narrow'))
- grad_gate: float32 [768, 2048], P(('wide', 'narrow'))
- grad_up: float32 [768, 2048], P(('wide', 'narrow'))
- grad_down: float32 [2048, 768], P(('wide', 'narrow'))
The draws below stay inside these ranges and needn't reach their ends.
All inputs are finite; a program needn't handle non-finite values.
Results may differ from the reference program's by a relative error of at most 0.015.
Values may be sent and summed in bfloat16 or wider, within the bound.
No kernel may reach another device: no remote copies, remote signals or barrier semaphores. Data moves between devices by JAX's collectives and lax.ppermute only.
A program may use at most 256 MiB of HBM per device.

```python
import math
import jax
import jax.numpy as jnp
from jax import lax

D = 768
HEADS = 12
HEAD_DIM = 64
FF = 2048
SOURCES = 3
SEQ = 1024
PLOTS = 32


def set_ends(drawn, stream_key, least, largest):
    extent = drawn.shape
    spot = [jax.random.randint(jax.random.fold_in(stream_key, axis), (), 0, extent[axis]) for axis in range(len(extent))]
    drawn = drawn.at[tuple(spot)].set(least)
    longest = extent.index(max(extent))
    spot[longest] = (spot[longest] + 1) % extent[longest]
    return drawn.at[tuple(spot)].set(largest)


def block_levels(own_key, dims, split, smallest, largest):
    loudness, own = 1.0, jax.random.fold_in(own_key, 6)
    for axis_at, shards_of in split:
        draws = jnp.exp(jax.random.uniform(jax.random.fold_in(own, axis_at), (shards_of,), jnp.float32, smallest / len(split), largest / len(split)))
        loudness = loudness * jnp.repeat(draws, dims[axis_at] // shards_of).reshape([-1 if axis == axis_at else 1 for axis in range(len(dims))])
    return loudness


def scatter_about(own_key, dims, deviation, bound, split=(), held_as=jnp.bfloat16):
    result = deviation * jax.random.normal(own_key, dims, jnp.float32)
    if split:
        result = result * block_levels(own_key, dims, split, -0.22, 0.18)
    return jnp.clip(result, -bound, bound).astype(held_as)


def setup_inputs(seed: int = 0) -> dict:
    seeds = jax.random.split(jax.random.key(seed), 14)
    return {
        "inputs": scatter_about(seeds[0], (PLOTS, SEQ, D), 1.0, 6.0, ((0, 16), (1, 2))),
        "out_grad": scatter_about(seeds[1], (PLOTS, SEQ, D), 1.0, 6.0, ((0, 16), (1, 2))),
        "source_id": set_ends(jax.random.randint(seeds[2], (PLOTS,), 0, SOURCES), jax.random.fold_in(seeds[2], 1), 0, SOURCES - 1).astype(jnp.int32),
        "source_weight": jnp.clip(jnp.exp(jax.random.uniform(seeds[3], (SOURCES,), jnp.float32, math.log(0.25), math.log(4.0))), 0.25, 4.0),
        "gain_attn": jnp.clip(1.0 + 0.1 * jax.random.normal(seeds[4], (D,), jnp.float32), 0.5, 1.5).astype(jnp.bfloat16),
        "gain_mlp": jnp.clip(1.0 + 0.1 * jax.random.normal(seeds[5], (D,), jnp.float32), 0.5, 1.5).astype(jnp.bfloat16),
        "w_query": scatter_about(seeds[6], (D, D), (D // 2) ** -0.5, 0.3125, ((0, 32),)),
        "w_key": scatter_about(seeds[7], (D, D), D ** -0.5, 0.21875, ((0, 32),)),
        "w_value": scatter_about(seeds[8], (D, D), D ** -0.5, 0.21875, ((0, 32),)),
        "w_attn_out": scatter_about(seeds[9], (D, D), (D // 32) ** -0.5, 1.25, ((0, 32),)),
        "w_gate": scatter_about(seeds[10], (D, FF), D ** -0.5, 0.21875, ((0, 32),)),
        "w_up": scatter_about(seeds[11], (D, FF), D ** -0.5, 0.21875, ((0, 32),)),
        "w_down": scatter_about(seeds[12], (FF, D), FF ** -0.5, 0.125, ((0, 32),)),
    }


@jax.custom_vjp
def low(v):
    return lax.optimization_barrier(v.astype(jnp.bfloat16)).astype(jnp.float32)

@jax.custom_vjp
def low_back(v):
    return v

def low_keep(v):
    return (low(v), None)

def low_pass(kept, grad):
    return (grad,)

def back_keep(v):
    return (v, None)

def back_low(kept, grad):
    return (low(grad),)
low.defvjp(low_keep, low_pass)
low_back.defvjp(back_keep, back_low)
EPS = 1e-06
HIGH = lax.Precision.HIGHEST

def rms(value, gain):
    return value * lax.rsqrt(lax.optimization_barrier(jnp.mean(value * value, -1, keepdims=True)) + EPS) * gain

def matmul(left, right):
    return jnp.dot(left, right, precision=HIGH)

def plot_forward(x, gain_one, gain_two, wq, wk, wv, wo, wg, wu, wd):
    n1 = low(rms(x, gain_one))
    q = low_back(low(matmul(n1, wq)))
    k = low_back(low(matmul(n1, wk)))
    v = low_back(low(matmul(n1, wv)))
    block = min(512, SEQ)
    q_blocks = q.reshape(SEQ // block, block, HEADS, HEAD_DIM)
    k_heads = k.reshape(SEQ, HEADS, HEAD_DIM)
    v_heads = v.reshape(SEQ, HEADS, HEAD_DIM)
    scale = HEAD_DIM ** (-0.5)

    def attend(q_block):
        scores = low_back(jnp.einsum('bhd,shd->hbs', q_block, k_heads, precision=HIGH) * scale)
        probs = jax.nn.softmax(scores, -1)
        return jnp.einsum('hbs,shd->bhd', low(probs), v_heads, precision=HIGH)
    heads_out = lax.map(jax.checkpoint(attend), q_blocks).reshape(SEQ, D)
    attn = low_back(low(heads_out))
    x1 = x + low_back(matmul(attn, wo))
    n2 = low(rms(x1, gain_two))
    gate = low_back(matmul(n2, wg))
    up = low_back(matmul(n2, wu))
    hidden = low(jax.nn.gelu(gate, approximate=True) * up)
    return x1 + low_back(matmul(hidden, wd))

def reference(inputs, out_grad, source_id, source_weight, gain_attn, gain_mlp, w_query, w_key, w_value, w_attn_out, w_gate, w_up, w_down):
    weights = tuple((a.astype(jnp.float32) for a in (gain_attn, gain_mlp, w_query, w_key, w_value, w_attn_out, w_gate, w_up, w_down)))
    onehot = (source_id[:, None] == jnp.arange(SOURCES, dtype=jnp.int32)[None, :]).astype(jnp.float32)
    plot_scale = lax.optimization_barrier(jnp.sum(onehot * source_weight[None, :], -1))

    def step(totals, item):
        x_plot, g_plot, s_plot = item
        out, back = jax.vjp(plot_forward, x_plot.astype(jnp.float32), *weights)
        grads = back(g_plot.astype(jnp.float32) * s_plot)
        new_totals = tuple((a + b for a, b in zip(totals, grads[1:])))
        return (new_totals, (out.astype(jnp.bfloat16), grads[0]))
    start = tuple((jnp.zeros(a.shape, jnp.float32) for a in weights))
    totals, (outs, input_grads) = lax.scan(step, start, (inputs, out_grad, plot_scale))
    return (outs, input_grads, totals[0], totals[1], totals[2], totals[3], totals[4], totals[5], totals[6], totals[7], totals[8])
```

```python
import functools
import math

import jax
import jax.numpy as jnp
from jax import lax
from jax.experimental import pallas as pl
from jax.experimental.pallas import tpu as pltpu
from jax.sharding import PartitionSpec as P

HEADS = 12
HEAD_DIM = 64


EPS = 1e-06
HIGH = lax.Precision.HIGHEST


def rms(value, gain):
    return value * lax.rsqrt(jnp.mean(value * value, -1, keepdims=True) + EPS) * gain


def matmul(left, right):
    return jnp.dot(left, right, preferred_element_type=jnp.float32)


def matmul_tn(left, right):
    return lax.dot_general(
        left, right, (((0,), (0,)), ((), ())), preferred_element_type=jnp.float32
    )


def matmul_nt(left, right):
    return lax.dot_general(
        left, right, (((1,), (1,)), ((), ())), preferred_element_type=jnp.float32
    )


def attend(items):
    query, keys, values = items
    rows = query.shape[0]
    total = keys.shape[0]
    scale = HEAD_DIM ** (-0.5)
    q_heads = query.reshape(rows, HEADS, HEAD_DIM)
    k_heads = keys.reshape(total, HEADS, HEAD_DIM)
    v_heads = values.reshape(total, HEADS, HEAD_DIM)
    scores = (
        jnp.einsum("rhd,shd->hrs", q_heads, k_heads, preferred_element_type=jnp.float32) * scale
    )
    peak = jnp.max(scores, -1, keepdims=True)
    expo = jnp.exp(scores - peak)
    summed = jnp.sum(expo, -1, keepdims=True)
    probs_full = expo / summed
    probs = probs_full.astype(jnp.bfloat16)
    heads_out = jnp.einsum("hrs,shd->rhd", probs, v_heads, preferred_element_type=jnp.float32)
    exact_out = jnp.einsum("hrs,shd->rhd", probs_full, v_heads.astype(jnp.float32), precision=HIGH)
    log_total = (peak + jnp.log(summed))[:, :, 0]
    return (heads_out.reshape(rows, HEADS * HEAD_DIM), log_total, exact_out)


def attend_back(items):
    query, keys, values, log_total, d_out = items
    rows = query.shape[0]
    total = keys.shape[0]
    width = HEADS * HEAD_DIM
    scale = HEAD_DIM ** (-0.5)
    q_heads = query.reshape(rows, HEADS, HEAD_DIM)
    k_heads = keys.reshape(total, HEADS, HEAD_DIM)
    v_heads = values.reshape(total, HEADS, HEAD_DIM)
    d_heads = d_out.reshape(rows, HEADS, HEAD_DIM)
    scores = (
        jnp.einsum("rhd,shd->hrs", q_heads, k_heads, preferred_element_type=jnp.float32) * scale
    )
    probs = jnp.exp(scores - log_total[:, :, None])
    probs_low = probs.astype(jnp.bfloat16)
    d_probs = jnp.einsum("rhd,shd->hrs", d_heads, v_heads, preferred_element_type=jnp.float32)
    center = jnp.sum(d_probs * probs, -1, keepdims=True)
    d_scores = (probs * (d_probs - center)).astype(jnp.bfloat16)
    d_query = (
        jnp.einsum("hrs,shd->rhd", d_scores, k_heads, preferred_element_type=jnp.float32) * scale
    )
    d_keys = (
        jnp.einsum("hrs,rhd->shd", d_scores, q_heads, preferred_element_type=jnp.float32) * scale
    )
    d_values = jnp.einsum("hrs,rhd->shd", probs_low, d_heads, preferred_element_type=jnp.float32)
    return (
        d_query.reshape(rows, width),
        d_keys.reshape(total, width),
        d_values.reshape(total, width),
    )


def local(
    inputs,
    out_grad,
    source_id,
    source_weight,
    gain_attn,
    gain_mlp,
    w_query,
    w_key,
    w_value,
    w_attn_out,
    w_gate,
    w_up,
    w_down,
):
    plots, rows, width = inputs.shape
    gathered = (
        lax.all_gather(gain_attn, ("wide", "narrow"), axis=0, tiled=True),
        lax.all_gather(gain_mlp, ("wide", "narrow"), axis=0, tiled=True),
        lax.all_gather(w_query, ("wide", "narrow"), axis=0, tiled=True),
        lax.all_gather(w_key, ("wide", "narrow"), axis=0, tiled=True),
        lax.all_gather(w_value, ("wide", "narrow"), axis=0, tiled=True),
        lax.all_gather(w_attn_out, ("wide", "narrow"), axis=0, tiled=True),
        lax.all_gather(w_gate, ("wide", "narrow"), axis=0, tiled=True),
        lax.all_gather(w_up, ("wide", "narrow"), axis=0, tiled=True),
        lax.all_gather(w_down, ("wide", "narrow"), axis=0, tiled=True),
    )
    gain_one, gain_two, wq, wk, wv, wo, wg, wu, wd = gathered
    gain_one = gain_one.astype(jnp.float32)
    gain_two = gain_two.astype(jnp.float32)
    x_rows = inputs.astype(jnp.float32).reshape(plots * rows, width)
    n1 = rms(x_rows, gain_one).astype(jnp.bfloat16)
    query = matmul(n1, wq).astype(jnp.bfloat16)
    keys_own = matmul(n1, wk).astype(jnp.bfloat16).reshape(plots, rows, width)
    values_own = matmul(n1, wv).astype(jnp.bfloat16).reshape(plots, rows, width)
    keys_all, values_all = (
        lax.all_gather(keys_own, "narrow", axis=1, tiled=True),
        lax.all_gather(values_own, "narrow", axis=1, tiled=True),
    )
    query_plots = query.reshape(plots, rows, width)
    heads_out, log_total, exact_out = lax.map(attend, (query_plots, keys_all, values_all))
    attn = heads_out.reshape(plots * rows, width).astype(jnp.bfloat16)
    x1 = x_rows + matmul(attn, wo)
    n2 = rms(x1, gain_two).astype(jnp.bfloat16)
    gate = matmul(n2, wg)
    up = matmul(n2, wu)
    gate_act, gelu_back = jax.vjp(lambda u: jax.nn.gelu(u, approximate=True), gate)
    hidden = (gate_act * up).astype(jnp.bfloat16)
    activations = (x1 + matmul(hidden, wd)).astype(jnp.bfloat16).reshape(plots, rows, width)
    onehot = (
        source_id[:, None] == jnp.arange(source_weight.shape[0], dtype=jnp.int32)[None, :]
    ).astype(jnp.float32)
    plot_scale = jnp.sum(onehot * source_weight[None, :], -1)
    cotangent = (out_grad.astype(jnp.float32) * plot_scale[:, None, None]).reshape(
        plots * rows, width
    )
    again = (
        lax.all_gather(gain_attn, ("wide", "narrow"), axis=0, tiled=True),
        lax.all_gather(gain_mlp, ("wide", "narrow"), axis=0, tiled=True),
        lax.all_gather(w_query, ("wide", "narrow"), axis=0, tiled=True),
        lax.all_gather(w_key, ("wide", "narrow"), axis=0, tiled=True),
        lax.all_gather(w_value, ("wide", "narrow"), axis=0, tiled=True),
        lax.all_gather(w_attn_out, ("wide", "narrow"), axis=0, tiled=True),
        lax.all_gather(w_gate, ("wide", "narrow"), axis=0, tiled=True),
        lax.all_gather(w_up, ("wide", "narrow"), axis=0, tiled=True),
        lax.all_gather(w_down, ("wide", "narrow"), axis=0, tiled=True),
    )
    gain_one, gain_two, wq, wk, wv, wo, wg, wu, wd = again
    gain_one = gain_one.astype(jnp.float32)
    gain_two = gain_two.astype(jnp.float32)
    d_y = cotangent.astype(jnp.bfloat16)
    d_hidden = matmul_nt(d_y, wd)
    grad_down = matmul_tn(hidden, d_y)
    d_gate = gelu_back(d_hidden * up)[0].astype(jnp.bfloat16)
    d_up = (d_hidden * gate_act).astype(jnp.bfloat16)
    grad_gate = matmul_tn(n2, d_gate)
    grad_up = matmul_tn(n2, d_up)
    d_n2 = matmul_nt(d_gate, wg) + matmul_nt(d_up, wu)
    _, norm_two_back = jax.vjp(rms, x1, gain_two)
    d_x1_norm, grad_gain_mlp = norm_two_back(d_n2)
    d_x1 = cotangent + d_x1_norm
    d_attn = d_x1.astype(jnp.bfloat16)
    grad_attn_out = matmul_tn(attn, d_attn)
    d_out = matmul_nt(d_attn, wo).astype(jnp.bfloat16).reshape(plots, rows, width)
    keys_all, values_all = (
        lax.all_gather(keys_own, "narrow", axis=1, tiled=True),
        lax.all_gather(values_own, "narrow", axis=1, tiled=True),
    )
    d_query, d_keys_part, d_values_part = lax.map(
        attend_back, (query_plots, keys_all, values_all, log_total, d_out)
    )
    d_keys, d_values = (
        lax.psum_scatter(
            d_keys_part.astype(jnp.bfloat16), "narrow", scatter_dimension=1, tiled=True
        ).astype(jnp.float32),
        lax.psum_scatter(
            d_values_part.astype(jnp.bfloat16), "narrow", scatter_dimension=1, tiled=True
        ).astype(jnp.float32),
    )
    dq_low = d_query.reshape(plots * rows, width).astype(jnp.bfloat16)
    dk_low = d_keys.reshape(plots * rows, width).astype(jnp.bfloat16)
    dv_low = d_values.reshape(plots * rows, width).astype(jnp.bfloat16)
    grad_query = matmul_tn(n1, dq_low)
    grad_key = matmul_tn(n1, dk_low)
    grad_value = matmul_tn(n1, dv_low)
    d_n1 = matmul_nt(dq_low, wq) + matmul_nt(dk_low, wk) + matmul_nt(dv_low, wv)
    _, norm_one_back = jax.vjp(rms, x_rows, gain_one)
    d_x_norm, grad_gain_attn = norm_one_back(d_n1)
    input_grad = (d_x1 + d_x_norm).reshape(plots, rows, width)
    grads = (
        grad_gain_attn,
        grad_gain_mlp,
        grad_query,
        grad_key,
        grad_value,
        grad_attn_out,
        grad_gate,
        grad_up,
        grad_down,
    )
    shards = (
        lax.psum_scatter(grads[0], ("wide", "narrow"), scatter_dimension=0, tiled=True),
        lax.psum_scatter(grads[1], ("wide", "narrow"), scatter_dimension=0, tiled=True),
        lax.psum_scatter(grads[2], ("wide", "narrow"), scatter_dimension=0, tiled=True),
        lax.psum_scatter(grads[3], ("wide", "narrow"), scatter_dimension=0, tiled=True),
        lax.psum_scatter(grads[4], ("wide", "narrow"), scatter_dimension=0, tiled=True),
        lax.psum_scatter(grads[5], ("wide", "narrow"), scatter_dimension=0, tiled=True),
        lax.psum_scatter(grads[6], ("wide", "narrow"), scatter_dimension=0, tiled=True),
        lax.psum_scatter(grads[7], ("wide", "narrow"), scatter_dimension=0, tiled=True),
        lax.psum_scatter(grads[8], ("wide", "narrow"), scatter_dimension=0, tiled=True),
    )
    return (
        activations,
        input_grad,
        shards[0],
        shards[1],
        shards[2],
        shards[3],
        shards[4],
        shards[5],
        shards[6],
        shards[7],
        shards[8],
    )


F32 = jnp.float32
BF16 = jnp.bfloat16
PAIR = 2 * HEAD_DIM
MIB = 1 << 20
TILE = 256


def params(limit=60):
    return pltpu.CompilerParams(vmem_limit_bytes=limit * MIB)


def whole(shape):
    return pl.BlockSpec(shape, lambda *_: (0,) * len(shape), pipeline_mode=pl.Buffered(1))


SCALARS = pl.BlockSpec(memory_space=pltpu.SMEM)
APART = pl.BlockSpec(memory_space=pl.ANY)


def swap(value, mask, size):
    return lax.ppermute(value, "wide", [(i, i ^ mask) for i in range(size)])


def swap_x(value):
    return lax.ppermute(value, "narrow", [(0, 1), (1, 0)])


def by_side(side, first, second):
    return jnp.where(side == 0, first, second)


def after(value, *others):
    return lax.optimization_barrier((value, *others))[0]


def pair_up(piece, give, side):
    other = swap_x(give)
    return jnp.concatenate([by_side(side, piece, other), by_side(side, other, piece)], 0)


def spread_z(unit, size):
    return jnp.stack([unit] + [swap(unit, 4 * k, size) for k in range(1, size // 4)])


def spread_xy(stack, size):
    return swap_x(stack), swap(stack, 2, size)


PIECES = ((0, 0), (1, 0), (0, 1), (1, 1))
DOWN_PIECES = ((0, 0), (0, 1))


def listing(refs, places=PIECES):
    found = []
    for at, ref in enumerate(refs):
        x, y = places[at % len(places)]
        core = at // len(places)
        for k in range(ref.shape[0]):
            found.append((ref, k, x, 4 * k + 2 * y + core))
    return found


def chip_sum(keep, arrived, part, parts=4):
    groups = keep.shape[0] // parts
    at = slice(part * groups, (part + 1) * groups)
    return keep[at].astype(F32) + arrived[at].astype(F32)


def diagonal_of(keep, arrived):
    return chip_sum(keep, arrived, 3).astype(BF16)


def over_y_of(keep, arrived):
    return chip_sum(keep, arrived, 1).astype(BF16)


def over_x_of(keep, arrived, corner):
    return (chip_sum(keep, arrived, 2) + corner.astype(F32)).astype(BF16)


def collect_own(keep, arrived, sides, units):
    return [sum([part[k].astype(F32) for part in (arrived, *sides)], keep[k].astype(F32)) for k in units]


def settle_rows(total, side):
    half = total.shape[0] // 2
    other = swap_x(by_side(side, total[half:], total[:half]).astype(BF16)).astype(F32)
    return by_side(side, total[:half], total[half:]) + other


def settle(total, side):
    half = total.shape[0] // 2
    mine = by_side(side, total[:half], total[half:])
    other = swap_x(by_side(side, total[half:], total[:half]).astype(BF16)).astype(F32)
    return by_side(side, mine, other), by_side(side, other, mine)


def file_rows(keep, send, me, side, half, lanes, source):
    groups = keep.shape[0] // 4
    size = keep.shape[1]
    for rel in range(4 * groups):
        slot = ((half ^ side) * 2 + rel // 2 % 2) * groups + rel // 4
        start = pl.multiple_of((me ^ rel) * size, 8)
        block = source[pl.ds(start, size), :].astype(BF16)
        (send if rel % 2 else keep)[slot, :, lanes] = block


def pack_kernel(place_ref, gain_attn_ref, gain_mlp_ref, *refs):
    qkv_refs, mlp_refs = refs[:3], refs[3:6]
    unit_ref, own_ref, give_ref, wide_s = refs[6:]
    rows, width = qkv_refs[0].shape
    halves = []
    for h, gain_ref in enumerate((gain_attn_ref, gain_mlp_ref)):
        wide_s[...] = jnp.zeros_like(wide_s)
        wide_s[0:1, :rows] = gain_ref[...].astype(F32)
        columns = []
        for pair in range(h * width // PAIR // 2, (h + 1) * width // PAIR // 2):
            columns += [ref[:, pair * PAIR : (pair + 1) * PAIR] for ref in qkv_refs]
        gains = jnp.transpose(wide_s[...])[:rows]
        halves.append(jnp.concatenate([jnp.concatenate(columns, 1).astype(F32), gains], 1))
    unit_ref[...] = jnp.concatenate(halves, 0).astype(BF16)
    side = place_ref[1]
    done = 0
    for ref in mlp_refs:
        half = ref.shape[1] // 2
        lanes = slice(done, done + half)
        first, second = ref[:, :half], ref[:, half:]

        @pl.when(side == 0)
        def _():
            own_ref[:, lanes] = first
            give_ref[:, lanes] = second

        @pl.when(side == 1)
        def _():
            own_ref[:, lanes] = second
            give_ref[:, lanes] = first

        done += half


def pack(place, gains, qkv_weights, mlp_weights):
    rows, width = qkv_weights[0].shape
    cols = sum(w.shape[1] for w in mlp_weights) // 2
    whole_in = pl.BlockSpec(memory_space=pltpu.VMEM)
    return pl.pallas_call(
        pack_kernel,
        in_specs=[SCALARS] + [whole_in] * 8,
        out_specs=[whole_in] * 3,
        out_shape=[
            jax.ShapeDtypeStruct((2 * rows, 3 * width // 2 + 128), BF16),
            jax.ShapeDtypeStruct((rows, cols), BF16),
            jax.ShapeDtypeStruct((rows, cols), BF16),
        ],
        scratch_shapes=[pltpu.VMEM((128, 128), F32)],
        compiler_params=params(),
        cost_estimate=pl.CostEstimate(flops=0, bytes_accessed=MIB, transcendentals=0),
        name="pack",
    )(place, *[gain[None, :] for gain in gains], *qkv_weights, *mlp_weights)


TRIPLE = 3 * PAIR


def project_kernel(place_ref, x_ref, *refs):
    pieces, (qkv_ref, n1_ref, gain_ref, held, staged, sems) = refs[:8], refs[-6:]
    width = x_ref.shape[1]
    cols = 3 * width // 2

    @pl.when(pl.program_id(0) == 0)
    def _():
        me, side = place_ref[0], place_ref[1]
        pairs, rows = staged.shape[1:3]
        copies = []
        for at, (ref, k, x, rel) in enumerate(listing(pieces)):
            copies.append(pltpu.make_async_copy(ref.at[k], staged.at[side ^ x, me ^ rel], sems.at[at]))
        for copy in copies:
            copy.start()
        for copy in copies:
            copy.wait()
        own = rows // 2
        for pair in range(pairs):
            units = [staged[x, pair].astype(F32) for x in range(2)]
            for h in range(2):
                both_rows = jnp.concatenate([unit[h * own : (h + 1) * own] for unit in units], 0)
                held[h, pair * rows : (pair + 1) * rows, :] = both_rows.astype(BF16)
        for h in range(2):
            gain_ref[h * 8 : h * 8 + 8, :] = jnp.transpose(held[h, :, cols:].astype(F32))[:8]

    x = x_ref[...].astype(F32)
    root = lax.rsqrt(jnp.mean(x * x, -1, keepdims=True) + EPS)
    n1 = (x * root * gain_ref[0:1, :]).astype(BF16)
    n1_ref[...] = n1
    is_query = lax.broadcasted_iota(jnp.int32, (1, cols), 1) % TRIPLE < PAIR
    scale = jnp.where(is_query, HEAD_DIM**-0.5, 1.0)
    for h in range(2):
        qkv_ref[:, h * cols : (h + 1) * cols] = (nn(n1, held[h, :, :cols]) * scale).astype(BF16)


def project(place, x, pieces, ready=()):
    rows, width = x.shape
    groups, unit_rows, unit_cols = pieces[0].shape
    held = (2, width, unit_cols)
    return pl.pallas_call(
        project_kernel,
        grid=(rows // TILE,),
        in_specs=[SCALARS, pl.BlockSpec((TILE, width), lambda i: (i, 0))] + [APART] * (len(pieces) + len(ready)),
        out_specs=[
            pl.BlockSpec((TILE, 3 * width), lambda i: (i, 0)),
            pl.BlockSpec((TILE, width), lambda i: (i, 0)),
            whole((16, width)),
            whole(held),
        ],
        out_shape=[
            jax.ShapeDtypeStruct((rows, 3 * width), BF16),
            jax.ShapeDtypeStruct((rows, width), BF16),
            jax.ShapeDtypeStruct((16, width), F32),
            jax.ShapeDtypeStruct(held, BF16),
        ],
        scratch_shapes=[
            pltpu.VMEM((2, 4 * groups, unit_rows, unit_cols), BF16),
            pltpu.SemaphoreType.DMA((len(pieces) * groups,)),
        ],
        compiler_params=params(),
        cost_estimate=pl.CostEstimate(
            flops=18 * rows * width * width, bytes_accessed=16 * rows * width, transcendentals=0
        ),
        name="project",
    )(place, x, *pieces, *ready)


def nt(left, right):
    return lax.dot_general(left, right, (((1,), (1,)), ((), ())), preferred_element_type=F32)


def tn(left, right):
    return lax.dot_general(left, right, (((0,), (0,)), ((), ())), preferred_element_type=F32)


def nn(left, right):
    return jnp.dot(left, right, preferred_element_type=F32)


STRIP = 128


def head_mask(head):
    lanes = lax.broadcasted_iota(jnp.int32, (1, PAIR), 1)
    return (lanes // HEAD_DIM) == head


SAFE = 60.0
QUERIES = 512


def attend_kernel(qkv_ref, *refs):
    o_ref, lse_ref, lse_s = refs[-3:]
    q_ref, keys, value = qkv_ref.at[:, pl.ds(0, PAIR)], qkv_ref[:, PAIR : 2 * PAIR], qkv_ref[:, 2 * PAIR :]
    masks = [head_mask(h) for h in range(2)]
    values = [jnp.where(mask, value, jnp.ones_like(value)) for mask in masks]
    size = min(QUERIES, q_ref.shape[0])

    def blocks(shifted):
        for start in range(0, q_ref.shape[0], size):
            rows = slice(start, start + size)
            queries = q_ref[rows, :]
            mixed, peaks = [], []
            for h in range(2):
                own = jnp.where(masks[h], queries, jnp.zeros_like(queries))
                scores = nt(own, keys)
                expo = []
                peaks.append(jnp.max(scores, -1, keepdims=True) if shifted else 0.0)
                for s in range(0, size, 64):
                    strip = scores[s : s + 64]
                    expo.append(jnp.exp(strip - peaks[h][s : s + 64] if shifted else strip).astype(BF16))
                mixed.append(nn(jnp.concatenate(expo, 0), values[h]))
            summed = pltpu.roll(jnp.where(masks[0], mixed[1], mixed[0]), HEAD_DIM, 1)
            o_ref[rows, :] = (jnp.where(masks[0], mixed[0], mixed[1]) * (1.0 / summed)).astype(BF16)
            peak = jnp.where(masks[0], peaks[0], peaks[1]) if shifted else 0.0
            lse_s[rows, :] = peak + jnp.log(summed)

    longest = []
    for part in (q_ref[...], keys):
        wide = part.astype(F32)
        longest.append(jnp.max(jnp.sum(wide * wide, -1, keepdims=True)))
    safe = longest[0] * longest[1] < SAFE * SAFE
    pl.when(safe)(lambda: blocks(False))
    pl.when(jnp.logical_not(safe))(lambda: blocks(True))
    turned = jnp.transpose(lse_s[...])
    for h in range(2):
        lse_ref[0, h : h + 1, :] = turned[h * HEAD_DIM : h * HEAD_DIM + 1]


def attend_fast(qkv, first, count, ready=()):
    rows = qkv.shape[0]
    return pl.pallas_call(
        attend_kernel,
        grid=(count,),
        in_specs=[pl.BlockSpec((rows, TRIPLE), lambda i: (0, first + i))] + [APART] * len(ready),
        out_specs=[
            pl.BlockSpec((rows, PAIR), lambda i: (0, i)),
            pl.BlockSpec((1, 8, rows), lambda i: (i, 0, 0)),
        ],
        out_shape=[
            jax.ShapeDtypeStruct((rows, count * PAIR), BF16),
            jax.ShapeDtypeStruct((count, 8, rows), F32),
        ],
        scratch_shapes=[pltpu.VMEM((rows, PAIR), F32)],
        compiler_params=params(),
        cost_estimate=pl.CostEstimate(
            flops=32 * rows * rows * count * PAIR, bytes_accessed=8 * rows * count * PAIR, transcendentals=0
        ),
        name="attend",
    )(qkv, *ready)


HIDDEN = 512


def mlp_kernel(place_ref, scale_ref, x_ref, g_ref, gain_ref, *refs):
    (act_ref, other_ref, dx1_ref, do_ref, keep_ref, send_ref, keep_down_ref, send_down_ref, dgain_ref,
     held, down, x1_s, n2_s, n2t_s, dy_s, acts, dn2, hid_s, dg_s, du_s, part_s, sems, sems_later) = refs[-23:]
    pieces, down_pieces, o_refs = refs[:8], refs[8:12], refs[12:-23]
    me, side = place_ref[0], place_ref[1]
    step = pl.program_id(0)
    rows, width = x_ref.shape
    hidden_size = down.shape[0]
    blocks = rows // TILE
    half = width // 2
    units = hidden_size // 2
    gain = gain_ref[8:9, :]
    pair_rows = keep_ref.shape[1]
    per_pair = keep_down_ref.shape[1]

    @pl.when(step == 0)
    def _():
        first, later = [], []
        for ref, k, x, rel in listing(pieces):
            pair = me ^ rel
            at_half = side ^ x
            source = ref.at[k]
            at = pl.ds(pl.multiple_of(pair * pair_rows, 16), pair_rows)
            for copies, sem, lanes in ((first, sems, pl.ds(0, half)), (later, sems_later, pl.ds(half, 2 * units))):
                copies.append(
                    pltpu.make_async_copy(source.at[:, lanes], held.at[at_half, at, lanes], sem.at[len(copies)])
                )
        for ref, k, _, rel in listing(down_pieces, DOWN_PIECES):
            at = pl.ds(pl.multiple_of((me ^ rel) * per_pair, 16), per_pair)
            later.append(pltpu.make_async_copy(ref.at[k], down.at[at, :], sems_later.at[len(later)]))
        for copy in first + later:
            copy.start()
        for copy in first:
            copy.wait()

        @pl.loop(0, blocks)
        def _(i):
            at = pl.ds(pl.multiple_of(i * TILE, TILE), TILE)
            heads = jnp.concatenate([ref[at, :] for ref in o_refs], 1)
            mixed = jnp.concatenate([nn(heads, held[h, :, :half]) for h in range(2)], 1)
            x1 = x_ref[at, :].astype(F32) + mixed
            x1_s[at, :] = x1
            acts[at, :] = x1
            root = lax.rsqrt(jnp.mean(x1 * x1, -1, keepdims=True) + EPS)
            n2_s[at, :] = (x1 * root * gain).astype(BF16)
            dy_s[at, :] = (g_ref[at, :].astype(F32) * scale_ref[0]).astype(BF16)
            dn2[at, :] = jnp.zeros((TILE, width), F32)

        for i in range(blocks):
            n2t_s[:, i * TILE : (i + 1) * TILE] = jnp.transpose(n2_s[i * TILE : (i + 1) * TILE, :])
        for copy in later:
            copy.wait()

    in_half = units // HIDDEN
    at_half = step // in_half
    lane = (step % in_half) * HIDDEN
    gate_at = pl.ds(pl.multiple_of(half + lane, 128), HIDDEN)
    up_at = pl.ds(pl.multiple_of(half + units + lane, 128), HIDDEN)
    w_gate = held[at_half, :, gate_at]
    w_up = held[at_half, :, up_at]
    hidden_rows = pl.ds(pl.multiple_of(step * HIDDEN, HIDDEN), HIDDEN)
    w_down = down[hidden_rows, :]
    c_one = math.sqrt(2 / math.pi)
    c_two = 0.044715 * c_one
    half_rows = rows // 2
    for base in range(0, rows, half_rows):
        at = slice(base, base + half_rows)
        gate_all = nn(n2_s[at, :], w_gate)
        up_all = nn(n2_s[at, :], w_up)
        dh_all = nt(dy_s[at, :], w_down)
        for s in range(0, half_rows, STRIP // 2):
            strip = slice(s, s + STRIP // 2)
            out = slice(base + s, base + s + STRIP // 2)
            gate, up, dh = gate_all[strip], up_all[strip], dh_all[strip]
            squared = gate * gate
            bend = jnp.tanh(gate * (c_one + c_two * squared))
            rise = 0.5 + 0.5 * bend
            gelu = gate * rise
            slope = rise + gate * (0.5 * (1.0 - bend * bend)) * (c_one + 3.0 * c_two * squared)
            hid_s[out, :] = (gelu * up).astype(BF16)
            dg_s[out, :] = (dh * up * slope).astype(BF16)
            du_s[out, :] = (dh * gelu).astype(BF16)
        acts[at, :] += nn(hid_s[at, :], w_down)
        dn2[at, :] += nt(dg_s[at, :], w_gate) + nt(du_s[at, :], w_up)

    for values, lanes in ((dg_s, gate_at), (du_s, up_at)):
        part_s[:, :HIDDEN] = nn(n2t_s[...], values[...])
        file_rows(keep_ref, send_ref, me, side, at_half, lanes, part_s.at[:, pl.ds(0, HIDDEN)])

    groups = keep_ref.shape[0] // 4
    step_total = tn(hid_s[...], dy_s[...]).astype(BF16)
    for nth in range(HIDDEN // per_pair):
        rel = (step * (HIDDEN // per_pair) + nth) ^ me
        slot = rel // 2 % 2 * groups + rel // 4
        block = step_total[nth * per_pair : (nth + 1) * per_pair]

        @pl.when(rel % 2 == 0)
        def _():
            keep_down_ref[slot] = block

        @pl.when(rel % 2 == 1)
        def _():
            send_down_ref[slot] = block

    @pl.when(step == pl.num_programs(0) - 1)
    def _():
        dgain_ref[...] = jnp.zeros_like(dgain_ref)

        act_ref[...] = acts[: rows // 2, :].astype(BF16)
        other_ref[...] = acts[rows // 2 :, :].astype(BF16)

        @pl.loop(0, blocks)
        def _(i):
            at = pl.ds(pl.multiple_of(i * TILE, TILE), TILE)
            x1 = x1_s[at, :]
            root = lax.rsqrt(jnp.mean(x1 * x1, -1, keepdims=True) + EPS)
            back = dn2[at, :]
            unit_x1 = x1 * root
            dgain_ref[0:1, :] += jnp.sum(back * unit_x1, 0, keepdims=True)
            lifted = back * gain
            inner = jnp.mean(lifted * unit_x1, -1, keepdims=True)
            d_x1 = g_ref[at, :].astype(F32) * scale_ref[0] + root * (lifted - unit_x1 * inner)
            dx1_ref[at, :] = d_x1
            low = d_x1.astype(BF16)
            n2_s[at, :] = low
            do = nt(low[:, :half], held[0, :, :half]) + nt(low[:, half:], held[1, :, :half])
            do_ref[at, :] = do.astype(BF16)

        done = 0
        for ref in o_refs:
            count = ref.shape[1]
            part_s[done : done + count, :] = tn(ref[...], n2_s[...])
            done += count
        for h in range(2):
            file_rows(keep_ref, send_ref, me, side, h, slice(0, half), part_s.at[:, pl.ds(h * half, half)])


def mlp(place, scale, heads, x, grad, gains, pieces, down_pieces):
    rows, width = x.shape
    groups, pair_rows, cols = pieces[0].shape
    per_pair = down_pieces[0].shape[1]
    hidden = 4 * groups * per_pair
    kept = (4 * groups, pair_rows, cols)
    kept_down = (2 * groups, per_pair, width)
    units = sum(piece.shape[0] for piece in pieces)
    return pl.pallas_call(
        mlp_kernel,
        grid=(hidden // HIDDEN,),
        in_specs=[SCALARS, SCALARS]
        + [whole((rows, width))] * 2
        + [whole(gains.shape)]
        + [APART] * (len(pieces) + len(down_pieces))
        + [whole(part.shape) for part in heads],
        out_specs=[whole((rows // 2, width))] * 2
        + [whole((rows, width))] * 2
        + [whole(kept)] * 2
        + [whole(kept_down)] * 2
        + [whole((8, width))],
        out_shape=[
            jax.ShapeDtypeStruct((rows // 2, width), BF16),
            jax.ShapeDtypeStruct((rows // 2, width), BF16),
            jax.ShapeDtypeStruct((rows, width), F32),
            jax.ShapeDtypeStruct((rows, width), BF16),
            jax.ShapeDtypeStruct(kept, BF16),
            jax.ShapeDtypeStruct(kept, BF16),
            jax.ShapeDtypeStruct(kept_down, BF16),
            jax.ShapeDtypeStruct(kept_down, BF16),
            jax.ShapeDtypeStruct((8, width), F32),
        ],
        scratch_shapes=[
            pltpu.VMEM((2, width, width // 2 + hidden), BF16),
            pltpu.VMEM((hidden, width), BF16),
            pltpu.VMEM((rows, width), F32),
            pltpu.VMEM((rows, width), BF16),
            pltpu.VMEM((width, rows), BF16),
            pltpu.VMEM((rows, width), BF16),
            pltpu.VMEM((rows, width), F32),
            pltpu.VMEM((rows, width), F32),
            pltpu.VMEM((rows, HIDDEN), BF16),
            pltpu.VMEM((rows, HIDDEN), BF16),
            pltpu.VMEM((rows, HIDDEN), BF16),
            pltpu.VMEM((width, width), F32),
            pltpu.SemaphoreType.DMA((units,)),
            pltpu.SemaphoreType.DMA((units + 4 * groups,)),
        ],
        compiler_params=params(),
        cost_estimate=pl.CostEstimate(
            flops=4 * rows * width * (3 * width + 9 * hidden),
            bytes_accessed=40 * MIB,
            transcendentals=0,
        ),
        name="mlp",
    )(place, scale, x, grad, gains, *pieces, *down_pieces, *heads)


def attend_back_kernel(qkv_ref, do_ref, o_ref, lse_ref, *refs):
    d_ref, token_ref, dk_s, dv_s = refs[-4:]
    q_ref, keys, values = qkv_ref.at[:, pl.ds(0, PAIR)], qkv_ref[:, PAIR : 2 * PAIR], qkv_ref[:, 2 * PAIR :]
    total = keys.shape[0]
    token_ref[...] = jnp.zeros_like(token_ref)
    scale = HEAD_DIM**-0.5
    k_own = jnp.concatenate([jnp.where(head_mask(h), keys, jnp.zeros_like(keys)) for h in range(2)], 0)
    prod = do_ref[...].astype(F32) * o_ref[...].astype(F32)
    high = prod.astype(BF16)
    low = (prod - high.astype(F32)).astype(BF16)
    chosen = (
        lax.broadcasted_iota(jnp.int32, (8, PAIR), 1) // HEAD_DIM
        == lax.broadcasted_iota(jnp.int32, (8, PAIR), 0)
    ).astype(BF16)
    delta = nt(chosen, high) + nt(chosen, low)
    for block in range(q_ref.shape[0] // TILE):
        rows = slice(block * TILE, (block + 1) * TILE)
        queries, d_out = q_ref[rows, :], do_ref[rows, :]
        q_own, d_own, probs, slopes = [], [], [], []
        for h in range(2):
            mask = head_mask(h)
            q_own.append(jnp.where(mask, queries, jnp.zeros_like(queries)))
            d_own.append(jnp.where(mask, d_out, jnp.zeros_like(d_out)))
            scores = nt(keys, q_own[h])
            d_probs = nt(values, d_own[h])
            lse = lse_ref[0, h : h + 1, rows]
            center = delta[h : h + 1, rows]
            p_strips, s_strips = [], []
            for s in range(total // STRIP):
                strip = slice(s * STRIP, (s + 1) * STRIP)
                p = jnp.exp(scores[strip] - lse)
                p_strips.append(p.astype(BF16))
                s_strips.append((p * (d_probs[strip] - center)).astype(BF16))
            probs.append(jnp.concatenate(p_strips, 0))
            slopes.append(jnp.concatenate(s_strips, 0))
        d_ref[rows, :PAIR] = (tn(jnp.concatenate(slopes, 0), k_own) * scale).astype(BF16)
        d_keys = nn(jnp.concatenate(slopes, 1), jnp.concatenate(q_own, 0))
        d_values = nn(jnp.concatenate(probs, 1), jnp.concatenate(d_own, 0))
        if block == 0:
            dk_s[...] = d_keys
            dv_s[...] = d_values
        else:
            dk_s[...] += d_keys
            dv_s[...] += d_values
    d_ref[:, PAIR : 2 * PAIR] = dk_s[...].astype(BF16)
    d_ref[:, 2 * PAIR :] = dv_s[...].astype(BF16)


def attend_back_fast(qkv, d_out, heads, lse, first, d_qkv, ready=()):
    rows = d_out.shape[0]
    count = lse.shape[0]
    into = [] if d_qkv is None else [d_qkv]
    return pl.pallas_call(
        attend_back_kernel,
        grid=(count,),
        in_specs=[
            pl.BlockSpec((rows, TRIPLE), lambda i: (0, first + i)),
            pl.BlockSpec((rows, PAIR), lambda i: (0, first + i)),
            pl.BlockSpec((rows, PAIR), lambda i: (0, i)),
            pl.BlockSpec((1, 8, rows), lambda i: (i, 0, 0)),
        ]
        + [APART] * (len(into) + len(ready)),
        out_specs=[pl.BlockSpec((rows, TRIPLE), lambda i: (0, first + i)), whole((8, 128))],
        out_shape=[jax.ShapeDtypeStruct(qkv.shape, BF16), jax.ShapeDtypeStruct((8, 128), F32)],
        input_output_aliases={4: 0} if into else {},
        scratch_shapes=[pltpu.VMEM((rows, PAIR), F32)] * 2,
        compiler_params=params(),
        cost_estimate=pl.CostEstimate(
            flops=50 * rows * rows * count * PAIR, bytes_accessed=16 * rows * count * PAIR, transcendentals=0
        ),
        name="attend_back",
    )(qkv, d_out, heads, lse, *into, *ready)


def input_back_kernel(d_ref, w_ref, x_ref, dx1_ref, gain_ref, *refs):
    own_ref, *other_refs, dgain_ref = refs[-4:]
    step = pl.program_id(0)
    cols = d_ref.shape[1] // 2
    back = nt(d_ref[:, :cols], w_ref[0, :, :cols]) + nt(d_ref[:, cols:], w_ref[1, :, :cols])
    x = x_ref[...].astype(F32)
    root = lax.rsqrt(jnp.mean(x * x, -1, keepdims=True) + EPS)
    unit = x * root

    @pl.when(step == 0)
    def _():
        dgain_ref[...] = jnp.zeros_like(dgain_ref)

    dgain_ref[0:1, :] += jnp.sum(back * unit, 0, keepdims=True)
    lifted = back * gain_ref[0:1, :]
    inner = jnp.mean(lifted * unit, -1, keepdims=True)
    d_x = dx1_ref[...] + root * (lifted - unit * inner)

    @pl.when(step < 2)
    def _():
        own_ref[...] = d_x

    for nth, ref in enumerate(other_refs):

        @pl.when(step == 2 + nth)
        def _():
            ref[...] = d_x.astype(BF16)


def input_back(d_qkv, weights, x, d_x1, gains, ready=()):
    rows, width = x.shape
    tile = rows // 4
    block = pl.BlockSpec((tile, width), lambda i: (i, 0))
    return pl.pallas_call(
        input_back_kernel,
        grid=(4,),
        in_specs=[
            pl.BlockSpec((tile, d_qkv.shape[1]), lambda i: (i, 0)),
            whole(weights.shape),
            block,
            block,
            whole(gains.shape),
        ]
        + [APART] * len(ready),
        out_specs=[pl.BlockSpec((tile, width), lambda i: (jnp.minimum(i, 1), 0))]
        + [whole((tile, width))] * 2
        + [whole((8, width))],
        out_shape=[
            jax.ShapeDtypeStruct((rows // 2, width), F32),
            jax.ShapeDtypeStruct((tile, width), BF16),
            jax.ShapeDtypeStruct((tile, width), BF16),
            jax.ShapeDtypeStruct((8, width), F32),
        ],
        compiler_params=params(),
        cost_estimate=pl.CostEstimate(
            flops=12 * rows * width * width, bytes_accessed=24 * rows * width, transcendentals=0
        ),
        name="input_back",
    )(d_qkv, weights, x, d_x1, gains, *ready)


def file_devices(keep, send, me, side, lanes, sources):
    groups = keep.shape[0] // 4
    own = keep.shape[1] // 2
    for rel in range(4 * groups):
        for x in range(2):
            start = pl.multiple_of((me ^ rel) * 2 * own + (side ^ x) * own, 8)
            block = jnp.concatenate([source[pl.ds(start, own), :] for source in sources], 0)
            slot = (x * 2 + rel // 2 % 2) * groups + rel // 4
            (send if rel % 2 else keep)[slot, :, lanes] = block.astype(BF16)


def project_back_kernel(place_ref, first_ref, second_ref, n1_ref, *refs):
    gain_refs, (keep_ref, send_ref, first_s, second_s, turned_s, wide_s) = refs[:2], refs[-6:]
    me, side = place_ref[0], place_ref[1]
    step = pl.program_id(0)
    rows, width = n1_ref.shape

    @pl.when(step == 0)
    def _():
        for i in range(rows // TILE):
            turned_s[:, i * TILE : (i + 1) * TILE] = jnp.transpose(n1_ref[i * TILE : (i + 1) * TILE, :])
        for ref, part in zip(gain_refs, (first_s, second_s)):
            wide_s[...] = jnp.zeros_like(wide_s)
            wide_s[0:1, :] = ref[0:1, :]
            part[:, :128] = jnp.transpose(wide_s[...])
        last = keep_ref.shape[2] - 128
        sources = [part.at[:, pl.ds(0, 128)] for part in (first_s, second_s)]
        file_devices(keep_ref, send_ref, me, side, slice(last, last + 128), sources)

    first_s[...] = nn(turned_s[...], first_ref[...])
    second_s[...] = nn(turned_s[...], second_ref[...])
    lanes = pl.ds(pl.multiple_of(step * TRIPLE, 128), TRIPLE)
    file_devices(keep_ref, send_ref, me, side, lanes, (first_s, second_s))


def project_back(place, d_qkv, n1, d_gains, kept, ready=()):
    rows, width = n1.shape
    steps = width // PAIR // 2
    return pl.pallas_call(
        project_back_kernel,
        grid=(steps,),
        in_specs=[
            SCALARS,
            pl.BlockSpec((rows, TRIPLE), lambda i: (0, i)),
            pl.BlockSpec((rows, TRIPLE), lambda i: (0, steps + i)),
            whole((rows, width)),
        ]
        + [whole((8, width))] * 2
        + [APART] * len(ready),
        out_specs=[whole(kept)] * 2,
        out_shape=[jax.ShapeDtypeStruct(kept, BF16)] * 2,
        scratch_shapes=[
            pltpu.VMEM((width, TRIPLE), F32),
            pltpu.VMEM((width, TRIPLE), F32),
            pltpu.VMEM((width, rows), BF16),
            pltpu.VMEM((128, width), F32),
        ],
        compiler_params=params(),
        cost_estimate=pl.CostEstimate(
            flops=12 * rows * width * width, bytes_accessed=24 * rows * width, transcendentals=0
        ),
        name="project_back",
    )(place, d_qkv, d_qkv, n1, *d_gains, *ready)


def give_half(plots, side):
    own = lax.dynamic_index_in_dim(plots, side, 0, keepdims=False)
    return own, lax.dynamic_index_in_dim(plots, 1 - side, 0, keepdims=False)


def halves_back(own, arrived, side):
    arrived = arrived.astype(own.dtype)
    return jnp.stack([by_side(side, own, arrived), by_side(side, arrived, own)])


CALLS = (3, 2, 1)


def local_fast(size, *arguments):
    (inputs, out_grad, source_id, source_weight, gain_attn, gain_mlp,
     w_query, w_key, w_value, w_attn_out, w_gate, w_up, w_down) = arguments
    half_rows, width = inputs.shape[1:]
    half = width // 2
    hidden = w_gate.shape[1]
    groups = size // 4
    side = lax.axis_index("narrow")
    place = jnp.stack([lax.axis_index("wide"), side]).astype(jnp.int32)

    pairs = width // PAIR
    unit_a, unit_b, give = pack(
        place, (gain_attn, gain_mlp), (w_query, w_key, w_value), (w_attn_out, w_gate, w_up)
    )
    stack_a = spread_z(unit_a, size)
    unit_b = pair_up(unit_b, give, side)
    unit_c = pair_up(w_down, after(w_down, unit_a), side)
    quarter = half_rows // 2
    own_x, give_x = give_half(after(inputs, unit_a), side)
    others = [swap_x(give_x[:quarter])]
    stack_a, unit_b, unit_c, others[0] = lax.optimization_barrier((stack_a, unit_b, unit_c, others[0]))
    x_a, y_a = spread_xy(stack_a, size)
    units_b = [unit_b, None, swap(unit_b, 8, size)]
    x_a, y_a, units_b[2] = lax.optimization_barrier((x_a, y_a, units_b[2]))
    d_a = swap(x_a, 2, size)
    others.append(swap_x(after(give_x[quarter:], x_a)))
    unit_b = after(unit_b, y_a)
    units_b[1] = swap(unit_b, 4, size)
    units_b += [swap(unit_b, 4 * k, size) for k in range(3, groups)]
    d_a, others[1], units_b[1], *units_b[3:] = lax.optimization_barrier((d_a, others[1], units_b[1], *units_b[3:]))
    x = jnp.concatenate([own_x, *others], 0)
    pieces_a = [stack_a, x_a, y_a, d_a]
    own_grad, give_grad = give_half(after(out_grad, x_a), side)
    grads = [swap_x(give_grad[:quarter]), swap_x(after(give_grad[quarter:], d_a))]
    pieces_a += [swap(piece, 1, size) for piece in pieces_a]

    source = lax.dynamic_index_in_dim(source_id, side, 0, keepdims=False)
    known = source == jnp.arange(source_weight.shape[0], dtype=jnp.int32)
    scale = jnp.sum(jnp.where(known, source_weight, 0.0))[None]

    stack_b = jnp.stack(units_b)
    unit_c = after(unit_c, *pieces_a[4:])
    units_c = [unit_c, None] + [swap(unit_c, 4 * k, size) for k in range(2, groups)]
    qkv, n1, gains, weights = project(place, x, pieces_a, [stack_b])
    x_b, y_b = spread_xy(stack_b, size)
    heads, lses = [], []
    for call, count in enumerate(CALLS):
        ready = [[grads[0]], [*heads, y_b, *units_c[2:], grads[1]], [*heads, units_c[1]]][call]
        made = attend_fast(qkv, sum(CALLS[:call]), count, ready)
        heads.append(made[0])
        lses.append(made[1])
        if call == 0:
            y_b, stack_b, unit_c, _ = lax.optimization_barrier((y_b, stack_b, unit_c, heads[-1]))
            d_b = swap_x(y_b)
            units_c[1] = swap(unit_c, 4, size)
            twins_b = [swap(stack_b, 1, size), swap(y_b, 1, size)]
        elif call == 1:
            stack_c = jnp.stack(lax.optimization_barrier((*units_c, heads[-1]))[:groups])
            y_c = swap(stack_c, 2, size)
            twins_c = [swap(stack_c, 1, size)]
    x_b, d_b, y_c, _ = lax.optimization_barrier((x_b, d_b, y_c, heads[-1]))
    grad = jnp.concatenate([own_grad, *grads], 0)
    pieces_b = [stack_b, x_b, y_b, d_b]
    pieces_b += [twins_b[0], swap(x_b, 1, size), twins_b[1], swap(d_b, 1, size)]
    pieces_c = [stack_c, y_c, *twins_c, swap(y_c, 1, size)]
    acts, other_acts, d_x1, d_out, keep, send, keep_c, send_c, d_gain = mlp(
        place, scale, heads, x, grad, gains, pieces_b, pieces_c
    )

    twin = swap(send, 1, size)
    twin_c = swap(send_c, 1, size)
    other_acts = swap_x(other_acts)
    d_qkv = None
    ready = []
    for call in reversed(range(len(CALLS))):
        start = sum(CALLS[:call])
        d_qkv, token = attend_back_fast(qkv, d_out, heads[call], lses[call], start, d_qkv, ready)
        if call == 2:
            twin, twin_c = lax.optimization_barrier((twin, twin_c, token))[:2]
            diagonal, over_y = diagonal_of(keep, twin), over_y_of(keep, twin)
            corner = swap(diagonal, 2, size)
            by_y = swap(after(over_y, diagonal), 2, size)
            ready = [diagonal, over_y, token]
        elif call == 1:
            over_y_c = chip_sum(keep_c, after(twin_c, token), 1, 2).astype(BF16)
            twin, other_acts, corner, over_y_c = lax.optimization_barrier((twin, other_acts, corner, over_y_c, token))[:4]
            over_x = over_x_of(keep, twin, corner)
            by_x = swap_x(over_x)
            ready = [over_x, token, other_acts, over_y_c]
    twin, by_x, by_y = lax.optimization_barrier((twin, by_x, by_y, token))[:3]
    sides = (by_x, by_y)
    far = [unit.astype(BF16) for unit in collect_own(keep, twin, sides, range(1, groups))]
    arrived_c = swap(after(over_y_c, by_y), 2, size)
    own, *other, d_gain_attn = input_back(d_qkv, weights, x, d_x1, gains, far)
    others = [swap_x(other[0])]
    kept = (4 * groups, *unit_a.shape)
    arrived = [swap(far[k - 1], 4 * k, size) for k in range(1, groups)]
    keep_a, send_a = project_back(place, d_qkv, n1, (d_gain_attn, d_gain), kept, [own, arrived[0]])
    send_a, arrived_c, others[0], *arrived[1:] = lax.optimization_barrier((send_a, arrived_c, others[0], *arrived[1:]))
    twin_a = swap(send_a, 1, size)
    diagonal = diagonal_of(keep_a, twin_a)
    corner = swap(diagonal, 2, size)
    keep, twin, by_x, by_y, keep_c, twin_c, other[1], acts, other_acts = lax.optimization_barrier(
        (keep, twin, by_x, by_y, keep_c, twin_c, other[1], acts, other_acts, diagonal)
    )[:9]
    others.append(swap_x(other[1]))
    total_c = chip_sum(keep_c, twin_c, 0, 2) + arrived_c.astype(F32)
    far_c = [swap(total_c[k].astype(BF16), 4 * k, size) for k in range(1, groups)]
    total_b = sum([part.astype(F32) for part in arrived], collect_own(keep, twin, (by_x, by_y), [0])[0])
    activations = halves_back(acts, other_acts, side)
    twin_a, corner, others[1] = lax.optimization_barrier((twin_a, corner, others[1]))
    sides = [swap_x(over_x_of(keep_a, twin_a, corner)), swap(over_y_of(keep_a, twin_a), 2, size)]
    total_b = after(total_b, corner)
    first_b, second_b = settle(total_b, side)
    input_grad = halves_back(own, jnp.concatenate(others, 0), side)
    twin_a, first_b, second_b, *rest = lax.optimization_barrier((twin_a, first_b, second_b, *sides, *far_c))
    sides, far_c = rest[:2], rest[2:]
    units = collect_own(keep_a, twin_a, sides, range(groups))
    arrived = [swap(units[k].astype(BF16), 4 * k, size) for k in range(1, groups)]
    far_c[-1] = after(far_c[-1], units[0])
    grad_down = settle_rows(sum([part.astype(F32) for part in far_c], total_c[0]), side)
    arrived[0], grad_down = lax.optimization_barrier((arrived[0], grad_down))
    total_a = sum([part.astype(F32) for part in arrived], units[0])
    own_rows = unit_a.shape[0] // 2
    first_a, second_a = total_a[:own_rows], total_a[own_rows:]

    def in_order(part):
        return jnp.concatenate(
            [
                piece[:, pair * TRIPLE + part * PAIR : pair * TRIPLE + (part + 1) * PAIR]
                for piece in (first_a, second_a)
                for pair in range(pairs // 2)
            ],
            1,
        )

    def joined(first, second, start, count):
        return jnp.concatenate([first[:, start : start + count], second[:, start : start + count]], 1)

    units = hidden // 2
    return (
        activations,
        input_grad,
        first_a[:, 3 * half],
        second_a[:, 3 * half],
        in_order(0),
        in_order(1),
        in_order(2),
        joined(first_b, second_b, 0, half),
        joined(first_b, second_b, half, units),
        joined(first_b, second_b, half + units, units),
        grad_down,
    )


def solution(mesh):
    size = mesh.shape["wide"]
    fits = mesh.shape["narrow"] == 2 and size == 16
    body = functools.partial(local_fast, size) if fits else local
    placed = (
        P("wide", "narrow", None),
        P("wide", "narrow", None),
        P("wide"),
        P(),
        P(("wide", "narrow")),
        P(("wide", "narrow")),
        P(("wide", "narrow"), None),
        P(("wide", "narrow"), None),
        P(("wide", "narrow"), None),
        P(("wide", "narrow"), None),
        P(("wide", "narrow"), None),
        P(("wide", "narrow"), None),
        P(("wide", "narrow"), None),
    )
    return jax.shard_map(
        body,
        mesh=mesh,
        in_specs=placed,
        out_specs=(
            P("wide", "narrow", None),
            P("wide", "narrow", None),
            P(("wide", "narrow")),
            P(("wide", "narrow")),
            P(("wide", "narrow"), None),
            P(("wide", "narrow"), None),
            P(("wide", "narrow"), None),
            P(("wide", "narrow"), None),
            P(("wide", "narrow"), None),
            P(("wide", "narrow"), None),
            P(("wide", "narrow"), None),
        ),
        check_vma=False,
    )
```

```python
import functools
import math

import jax
import jax.numpy as jnp
from jax import lax
from jax.experimental import pallas as pl
from jax.experimental.pallas import tpu as pltpu
from jax.sharding import PartitionSpec as P

HEADS = 12
HEAD_DIM = 64


EPS = 1e-06
HIGH = lax.Precision.HIGHEST


def rms(value, gain):
    return value * lax.rsqrt(jnp.mean(value * value, -1, keepdims=True) + EPS) * gain


def matmul(left, right):
    return jnp.dot(left, right, preferred_element_type=jnp.float32)


def matmul_tn(left, right):
    return lax.dot_general(
        left, right, (((0,), (0,)), ((), ())), preferred_element_type=jnp.float32
    )


def matmul_nt(left, right):
    return lax.dot_general(
        left, right, (((1,), (1,)), ((), ())), preferred_element_type=jnp.float32
    )


def attend(items):
    query, keys, values = items
    rows = query.shape[0]
    total = keys.shape[0]
    scale = HEAD_DIM ** (-0.5)
    q_heads = query.reshape(rows, HEADS, HEAD_DIM)
    k_heads = keys.reshape(total, HEADS, HEAD_DIM)
    v_heads = values.reshape(total, HEADS, HEAD_DIM)
    scores = (
        jnp.einsum("rhd,shd->hrs", q_heads, k_heads, preferred_element_type=jnp.float32) * scale
    )
    peak = jnp.max(scores, -1, keepdims=True)
    expo = jnp.exp(scores - peak)
    summed = jnp.sum(expo, -1, keepdims=True)
    probs_full = expo / summed
    probs = probs_full.astype(jnp.bfloat16)
    heads_out = jnp.einsum("hrs,shd->rhd", probs, v_heads, preferred_element_type=jnp.float32)
    exact_out = jnp.einsum("hrs,shd->rhd", probs_full, v_heads.astype(jnp.float32), precision=HIGH)
    log_total = (peak + jnp.log(summed))[:, :, 0]
    return (heads_out.reshape(rows, HEADS * HEAD_DIM), log_total, exact_out)


def attend_back(items):
    query, keys, values, log_total, d_out = items
    rows = query.shape[0]
    total = keys.shape[0]
    width = HEADS * HEAD_DIM
    scale = HEAD_DIM ** (-0.5)
    q_heads = query.reshape(rows, HEADS, HEAD_DIM)
    k_heads = keys.reshape(total, HEADS, HEAD_DIM)
    v_heads = values.reshape(total, HEADS, HEAD_DIM)
    d_heads = d_out.reshape(rows, HEADS, HEAD_DIM)
    scores = (
        jnp.einsum("rhd,shd->hrs", q_heads, k_heads, preferred_element_type=jnp.float32) * scale
    )
    probs = jnp.exp(scores - log_total[:, :, None])
    probs_low = probs.astype(jnp.bfloat16)
    d_probs = jnp.einsum("rhd,shd->hrs", d_heads, v_heads, preferred_element_type=jnp.float32)
    center = jnp.sum(d_probs * probs, -1, keepdims=True)
    d_scores = (probs * (d_probs - center)).astype(jnp.bfloat16)
    d_query = (
        jnp.einsum("hrs,shd->rhd", d_scores, k_heads, preferred_element_type=jnp.float32) * scale
    )
    d_keys = (
        jnp.einsum("hrs,rhd->shd", d_scores, q_heads, preferred_element_type=jnp.float32) * scale
    )
    d_values = jnp.einsum("hrs,rhd->shd", probs_low, d_heads, preferred_element_type=jnp.float32)
    return (
        d_query.reshape(rows, width),
        d_keys.reshape(total, width),
        d_values.reshape(total, width),
    )


def local(
    inputs,
    out_grad,
    source_id,
    source_weight,
    gain_attn,
    gain_mlp,
    w_query,
    w_key,
    w_value,
    w_attn_out,
    w_gate,
    w_up,
    w_down,
):
    plots, rows, width = inputs.shape
    gathered = (
        lax.all_gather(gain_attn, ("wide", "narrow"), axis=0, tiled=True),
        lax.all_gather(gain_mlp, ("wide", "narrow"), axis=0, tiled=True),
        lax.all_gather(w_query, ("wide", "narrow"), axis=0, tiled=True),
        lax.all_gather(w_key, ("wide", "narrow"), axis=0, tiled=True),
        lax.all_gather(w_value, ("wide", "narrow"), axis=0, tiled=True),
        lax.all_gather(w_attn_out, ("wide", "narrow"), axis=0, tiled=True),
        lax.all_gather(w_gate, ("wide", "narrow"), axis=0, tiled=True),
        lax.all_gather(w_up, ("wide", "narrow"), axis=0, tiled=True),
        lax.all_gather(w_down, ("wide", "narrow"), axis=0, tiled=True),
    )
    gain_one, gain_two, wq, wk, wv, wo, wg, wu, wd = gathered
    gain_one = gain_one.astype(jnp.float32)
    gain_two = gain_two.astype(jnp.float32)
    x_rows = inputs.astype(jnp.float32).reshape(plots * rows, width)
    n1 = rms(x_rows, gain_one).astype(jnp.bfloat16)
    query = matmul(n1, wq).astype(jnp.bfloat16)
    keys_own = matmul(n1, wk).astype(jnp.bfloat16).reshape(plots, rows, width)
    values_own = matmul(n1, wv).astype(jnp.bfloat16).reshape(plots, rows, width)
    keys_all, values_all = (
        lax.all_gather(keys_own, "narrow", axis=1, tiled=True),
        lax.all_gather(values_own, "narrow", axis=1, tiled=True),
    )
    query_plots = query.reshape(plots, rows, width)
    heads_out, log_total, exact_out = lax.map(attend, (query_plots, keys_all, values_all))
    attn = heads_out.reshape(plots * rows, width).astype(jnp.bfloat16)
    x1 = x_rows + matmul(attn, wo)
    n2 = rms(x1, gain_two).astype(jnp.bfloat16)
    gate = matmul(n2, wg)
    up = matmul(n2, wu)
    gate_act, gelu_back = jax.vjp(lambda u: jax.nn.gelu(u, approximate=True), gate)
    hidden = (gate_act * up).astype(jnp.bfloat16)
    activations = (x1 + matmul(hidden, wd)).astype(jnp.bfloat16).reshape(plots, rows, width)
    onehot = (
        source_id[:, None] == jnp.arange(source_weight.shape[0], dtype=jnp.int32)[None, :]
    ).astype(jnp.float32)
    plot_scale = jnp.sum(onehot * source_weight[None, :], -1)
    cotangent = (out_grad.astype(jnp.float32) * plot_scale[:, None, None]).reshape(
        plots * rows, width
    )
    again = (
        lax.all_gather(gain_attn, ("wide", "narrow"), axis=0, tiled=True),
        lax.all_gather(gain_mlp, ("wide", "narrow"), axis=0, tiled=True),
        lax.all_gather(w_query, ("wide", "narrow"), axis=0, tiled=True),
        lax.all_gather(w_key, ("wide", "narrow"), axis=0, tiled=True),
        lax.all_gather(w_value, ("wide", "narrow"), axis=0, tiled=True),
        lax.all_gather(w_attn_out, ("wide", "narrow"), axis=0, tiled=True),
        lax.all_gather(w_gate, ("wide", "narrow"), axis=0, tiled=True),
        lax.all_gather(w_up, ("wide", "narrow"), axis=0, tiled=True),
        lax.all_gather(w_down, ("wide", "narrow"), axis=0, tiled=True),
    )
    gain_one, gain_two, wq, wk, wv, wo, wg, wu, wd = again
    gain_one = gain_one.astype(jnp.float32)
    gain_two = gain_two.astype(jnp.float32)
    d_y = cotangent.astype(jnp.bfloat16)
    d_hidden = matmul_nt(d_y, wd)
    grad_down = matmul_tn(hidden, d_y)
    d_gate = gelu_back(d_hidden * up)[0].astype(jnp.bfloat16)
    d_up = (d_hidden * gate_act).astype(jnp.bfloat16)
    grad_gate = matmul_tn(n2, d_gate)
    grad_up = matmul_tn(n2, d_up)
    d_n2 = matmul_nt(d_gate, wg) + matmul_nt(d_up, wu)
    _, norm_two_back = jax.vjp(rms, x1, gain_two)
    d_x1_norm, grad_gain_mlp = norm_two_back(d_n2)
    d_x1 = cotangent + d_x1_norm
    d_attn = d_x1.astype(jnp.bfloat16)
    grad_attn_out = matmul_tn(attn, d_attn)
    d_out = matmul_nt(d_attn, wo).astype(jnp.bfloat16).reshape(plots, rows, width)
    keys_all, values_all = (
        lax.all_gather(keys_own, "narrow", axis=1, tiled=True),
        lax.all_gather(values_own, "narrow", axis=1, tiled=True),
    )
    d_query, d_keys_part, d_values_part = lax.map(
        attend_back, (query_plots, keys_all, values_all, log_total, d_out)
    )
    d_keys, d_values = (
        lax.psum_scatter(
            d_keys_part.astype(jnp.bfloat16), "narrow", scatter_dimension=1, tiled=True
        ).astype(jnp.float32),
        lax.psum_scatter(
            d_values_part.astype(jnp.bfloat16), "narrow", scatter_dimension=1, tiled=True
        ).astype(jnp.float32),
    )
    dq_low = d_query.reshape(plots * rows, width).astype(jnp.bfloat16)
    dk_low = d_keys.reshape(plots * rows, width).astype(jnp.bfloat16)
    dv_low = d_values.reshape(plots * rows, width).astype(jnp.bfloat16)
    grad_query = matmul_tn(n1, dq_low)
    grad_key = matmul_tn(n1, dk_low)
    grad_value = matmul_tn(n1, dv_low)
    d_n1 = matmul_nt(dq_low, wq) + matmul_nt(dk_low, wk) + matmul_nt(dv_low, wv)
    _, norm_one_back = jax.vjp(rms, x_rows, gain_one)
    d_x_norm, grad_gain_attn = norm_one_back(d_n1)
    input_grad = (d_x1 + d_x_norm).reshape(plots, rows, width)
    grads = (
        grad_gain_attn,
        grad_gain_mlp,
        grad_query,
        grad_key,
        grad_value,
        grad_attn_out,
        grad_gate,
        grad_up,
        grad_down,
    )
    shards = (
        lax.psum_scatter(grads[0], ("wide", "narrow"), scatter_dimension=0, tiled=True),
        lax.psum_scatter(grads[1], ("wide", "narrow"), scatter_dimension=0, tiled=True),
        lax.psum_scatter(grads[2], ("wide", "narrow"), scatter_dimension=0, tiled=True),
        lax.psum_scatter(grads[3], ("wide", "narrow"), scatter_dimension=0, tiled=True),
        lax.psum_scatter(grads[4], ("wide", "narrow"), scatter_dimension=0, tiled=True),
        lax.psum_scatter(grads[5], ("wide", "narrow"), scatter_dimension=0, tiled=True),
        lax.psum_scatter(grads[6], ("wide", "narrow"), scatter_dimension=0, tiled=True),
        lax.psum_scatter(grads[7], ("wide", "narrow"), scatter_dimension=0, tiled=True),
        lax.psum_scatter(grads[8], ("wide", "narrow"), scatter_dimension=0, tiled=True),
    )
    return (
        activations,
        input_grad,
        shards[0],
        shards[1],
        shards[2],
        shards[3],
        shards[4],
        shards[5],
        shards[6],
        shards[7],
        shards[8],
    )


F32 = jnp.float32
BF16 = jnp.bfloat16
PAIR = 2 * HEAD_DIM
MIB = 1 << 20
TILE = 256


def params(limit=60):
    return pltpu.CompilerParams(vmem_limit_bytes=limit * MIB)


def whole(shape):
    return pl.BlockSpec(shape, lambda *_: (0,) * len(shape), pipeline_mode=pl.Buffered(1))


SCALARS = pl.BlockSpec(memory_space=pltpu.SMEM)
APART = pl.BlockSpec(memory_space=pl.ANY)


def swap(value, mask, size):
    return lax.ppermute(value, "wide", [(i, i ^ mask) for i in range(size)])


def swap_x(value):
    return lax.ppermute(value, "narrow", [(0, 1), (1, 0)])


def by_side(side, first, second):
    return jnp.where(side == 0, first, second)


def after(value, *others):
    return lax.optimization_barrier((value, *others))[0]


def pair_up(piece, give, side):
    other = swap_x(give)
    return jnp.concatenate([by_side(side, piece, other), by_side(side, other, piece)], 0)


def spread_z(unit, size):
    return jnp.stack([unit] + [swap(unit, 4 * k, size) for k in range(1, size // 4)])


def spread_xy(stack, size):
    return swap_x(stack), swap(stack, 2, size)


PIECES = ((0, 0), (1, 0), (0, 1), (1, 1))
DOWN_PIECES = ((0, 0), (0, 1))


def listing(refs, places=PIECES):
    found = []
    for at, ref in enumerate(refs):
        x, y = places[at % len(places)]
        core = at // len(places)
        for k in range(ref.shape[0]):
            found.append((ref, k, x, 4 * k + 2 * y + core))
    return found


def chip_sum(keep, arrived, part, parts=4):
    groups = keep.shape[0] // parts
    at = slice(part * groups, (part + 1) * groups)
    return keep[at].astype(F32) + arrived[at].astype(F32)


def diagonal_of(keep, arrived):
    return chip_sum(keep, arrived, 3).astype(BF16)


def over_y_of(keep, arrived):
    return chip_sum(keep, arrived, 1).astype(BF16)


def over_x_of(keep, arrived, corner):
    return (chip_sum(keep, arrived, 2) + corner.astype(F32)).astype(BF16)


def collect_own(keep, arrived, sides, units):
    return [sum([part[k].astype(F32) for part in (arrived, *sides)], keep[k].astype(F32)) for k in units]


def settle_rows(total, side):
    half = total.shape[0] // 2
    other = swap_x(by_side(side, total[half:], total[:half]).astype(BF16)).astype(F32)
    return by_side(side, total[:half], total[half:]) + other


def settle(total, side):
    half = total.shape[0] // 2
    mine = by_side(side, total[:half], total[half:])
    other = swap_x(by_side(side, total[half:], total[:half]).astype(BF16)).astype(F32)
    return by_side(side, mine, other), by_side(side, other, mine)


def file_rows(keep, send, me, side, half, lanes, source):
    groups = keep.shape[0] // 4
    size = keep.shape[1]
    for rel in range(4 * groups):
        slot = ((half ^ side) * 2 + rel // 2 % 2) * groups + rel // 4
        start = pl.multiple_of((me ^ rel) * size, 8)
        block = source[pl.ds(start, size), :].astype(BF16)
        (send if rel % 2 else keep)[slot, :, lanes] = block


def pack_kernel(place_ref, gain_attn_ref, gain_mlp_ref, *refs):
    qkv_refs, mlp_refs = refs[:3], refs[3:6]
    unit_ref, own_ref, give_ref, wide_s = refs[6:]
    rows, width = qkv_refs[0].shape
    halves = []
    for h, gain_ref in enumerate((gain_attn_ref, gain_mlp_ref)):
        wide_s[...] = jnp.zeros_like(wide_s)
        wide_s[0:1, :rows] = gain_ref[...].astype(F32)
        columns = []
        for pair in range(h * width // PAIR // 2, (h + 1) * width // PAIR // 2):
            columns += [ref[:, pair * PAIR : (pair + 1) * PAIR] for ref in qkv_refs]
        gains = jnp.transpose(wide_s[...])[:rows]
        halves.append(jnp.concatenate([jnp.concatenate(columns, 1).astype(F32), gains], 1))
    unit_ref[...] = jnp.concatenate(halves, 0).astype(BF16)
    side = place_ref[1]
    done = 0
    for ref in mlp_refs:
        half = ref.shape[1] // 2
        lanes = slice(done, done + half)
        first, second = ref[:, :half], ref[:, half:]

        @pl.when(side == 0)
        def _():
            own_ref[:, lanes] = first
            give_ref[:, lanes] = second

        @pl.when(side == 1)
        def _():
            own_ref[:, lanes] = second
            give_ref[:, lanes] = first

        done += half


def pack(place, gains, qkv_weights, mlp_weights):
    rows, width = qkv_weights[0].shape
    cols = sum(w.shape[1] for w in mlp_weights) // 2
    whole_in = pl.BlockSpec(memory_space=pltpu.VMEM)
    return pl.pallas_call(
        pack_kernel,
        in_specs=[SCALARS] + [whole_in] * 8,
        out_specs=[whole_in] * 3,
        out_shape=[
            jax.ShapeDtypeStruct((2 * rows, 3 * width // 2 + 128), BF16),
            jax.ShapeDtypeStruct((rows, cols), BF16),
            jax.ShapeDtypeStruct((rows, cols), BF16),
        ],
        scratch_shapes=[pltpu.VMEM((128, 128), F32)],
        compiler_params=params(),
        cost_estimate=pl.CostEstimate(flops=0, bytes_accessed=MIB, transcendentals=0),
        name="pack",
    )(place, *[gain[None, :] for gain in gains], *qkv_weights, *mlp_weights)


TRIPLE = 3 * PAIR


def project_kernel(place_ref, own_ref, third_ref, fourth_ref, *refs):
    pieces, (qkv_ref, n1_ref, gain_ref, held, staged, sems) = refs[:8], refs[-6:]
    step = pl.program_id(0)
    width = own_ref.shape[1]
    cols = 3 * width // 2

    @pl.when(pl.program_id(0) == 0)
    def _():
        me, side = place_ref[0], place_ref[1]
        pairs, rows = staged.shape[1:3]
        copies = []
        for at, (ref, k, x, rel) in enumerate(listing(pieces)):
            copies.append(pltpu.make_async_copy(ref.at[k], staged.at[side ^ x, me ^ rel], sems.at[at]))
        for copy in copies:
            copy.start()
        for copy in copies:
            copy.wait()
        own = rows // 2
        for pair in range(pairs):
            units = [staged[x, pair].astype(F32) for x in range(2)]
            for h in range(2):
                both_rows = jnp.concatenate([unit[h * own : (h + 1) * own] for unit in units], 0)
                held[h, pair * rows : (pair + 1) * rows, :] = both_rows.astype(BF16)
        for h in range(2):
            gain_ref[h * 8 : h * 8 + 8, :] = jnp.transpose(held[h, :, cols:].astype(F32))[:8]

    short = own_ref.shape[0] - third_ref.shape[0]
    third = jnp.concatenate([third_ref[...], fourth_ref[:short, :]], 0)
    x = jnp.where(step < 2, own_ref[...], jnp.where(step == 2, third, fourth_ref[short:, :])).astype(F32)
    root = lax.rsqrt(jnp.mean(x * x, -1, keepdims=True) + EPS)
    n1 = (x * root * gain_ref[0:1, :]).astype(BF16)
    n1_ref[...] = n1
    is_query = lax.broadcasted_iota(jnp.int32, (1, cols), 1) % TRIPLE < PAIR
    scale = jnp.where(is_query, HEAD_DIM**-0.5, 1.0)
    for h in range(2):
        qkv_ref[:, h * cols : (h + 1) * cols] = (nn(n1, held[h, :, :cols]) * scale).astype(BF16)


def project(place, own, others, pieces, ready=()):
    rows, width = 2 * own.shape[0], own.shape[1]
    tile = rows // 4
    groups, unit_rows, unit_cols = pieces[0].shape
    held = (2, width, unit_cols)
    return pl.pallas_call(
        project_kernel,
        grid=(4,),
        in_specs=[SCALARS, pl.BlockSpec((tile, width), lambda i: (jnp.minimum(i, 1), 0))]
        + [whole(part.shape) for part in others]
        + [APART] * (len(pieces) + len(ready)),
        out_specs=[
            pl.BlockSpec((tile, 3 * width), lambda i: (i, 0)),
            pl.BlockSpec((tile, width), lambda i: (i, 0)),
            whole((16, width)),
            whole(held),
        ],
        out_shape=[
            jax.ShapeDtypeStruct((rows, 3 * width), BF16),
            jax.ShapeDtypeStruct((rows, width), BF16),
            jax.ShapeDtypeStruct((16, width), F32),
            jax.ShapeDtypeStruct(held, BF16),
        ],
        scratch_shapes=[
            pltpu.VMEM((2, 4 * groups, unit_rows, unit_cols), BF16),
            pltpu.SemaphoreType.DMA((len(pieces) * groups,)),
        ],
        compiler_params=params(),
        cost_estimate=pl.CostEstimate(
            flops=18 * rows * width * width, bytes_accessed=16 * rows * width, transcendentals=0
        ),
        name="project",
    )(place, own, *others, *pieces, *ready)


def nt(left, right):
    return lax.dot_general(left, right, (((1,), (1,)), ((), ())), preferred_element_type=F32)


def tn(left, right):
    return lax.dot_general(left, right, (((0,), (0,)), ((), ())), preferred_element_type=F32)


def nn(left, right):
    return jnp.dot(left, right, preferred_element_type=F32)


STRIP = 128


def head_mask(head):
    lanes = lax.broadcasted_iota(jnp.int32, (1, PAIR), 1)
    return (lanes // HEAD_DIM) == head


SAFE = 60.0
QUERIES = 512


def attend_kernel(qkv_ref, *refs):
    o_ref, lse_ref, lse_s = refs[-3:]
    q_ref, keys, value = qkv_ref.at[:, pl.ds(0, PAIR)], qkv_ref[:, PAIR : 2 * PAIR], qkv_ref[:, 2 * PAIR :]
    masks = [head_mask(h) for h in range(2)]
    values = [jnp.where(mask, value, jnp.ones_like(value)) for mask in masks]
    size = min(QUERIES, q_ref.shape[0])

    def blocks(shifted):
        for start in range(0, q_ref.shape[0], size):
            rows = slice(start, start + size)
            queries = q_ref[rows, :]
            mixed, peaks = [], []
            for h in range(2):
                own = jnp.where(masks[h], queries, jnp.zeros_like(queries))
                scores = nt(own, keys)
                expo = []
                peaks.append(jnp.max(scores, -1, keepdims=True) if shifted else 0.0)
                for s in range(0, size, 64):
                    strip = scores[s : s + 64]
                    expo.append(jnp.exp(strip - peaks[h][s : s + 64] if shifted else strip).astype(BF16))
                mixed.append(nn(jnp.concatenate(expo, 0), values[h]))
            summed = pltpu.roll(jnp.where(masks[0], mixed[1], mixed[0]), HEAD_DIM, 1)
            o_ref[rows, :] = (jnp.where(masks[0], mixed[0], mixed[1]) * (1.0 / summed)).astype(BF16)
            peak = jnp.where(masks[0], peaks[0], peaks[1]) if shifted else 0.0
            lse_s[rows, :] = peak + jnp.log(summed)

    longest = []
    for part in (q_ref[...], keys):
        wide = part.astype(F32)
        longest.append(jnp.max(jnp.sum(wide * wide, -1, keepdims=True)))
    safe = longest[0] * longest[1] < SAFE * SAFE
    pl.when(safe)(lambda: blocks(False))
    pl.when(jnp.logical_not(safe))(lambda: blocks(True))
    turned = jnp.transpose(lse_s[...])
    for h in range(2):
        lse_ref[0, h : h + 1, :] = turned[h * HEAD_DIM : h * HEAD_DIM + 1]


def attend_fast(qkv, first, count, ready=()):
    rows = qkv.shape[0]
    return pl.pallas_call(
        attend_kernel,
        grid=(count,),
        in_specs=[pl.BlockSpec((rows, TRIPLE), lambda i: (0, first + i))] + [APART] * len(ready),
        out_specs=[
            pl.BlockSpec((rows, PAIR), lambda i: (0, i)),
            pl.BlockSpec((1, 8, rows), lambda i: (i, 0, 0)),
        ],
        out_shape=[
            jax.ShapeDtypeStruct((rows, count * PAIR), BF16),
            jax.ShapeDtypeStruct((count, 8, rows), F32),
        ],
        scratch_shapes=[pltpu.VMEM((rows, PAIR), F32)],
        compiler_params=params(),
        cost_estimate=pl.CostEstimate(
            flops=32 * rows * rows * count * PAIR, bytes_accessed=8 * rows * count * PAIR, transcendentals=0
        ),
        name="attend",
    )(qkv, *ready)


HIDDEN = 512


def mlp_kernel(place_ref, source_ref, weight_ref, x_ref, own_g_ref, third_g_ref, fourth_g_ref, gain_ref, *refs):
    (act_ref, other_ref, dx1_ref, do_ref, keep_ref, send_ref, keep_down_ref, send_down_ref, dgain_ref,
     held, down, g_ref, x1_s, n2_s, n2t_s, dy_s, acts, dn2, hid_s, dg_s, du_s, part_s, sems, sems_later) = refs[-24:]
    pieces, down_pieces, o_refs = refs[:8], refs[8:12], refs[12:-24]
    me, side = place_ref[0], place_ref[1]
    scale = weight_ref[source_ref[side]]
    step = pl.program_id(0)
    rows, width = x_ref.shape
    hidden_size = down.shape[0]
    blocks = rows // TILE
    half = width // 2
    units = hidden_size // 2
    gain = gain_ref[8:9, :]
    pair_rows = keep_ref.shape[1]
    per_pair = keep_down_ref.shape[1]

    @pl.when(step == 0)
    def _():
        first, later = [], []
        for ref, k, x, rel in listing(pieces):
            pair = me ^ rel
            at_half = side ^ x
            source = ref.at[k]
            at = pl.ds(pl.multiple_of(pair * pair_rows, 16), pair_rows)
            for copies, sem, lanes in ((first, sems, pl.ds(0, half)), (later, sems_later, pl.ds(half, 2 * units))):
                copies.append(
                    pltpu.make_async_copy(source.at[:, lanes], held.at[at_half, at, lanes], sem.at[len(copies)])
                )
        for ref, k, _, rel in listing(down_pieces, DOWN_PIECES):
            at = pl.ds(pl.multiple_of((me ^ rel) * per_pair, 16), per_pair)
            later.append(pltpu.make_async_copy(ref.at[k], down.at[at, :], sems_later.at[len(later)]))
        for copy in first + later:
            copy.start()
        done = 0
        for ref in (own_g_ref, third_g_ref, fourth_g_ref):
            g_ref[done : done + ref.shape[0], :] = ref[...]
            done += ref.shape[0]
        for copy in first:
            copy.wait()

        @pl.loop(0, blocks)
        def _(i):
            at = pl.ds(pl.multiple_of(i * TILE, TILE), TILE)
            heads = jnp.concatenate([ref[at, :] for ref in o_refs], 1)
            mixed = jnp.concatenate([nn(heads, held[h, :, :half]) for h in range(2)], 1)
            x1 = x_ref[at, :].astype(F32) + mixed
            x1_s[at, :] = x1
            acts[at, :] = x1
            root = lax.rsqrt(jnp.mean(x1 * x1, -1, keepdims=True) + EPS)
            n2_s[at, :] = (x1 * root * gain).astype(BF16)
            dy_s[at, :] = (g_ref[at, :].astype(F32) * scale).astype(BF16)
            dn2[at, :] = jnp.zeros((TILE, width), F32)

        for i in range(blocks):
            n2t_s[:, i * TILE : (i + 1) * TILE] = jnp.transpose(n2_s[i * TILE : (i + 1) * TILE, :])
        for copy in later:
            copy.wait()

    in_half = units // HIDDEN
    at_half = step // in_half
    lane = (step % in_half) * HIDDEN
    gate_at = pl.ds(pl.multiple_of(half + lane, 128), HIDDEN)
    up_at = pl.ds(pl.multiple_of(half + units + lane, 128), HIDDEN)
    w_gate = held[at_half, :, gate_at]
    w_up = held[at_half, :, up_at]
    hidden_rows = pl.ds(pl.multiple_of(step * HIDDEN, HIDDEN), HIDDEN)
    w_down = down[hidden_rows, :]
    c_one = math.sqrt(2 / math.pi)
    c_two = 0.044715 * c_one
    half_rows = rows // 2
    for base in range(0, rows, half_rows):
        at = slice(base, base + half_rows)
        gate_all = nn(n2_s[at, :], w_gate)
        up_all = nn(n2_s[at, :], w_up)
        dh_all = nt(dy_s[at, :], w_down)
        for s in range(0, half_rows, STRIP // 2):
            strip = slice(s, s + STRIP // 2)
            out = slice(base + s, base + s + STRIP // 2)
            gate, up, dh = gate_all[strip], up_all[strip], dh_all[strip]
            squared = gate * gate
            bend = jnp.tanh(gate * (c_one + c_two * squared))
            rise = 0.5 + 0.5 * bend
            gelu = gate * rise
            slope = rise + gate * (0.5 * (1.0 - bend * bend)) * (c_one + 3.0 * c_two * squared)
            hid_s[out, :] = (gelu * up).astype(BF16)
            dg_s[out, :] = (dh * up * slope).astype(BF16)
            du_s[out, :] = (dh * gelu).astype(BF16)
        acts[at, :] += nn(hid_s[at, :], w_down)
        dn2[at, :] += nt(dg_s[at, :], w_gate) + nt(du_s[at, :], w_up)

    for values, lanes in ((dg_s, gate_at), (du_s, up_at)):
        part_s[:, :HIDDEN] = nn(n2t_s[...], values[...])
        file_rows(keep_ref, send_ref, me, side, at_half, lanes, part_s.at[:, pl.ds(0, HIDDEN)])

    groups = keep_ref.shape[0] // 4
    step_total = tn(hid_s[...], dy_s[...]).astype(BF16)
    for nth in range(HIDDEN // per_pair):
        rel = (step * (HIDDEN // per_pair) + nth) ^ me
        slot = rel // 2 % 2 * groups + rel // 4
        block = step_total[nth * per_pair : (nth + 1) * per_pair]

        @pl.when(rel % 2 == 0)
        def _():
            keep_down_ref[slot] = block

        @pl.when(rel % 2 == 1)
        def _():
            send_down_ref[slot] = block

    @pl.when(step == pl.num_programs(0) - 1)
    def _():
        dgain_ref[...] = jnp.zeros_like(dgain_ref)

        act_ref[...] = acts[: rows // 2, :].astype(BF16)
        other_ref[...] = acts[rows // 2 :, :].astype(BF16)

        @pl.loop(0, blocks)
        def _(i):
            at = pl.ds(pl.multiple_of(i * TILE, TILE), TILE)
            x1 = x1_s[at, :]
            root = lax.rsqrt(jnp.mean(x1 * x1, -1, keepdims=True) + EPS)
            back = dn2[at, :]
            unit_x1 = x1 * root
            dgain_ref[0:1, :] += jnp.sum(back * unit_x1, 0, keepdims=True)
            lifted = back * gain
            inner = jnp.mean(lifted * unit_x1, -1, keepdims=True)
            d_x1 = g_ref[at, :].astype(F32) * scale + root * (lifted - unit_x1 * inner)
            dx1_ref[at, :] = d_x1
            low = d_x1.astype(BF16)
            n2_s[at, :] = low
            do = nt(low[:, :half], held[0, :, :half]) + nt(low[:, half:], held[1, :, :half])
            do_ref[at, :] = do.astype(BF16)

        done = 0
        for ref in o_refs:
            count = ref.shape[1]
            part_s[done : done + count, :] = tn(ref[...], n2_s[...])
            done += count
        for h in range(2):
            file_rows(keep_ref, send_ref, me, side, h, slice(0, half), part_s.at[:, pl.ds(h * half, half)])


def mlp(place, source, weight, heads, x, grads, gains, pieces, down_pieces):
    rows, width = x.shape
    groups, pair_rows, cols = pieces[0].shape
    per_pair = down_pieces[0].shape[1]
    hidden = 4 * groups * per_pair
    kept = (4 * groups, pair_rows, cols)
    kept_down = (2 * groups, per_pair, width)
    units = sum(piece.shape[0] for piece in pieces)
    return pl.pallas_call(
        mlp_kernel,
        grid=(hidden // HIDDEN,),
        in_specs=[SCALARS] * 3
        + [whole((rows, width))]
        + [whole(part.shape) for part in grads]
        + [whole(gains.shape)]
        + [APART] * (len(pieces) + len(down_pieces))
        + [whole(part.shape) for part in heads],
        out_specs=[whole((rows // 2, width))] * 2
        + [whole((rows, width))] * 2
        + [whole(kept)] * 2
        + [whole(kept_down)] * 2
        + [whole((8, width))],
        out_shape=[
            jax.ShapeDtypeStruct((rows // 2, width), BF16),
            jax.ShapeDtypeStruct((rows // 2, width), BF16),
            jax.ShapeDtypeStruct((rows, width), F32),
            jax.ShapeDtypeStruct((rows, width), BF16),
            jax.ShapeDtypeStruct(kept, BF16),
            jax.ShapeDtypeStruct(kept, BF16),
            jax.ShapeDtypeStruct(kept_down, BF16),
            jax.ShapeDtypeStruct(kept_down, BF16),
            jax.ShapeDtypeStruct((8, width), F32),
        ],
        scratch_shapes=[
            pltpu.VMEM((2, width, width // 2 + hidden), BF16),
            pltpu.VMEM((hidden, width), BF16),
            pltpu.VMEM((rows, width), BF16),
            pltpu.VMEM((rows, width), F32),
            pltpu.VMEM((rows, width), BF16),
            pltpu.VMEM((width, rows), BF16),
            pltpu.VMEM((rows, width), BF16),
            pltpu.VMEM((rows, width), F32),
            pltpu.VMEM((rows, width), F32),
            pltpu.VMEM((rows, HIDDEN), BF16),
            pltpu.VMEM((rows, HIDDEN), BF16),
            pltpu.VMEM((rows, HIDDEN), BF16),
            pltpu.VMEM((width, width), F32),
            pltpu.SemaphoreType.DMA((units,)),
            pltpu.SemaphoreType.DMA((units + 4 * groups,)),
        ],
        compiler_params=params(),
        cost_estimate=pl.CostEstimate(
            flops=4 * rows * width * (3 * width + 9 * hidden),
            bytes_accessed=40 * MIB,
            transcendentals=0,
        ),
        name="mlp",
    )(place, source, weight, x, *grads, gains, *pieces, *down_pieces, *heads)


def attend_back_kernel(qkv_ref, do_ref, o_ref, lse_ref, *refs):
    d_ref, token_ref, dk_s, dv_s = refs[-4:]
    q_ref, keys, values = qkv_ref.at[:, pl.ds(0, PAIR)], qkv_ref[:, PAIR : 2 * PAIR], qkv_ref[:, 2 * PAIR :]
    total = keys.shape[0]
    token_ref[...] = jnp.zeros_like(token_ref)
    scale = HEAD_DIM**-0.5
    k_own = jnp.concatenate([jnp.where(head_mask(h), keys, jnp.zeros_like(keys)) for h in range(2)], 0)
    prod = do_ref[...].astype(F32) * o_ref[...].astype(F32)
    high = prod.astype(BF16)
    low = (prod - high.astype(F32)).astype(BF16)
    chosen = (
        lax.broadcasted_iota(jnp.int32, (8, PAIR), 1) // HEAD_DIM
        == lax.broadcasted_iota(jnp.int32, (8, PAIR), 0)
    ).astype(BF16)
    delta = nt(chosen, high) + nt(chosen, low)
    for block in range(q_ref.shape[0] // TILE):
        rows = slice(block * TILE, (block + 1) * TILE)
        queries, d_out = q_ref[rows, :], do_ref[rows, :]
        q_own, d_own, probs, slopes = [], [], [], []
        for h in range(2):
            mask = head_mask(h)
            q_own.append(jnp.where(mask, queries, jnp.zeros_like(queries)))
            d_own.append(jnp.where(mask, d_out, jnp.zeros_like(d_out)))
            scores = nt(keys, q_own[h])
            d_probs = nt(values, d_own[h])
            lse = lse_ref[0, h : h + 1, rows]
            center = delta[h : h + 1, rows]
            p_strips, s_strips = [], []
            for s in range(total // STRIP):
                strip = slice(s * STRIP, (s + 1) * STRIP)
                p = jnp.exp(scores[strip] - lse)
                p_strips.append(p.astype(BF16))
                s_strips.append((p * (d_probs[strip] - center)).astype(BF16))
            probs.append(jnp.concatenate(p_strips, 0))
            slopes.append(jnp.concatenate(s_strips, 0))
        d_ref[rows, :PAIR] = (tn(jnp.concatenate(slopes, 0), k_own) * scale).astype(BF16)
        d_keys = nn(jnp.concatenate(slopes, 1), jnp.concatenate(q_own, 0))
        d_values = nn(jnp.concatenate(probs, 1), jnp.concatenate(d_own, 0))
        if block == 0:
            dk_s[...] = d_keys
            dv_s[...] = d_values
        else:
            dk_s[...] += d_keys
            dv_s[...] += d_values
    d_ref[:, PAIR : 2 * PAIR] = dk_s[...].astype(BF16)
    d_ref[:, 2 * PAIR :] = dv_s[...].astype(BF16)


def attend_back_fast(qkv, d_out, heads, lse, first, d_qkv, ready=()):
    rows = d_out.shape[0]
    count = lse.shape[0]
    into = [] if d_qkv is None else [d_qkv]
    return pl.pallas_call(
        attend_back_kernel,
        grid=(count,),
        in_specs=[
            pl.BlockSpec((rows, TRIPLE), lambda i: (0, first + i)),
            pl.BlockSpec((rows, PAIR), lambda i: (0, first + i)),
            pl.BlockSpec((rows, PAIR), lambda i: (0, i)),
            pl.BlockSpec((1, 8, rows), lambda i: (i, 0, 0)),
        ]
        + [APART] * (len(into) + len(ready)),
        out_specs=[pl.BlockSpec((rows, TRIPLE), lambda i: (0, first + i)), whole((8, 128))],
        out_shape=[jax.ShapeDtypeStruct(qkv.shape, BF16), jax.ShapeDtypeStruct((8, 128), F32)],
        input_output_aliases={4: 0} if into else {},
        scratch_shapes=[pltpu.VMEM((rows, PAIR), F32)] * 2,
        compiler_params=params(),
        cost_estimate=pl.CostEstimate(
            flops=50 * rows * rows * count * PAIR, bytes_accessed=16 * rows * count * PAIR, transcendentals=0
        ),
        name="attend_back",
    )(qkv, d_out, heads, lse, *into, *ready)


def input_back_kernel(d_ref, w_ref, x_ref, dx1_ref, gain_ref, *refs):
    own_ref, *other_refs, dgain_ref = refs[-4:]
    step = pl.program_id(0)
    cols = d_ref.shape[1] // 2
    back = nt(d_ref[:, :cols], w_ref[0, :, :cols]) + nt(d_ref[:, cols:], w_ref[1, :, :cols])
    x = x_ref[...].astype(F32)
    root = lax.rsqrt(jnp.mean(x * x, -1, keepdims=True) + EPS)
    unit = x * root

    @pl.when(step == 0)
    def _():
        dgain_ref[...] = jnp.zeros_like(dgain_ref)

    dgain_ref[0:1, :] += jnp.sum(back * unit, 0, keepdims=True)
    lifted = back * gain_ref[0:1, :]
    inner = jnp.mean(lifted * unit, -1, keepdims=True)
    d_x = dx1_ref[...] + root * (lifted - unit * inner)

    @pl.when(step == 0)
    def _():
        own_ref[...] = d_x

    @pl.when(step == 1)
    def _():
        done = 0
        for ref in other_refs:
            ref[...] = d_x[done : done + ref.shape[0]].astype(BF16)
            done += ref.shape[0]


def input_back(d_qkv, weights, x, d_x1, gains, ready=()):
    rows, width = x.shape
    tile = rows // 2
    block = pl.BlockSpec((tile, width), lambda i: (i, 0))
    return pl.pallas_call(
        input_back_kernel,
        grid=(2,),
        in_specs=[
            pl.BlockSpec((tile, d_qkv.shape[1]), lambda i: (i, 0)),
            whole(weights.shape),
            block,
            block,
            whole(gains.shape),
        ]
        + [APART] * len(ready),
        out_specs=[whole((tile, width))]
        + [whole((tile // 2, width))] * 2
        + [whole((8, width))],
        out_shape=[
            jax.ShapeDtypeStruct((rows // 2, width), F32),
            jax.ShapeDtypeStruct((tile // 2, width), BF16),
            jax.ShapeDtypeStruct((tile // 2, width), BF16),
            jax.ShapeDtypeStruct((8, width), F32),
        ],
        compiler_params=params(),
        cost_estimate=pl.CostEstimate(
            flops=12 * rows * width * width, bytes_accessed=24 * rows * width, transcendentals=0
        ),
        name="input_back",
    )(d_qkv, weights, x, d_x1, gains, *ready)


def file_devices(keep, send, me, side, lanes, sources):
    groups = keep.shape[0] // 4
    own = keep.shape[1] // 2
    for rel in range(4 * groups):
        for x in range(2):
            start = pl.multiple_of((me ^ rel) * 2 * own + (side ^ x) * own, 8)
            block = jnp.concatenate([source[pl.ds(start, own), :] for source in sources], 0)
            slot = (x * 2 + rel // 2 % 2) * groups + rel // 4
            (send if rel % 2 else keep)[slot, :, lanes] = block.astype(BF16)


def project_back_kernel(place_ref, first_ref, second_ref, n1_ref, *refs):
    gain_refs, (keep_ref, send_ref, first_s, second_s, turned_s, wide_s) = refs[:2], refs[-6:]
    me, side = place_ref[0], place_ref[1]
    step = pl.program_id(0)
    rows, width = n1_ref.shape

    @pl.when(step == 0)
    def _():
        for i in range(rows // TILE):
            turned_s[:, i * TILE : (i + 1) * TILE] = jnp.transpose(n1_ref[i * TILE : (i + 1) * TILE, :])
        for ref, part in zip(gain_refs, (first_s, second_s)):
            wide_s[...] = jnp.zeros_like(wide_s)
            wide_s[0:1, :] = ref[0:1, :]
            part[:, :128] = jnp.transpose(wide_s[...])
        last = keep_ref.shape[2] - 128
        sources = [part.at[:, pl.ds(0, 128)] for part in (first_s, second_s)]
        file_devices(keep_ref, send_ref, me, side, slice(last, last + 128), sources)

    first_s[...] = nn(turned_s[...], first_ref[...])
    second_s[...] = nn(turned_s[...], second_ref[...])
    lanes = pl.ds(pl.multiple_of(step * TRIPLE, 128), TRIPLE)
    file_devices(keep_ref, send_ref, me, side, lanes, (first_s, second_s))


def project_back(place, d_qkv, n1, d_gains, kept, ready=()):
    rows, width = n1.shape
    steps = width // PAIR // 2
    return pl.pallas_call(
        project_back_kernel,
        grid=(steps,),
        in_specs=[
            SCALARS,
            pl.BlockSpec((rows, TRIPLE), lambda i: (0, i)),
            pl.BlockSpec((rows, TRIPLE), lambda i: (0, steps + i)),
            whole((rows, width)),
        ]
        + [whole((8, width))] * 2
        + [APART] * len(ready),
        out_specs=[whole(kept)] * 2,
        out_shape=[jax.ShapeDtypeStruct(kept, BF16)] * 2,
        scratch_shapes=[
            pltpu.VMEM((width, TRIPLE), F32),
            pltpu.VMEM((width, TRIPLE), F32),
            pltpu.VMEM((width, rows), BF16),
            pltpu.VMEM((128, width), F32),
        ],
        compiler_params=params(),
        cost_estimate=pl.CostEstimate(
            flops=12 * rows * width * width, bytes_accessed=24 * rows * width, transcendentals=0
        ),
        name="project_back",
    )(place, d_qkv, d_qkv, n1, *d_gains, *ready)


def give_half(plots, side):
    own = lax.dynamic_index_in_dim(plots, side, 0, keepdims=False)
    return own, lax.dynamic_index_in_dim(plots, 1 - side, 0, keepdims=False)


def halves_back(own, arrived, side):
    arrived = arrived.astype(own.dtype)
    return jnp.stack([by_side(side, own, arrived), by_side(side, arrived, own)])


CALLS = (3, 2, 1)


def local_fast(size, *arguments):
    (inputs, out_grad, source_id, source_weight, gain_attn, gain_mlp,
     w_query, w_key, w_value, w_attn_out, w_gate, w_up, w_down) = arguments
    half_rows, width = inputs.shape[1:]
    half = width // 2
    hidden = w_gate.shape[1]
    groups = size // 4
    side = lax.axis_index("narrow")
    place = jnp.stack([lax.axis_index("wide"), side]).astype(jnp.int32)

    pairs = width // PAIR
    unit_a, unit_b, give = pack(
        place, (gain_attn, gain_mlp), (w_query, w_key, w_value), (w_attn_out, w_gate, w_up)
    )
    stack_a = spread_z(unit_a, size)
    unit_b = pair_up(unit_b, give, side)
    unit_c = pair_up(w_down, after(w_down, unit_a), side)
    quarter = half_rows // 2
    own_x, give_x = give_half(after(inputs, unit_a), side)
    short = quarter // 2
    others = [swap_x(give_x[:short])]
    stack_a, unit_b, unit_c, others[0] = lax.optimization_barrier((stack_a, unit_b, unit_c, others[0]))
    x_a, y_a = spread_xy(stack_a, size)
    units_b = [unit_b, None, swap(unit_b, 8, size)]
    near_c = swap(unit_c, 4, size)
    x_a, y_a, units_b[2], near_c = lax.optimization_barrier((x_a, y_a, units_b[2], near_c))
    d_a = swap(x_a, 2, size)
    others.append(swap_x(after(give_x[short:], x_a)))
    unit_b = after(unit_b, y_a)
    units_b[1] = swap(unit_b, 4, size)
    units_b += [swap(unit_b, 4 * k, size) for k in range(3, groups)]
    d_a, others[1], units_b[1], *units_b[3:] = lax.optimization_barrier((d_a, others[1], units_b[1], *units_b[3:]))
    pieces_a = [stack_a, x_a, y_a, d_a]
    own_grad, give_grad = give_half(after(out_grad, x_a), side)
    grads = [own_grad, swap_x(give_grad[:quarter]), swap_x(after(give_grad[quarter:], d_a))]
    pieces_a += [swap(piece, 1, size) for piece in pieces_a]

    stack_b = jnp.stack(units_b)
    unit_c = after(unit_c, *pieces_a[4:])
    units_c = [unit_c, near_c] + [swap(unit_c, 4 * k, size) for k in range(2, groups)]
    qkv, n1, gains, weights = project(place, own_x, others, pieces_a, [stack_b])
    x_b, y_b = spread_xy(stack_b, size)
    heads, lses = [], []
    for call, count in enumerate(CALLS):
        ready = [[grads[1]], [*heads, y_b, *units_c], [*heads, grads[2]]][call]
        made = attend_fast(qkv, sum(CALLS[:call]), count, ready)
        heads.append(made[0])
        lses.append(made[1])
        if call == 0:
            y_b, stack_b, *units_c = lax.optimization_barrier((y_b, stack_b, *units_c, heads[-1]))[:-1]
            d_b = swap_x(y_b)
            stack_c = jnp.stack(units_c)
            y_c = swap(stack_c, 2, size)
            twins_b = [swap(stack_b, 1, size), swap(y_b, 1, size)]
            twins_c = [swap(stack_c, 1, size)]
    x = jnp.concatenate(lax.optimization_barrier((own_x, *others, heads[-1]))[:3], 0)
    x_b, d_b, y_c, _ = lax.optimization_barrier((x_b, d_b, y_c, heads[-1]))
    pieces_b = [stack_b, x_b, y_b, d_b]
    pieces_b += [twins_b[0], swap(x_b, 1, size), twins_b[1], swap(d_b, 1, size)]
    pieces_c = [stack_c, y_c, *twins_c, swap(y_c, 1, size)]
    acts, other_acts, d_x1, d_out, keep, send, keep_c, send_c, d_gain = mlp(
        place, source_id, source_weight, heads, x, grads, gains, pieces_b, pieces_c
    )

    twin = swap(send, 1, size)
    twin_c = swap(send_c, 1, size)
    other_acts = swap_x(other_acts)
    d_qkv = None
    ready = []
    for call in reversed(range(len(CALLS))):
        start = sum(CALLS[:call])
        d_qkv, token = attend_back_fast(qkv, d_out, heads[call], lses[call], start, d_qkv, ready)
        if call == 2:
            twin, twin_c = lax.optimization_barrier((twin, twin_c, token))[:2]
            diagonal, over_y = diagonal_of(keep, twin), over_y_of(keep, twin)
            corner = swap(diagonal, 2, size)
            by_y = swap(after(over_y, diagonal), 2, size)
            ready = [diagonal, over_y, token]
        elif call == 1:
            over_y_c = chip_sum(keep_c, after(twin_c, token), 1, 2).astype(BF16)
            twin, other_acts, corner, over_y_c = lax.optimization_barrier((twin, other_acts, corner, over_y_c, token))[:4]
            over_x = over_x_of(keep, twin, corner)
            by_x = swap_x(over_x)
            ready = [over_x, token, other_acts, over_y_c]
    twin, by_x, by_y = lax.optimization_barrier((twin, by_x, by_y, token))[:3]
    sides = (by_x, by_y)
    far = [unit.astype(BF16) for unit in collect_own(keep, twin, sides, range(1, groups))]
    arrived_c = swap(after(over_y_c, by_y), 2, size)
    own, *other, d_gain_attn = input_back(d_qkv, weights, x, d_x1, gains, far)
    others = [swap_x(part) for part in other]
    kept = (4 * groups, *unit_a.shape)
    arrived = [swap(far[k - 1], 4 * k, size) for k in range(1, groups)]
    keep_a, send_a = project_back(place, d_qkv, n1, (d_gain_attn, d_gain), kept, [own, arrived[0]])
    send_a, arrived_c, others[0], *arrived[1:] = lax.optimization_barrier((send_a, arrived_c, others[0], *arrived[1:]))
    twin_a = swap(send_a, 1, size)
    diagonal = diagonal_of(keep_a, twin_a)
    corner = swap(diagonal, 2, size)
    keep, twin, by_x, by_y, keep_c, twin_c = lax.optimization_barrier(
        (keep, twin, by_x, by_y, keep_c, twin_c, diagonal)
    )[:6]
    total_c = chip_sum(keep_c, twin_c, 0, 2) + arrived_c.astype(F32)
    far_c = [swap(total_c[k].astype(BF16), 4 * k, size) for k in range(1, groups)]
    total_b = sum([part.astype(F32) for part in arrived], collect_own(keep, twin, (by_x, by_y), [0])[0])
    first_b, second_b = settle(total_b, side)
    twin_a, corner, others[1], first_b = lax.optimization_barrier((twin_a, corner, others[1], first_b))
    sides = [swap_x(over_x_of(keep_a, twin_a, corner)), swap(over_y_of(keep_a, twin_a), 2, size)]
    twin_a, *rest = lax.optimization_barrier((twin_a, *sides, *far_c))
    sides, far_c = rest[:2], rest[2:]
    units = collect_own(keep_a, twin_a, sides, range(groups))
    arrived = [swap(units[k].astype(BF16), 4 * k, size) for k in range(1, groups)]
    far_c[-1] = after(far_c[-1], units[0])
    others[1], other_acts, _ = lax.optimization_barrier((others[1], other_acts, units[0]))
    activations = halves_back(acts, other_acts, side)
    input_grad = halves_back(own, jnp.concatenate(others, 0), side)
    grad_down = settle_rows(sum([part.astype(F32) for part in far_c], total_c[0]), side)
    arrived[0], grad_down = lax.optimization_barrier((arrived[0], grad_down))
    total_a = sum([part.astype(F32) for part in arrived], units[0])
    own_rows = unit_a.shape[0] // 2
    first_a, second_a = total_a[:own_rows], total_a[own_rows:]

    def in_order(part):
        return jnp.concatenate(
            [
                piece[:, pair * TRIPLE + part * PAIR : pair * TRIPLE + (part + 1) * PAIR]
                for piece in (first_a, second_a)
                for pair in range(pairs // 2)
            ],
            1,
        )

    def joined(first, second, start, count):
        return jnp.concatenate([first[:, start : start + count], second[:, start : start + count]], 1)

    units = hidden // 2
    return (
        activations,
        input_grad,
        first_a[:, 3 * half],
        second_a[:, 3 * half],
        in_order(0),
        in_order(1),
        in_order(2),
        joined(first_b, second_b, 0, half),
        joined(first_b, second_b, half, units),
        joined(first_b, second_b, half + units, units),
        grad_down,
    )


def solution(mesh):
    size = mesh.shape["wide"]
    fits = mesh.shape["narrow"] == 2 and size == 16
    body = functools.partial(local_fast, size) if fits else local
    placed = (
        P("wide", "narrow", None),
        P("wide", "narrow", None),
        P("wide"),
        P(),
        P(("wide", "narrow")),
        P(("wide", "narrow")),
        P(("wide", "narrow"), None),
        P(("wide", "narrow"), None),
        P(("wide", "narrow"), None),
        P(("wide", "narrow"), None),
        P(("wide", "narrow"), None),
        P(("wide", "narrow"), None),
        P(("wide", "narrow"), None),
    )
    return jax.shard_map(
        body,
        mesh=mesh,
        in_specs=placed,
        out_specs=(
            P("wide", "narrow", None),
            P("wide", "narrow", None),
            P(("wide", "narrow")),
            P(("wide", "narrow")),
            P(("wide", "narrow"), None),
            P(("wide", "narrow"), None),
            P(("wide", "narrow"), None),
            P(("wide", "narrow"), None),
            P(("wide", "narrow"), None),
            P(("wide", "narrow"), None),
            P(("wide", "narrow"), None),
        ),
        check_vma=False,
    )
```

```python
import functools
import math

import jax
import jax.numpy as jnp
from jax import lax
from jax.experimental import pallas as pl
from jax.experimental.pallas import tpu as pltpu
from jax.sharding import PartitionSpec as P

HEADS = 12
HEAD_DIM = 64


EPS = 1e-06
HIGH = lax.Precision.HIGHEST


def rms(value, gain):
    return value * lax.rsqrt(jnp.mean(value * value, -1, keepdims=True) + EPS) * gain


def matmul(left, right):
    return jnp.dot(left, right, preferred_element_type=jnp.float32)


def matmul_tn(left, right):
    return lax.dot_general(
        left, right, (((0,), (0,)), ((), ())), preferred_element_type=jnp.float32
    )


def matmul_nt(left, right):
    return lax.dot_general(
        left, right, (((1,), (1,)), ((), ())), preferred_element_type=jnp.float32
    )


def attend(items):
    query, keys, values = items
    rows = query.shape[0]
    total = keys.shape[0]
    scale = HEAD_DIM ** (-0.5)
    q_heads = query.reshape(rows, HEADS, HEAD_DIM)
    k_heads = keys.reshape(total, HEADS, HEAD_DIM)
    v_heads = values.reshape(total, HEADS, HEAD_DIM)
    scores = (
        jnp.einsum("rhd,shd->hrs", q_heads, k_heads, preferred_element_type=jnp.float32) * scale
    )
    peak = jnp.max(scores, -1, keepdims=True)
    expo = jnp.exp(scores - peak)
    summed = jnp.sum(expo, -1, keepdims=True)
    probs_full = expo / summed
    probs = probs_full.astype(jnp.bfloat16)
    heads_out = jnp.einsum("hrs,shd->rhd", probs, v_heads, preferred_element_type=jnp.float32)
    exact_out = jnp.einsum("hrs,shd->rhd", probs_full, v_heads.astype(jnp.float32), precision=HIGH)
    log_total = (peak + jnp.log(summed))[:, :, 0]
    return (heads_out.reshape(rows, HEADS * HEAD_DIM), log_total, exact_out)


def attend_back(items):
    query, keys, values, log_total, d_out = items
    rows = query.shape[0]
    total = keys.shape[0]
    width = HEADS * HEAD_DIM
    scale = HEAD_DIM ** (-0.5)
    q_heads = query.reshape(rows, HEADS, HEAD_DIM)
    k_heads = keys.reshape(total, HEADS, HEAD_DIM)
    v_heads = values.reshape(total, HEADS, HEAD_DIM)
    d_heads = d_out.reshape(rows, HEADS, HEAD_DIM)
    scores = (
        jnp.einsum("rhd,shd->hrs", q_heads, k_heads, preferred_element_type=jnp.float32) * scale
    )
    probs = jnp.exp(scores - log_total[:, :, None])
    probs_low = probs.astype(jnp.bfloat16)
    d_probs = jnp.einsum("rhd,shd->hrs", d_heads, v_heads, preferred_element_type=jnp.float32)
    center = jnp.sum(d_probs * probs, -1, keepdims=True)
    d_scores = (probs * (d_probs - center)).astype(jnp.bfloat16)
    d_query = (
        jnp.einsum("hrs,shd->rhd", d_scores, k_heads, preferred_element_type=jnp.float32) * scale
    )
    d_keys = (
        jnp.einsum("hrs,rhd->shd", d_scores, q_heads, preferred_element_type=jnp.float32) * scale
    )
    d_values = jnp.einsum("hrs,rhd->shd", probs_low, d_heads, preferred_element_type=jnp.float32)
    return (
        d_query.reshape(rows, width),
        d_keys.reshape(total, width),
        d_values.reshape(total, width),
    )


def local(
    inputs,
    out_grad,
    source_id,
    source_weight,
    gain_attn,
    gain_mlp,
    w_query,
    w_key,
    w_value,
    w_attn_out,
    w_gate,
    w_up,
    w_down,
):
    plots, rows, width = inputs.shape
    gathered = (
        lax.all_gather(gain_attn, ("wide", "narrow"), axis=0, tiled=True),
        lax.all_gather(gain_mlp, ("wide", "narrow"), axis=0, tiled=True),
        lax.all_gather(w_query, ("wide", "narrow"), axis=0, tiled=True),
        lax.all_gather(w_key, ("wide", "narrow"), axis=0, tiled=True),
        lax.all_gather(w_value, ("wide", "narrow"), axis=0, tiled=True),
        lax.all_gather(w_attn_out, ("wide", "narrow"), axis=0, tiled=True),
        lax.all_gather(w_gate, ("wide", "narrow"), axis=0, tiled=True),
        lax.all_gather(w_up, ("wide", "narrow"), axis=0, tiled=True),
        lax.all_gather(w_down, ("wide", "narrow"), axis=0, tiled=True),
    )
    gain_one, gain_two, wq, wk, wv, wo, wg, wu, wd = gathered
    gain_one = gain_one.astype(jnp.float32)
    gain_two = gain_two.astype(jnp.float32)
    x_rows = inputs.astype(jnp.float32).reshape(plots * rows, width)
    n1 = rms(x_rows, gain_one).astype(jnp.bfloat16)
    query = matmul(n1, wq).astype(jnp.bfloat16)
    keys_own = matmul(n1, wk).astype(jnp.bfloat16).reshape(plots, rows, width)
    values_own = matmul(n1, wv).astype(jnp.bfloat16).reshape(plots, rows, width)
    keys_all, values_all = (
        lax.all_gather(keys_own, "narrow", axis=1, tiled=True),
        lax.all_gather(values_own, "narrow", axis=1, tiled=True),
    )
    query_plots = query.reshape(plots, rows, width)
    heads_out, log_total, exact_out = lax.map(attend, (query_plots, keys_all, values_all))
    attn = heads_out.reshape(plots * rows, width).astype(jnp.bfloat16)
    x1 = x_rows + matmul(attn, wo)
    n2 = rms(x1, gain_two).astype(jnp.bfloat16)
    gate = matmul(n2, wg)
    up = matmul(n2, wu)
    gate_act, gelu_back = jax.vjp(lambda u: jax.nn.gelu(u, approximate=True), gate)
    hidden = (gate_act * up).astype(jnp.bfloat16)
    activations = (x1 + matmul(hidden, wd)).astype(jnp.bfloat16).reshape(plots, rows, width)
    onehot = (
        source_id[:, None] == jnp.arange(source_weight.shape[0], dtype=jnp.int32)[None, :]
    ).astype(jnp.float32)
    plot_scale = jnp.sum(onehot * source_weight[None, :], -1)
    cotangent = (out_grad.astype(jnp.float32) * plot_scale[:, None, None]).reshape(
        plots * rows, width
    )
    again = (
        lax.all_gather(gain_attn, ("wide", "narrow"), axis=0, tiled=True),
        lax.all_gather(gain_mlp, ("wide", "narrow"), axis=0, tiled=True),
        lax.all_gather(w_query, ("wide", "narrow"), axis=0, tiled=True),
        lax.all_gather(w_key, ("wide", "narrow"), axis=0, tiled=True),
        lax.all_gather(w_value, ("wide", "narrow"), axis=0, tiled=True),
        lax.all_gather(w_attn_out, ("wide", "narrow"), axis=0, tiled=True),
        lax.all_gather(w_gate, ("wide", "narrow"), axis=0, tiled=True),
        lax.all_gather(w_up, ("wide", "narrow"), axis=0, tiled=True),
        lax.all_gather(w_down, ("wide", "narrow"), axis=0, tiled=True),
    )
    gain_one, gain_two, wq, wk, wv, wo, wg, wu, wd = again
    gain_one = gain_one.astype(jnp.float32)
    gain_two = gain_two.astype(jnp.float32)
    d_y = cotangent.astype(jnp.bfloat16)
    d_hidden = matmul_nt(d_y, wd)
    grad_down = matmul_tn(hidden, d_y)
    d_gate = gelu_back(d_hidden * up)[0].astype(jnp.bfloat16)
    d_up = (d_hidden * gate_act).astype(jnp.bfloat16)
    grad_gate = matmul_tn(n2, d_gate)
    grad_up = matmul_tn(n2, d_up)
    d_n2 = matmul_nt(d_gate, wg) + matmul_nt(d_up, wu)
    _, norm_two_back = jax.vjp(rms, x1, gain_two)
    d_x1_norm, grad_gain_mlp = norm_two_back(d_n2)
    d_x1 = cotangent + d_x1_norm
    d_attn = d_x1.astype(jnp.bfloat16)
    grad_attn_out = matmul_tn(attn, d_attn)
    d_out = matmul_nt(d_attn, wo).astype(jnp.bfloat16).reshape(plots, rows, width)
    keys_all, values_all = (
        lax.all_gather(keys_own, "narrow", axis=1, tiled=True),
        lax.all_gather(values_own, "narrow", axis=1, tiled=True),
    )
    d_query, d_keys_part, d_values_part = lax.map(
        attend_back, (query_plots, keys_all, values_all, log_total, d_out)
    )
    d_keys, d_values = (
        lax.psum_scatter(
            d_keys_part.astype(jnp.bfloat16), "narrow", scatter_dimension=1, tiled=True
        ).astype(jnp.float32),
        lax.psum_scatter(
            d_values_part.astype(jnp.bfloat16), "narrow", scatter_dimension=1, tiled=True
        ).astype(jnp.float32),
    )
    dq_low = d_query.reshape(plots * rows, width).astype(jnp.bfloat16)
    dk_low = d_keys.reshape(plots * rows, width).astype(jnp.bfloat16)
    dv_low = d_values.reshape(plots * rows, width).astype(jnp.bfloat16)
    grad_query = matmul_tn(n1, dq_low)
    grad_key = matmul_tn(n1, dk_low)
    grad_value = matmul_tn(n1, dv_low)
    d_n1 = matmul_nt(dq_low, wq) + matmul_nt(dk_low, wk) + matmul_nt(dv_low, wv)
    _, norm_one_back = jax.vjp(rms, x_rows, gain_one)
    d_x_norm, grad_gain_attn = norm_one_back(d_n1)
    input_grad = (d_x1 + d_x_norm).reshape(plots, rows, width)
    grads = (
        grad_gain_attn,
        grad_gain_mlp,
        grad_query,
        grad_key,
        grad_value,
        grad_attn_out,
        grad_gate,
        grad_up,
        grad_down,
    )
    shards = (
        lax.psum_scatter(grads[0], ("wide", "narrow"), scatter_dimension=0, tiled=True),
        lax.psum_scatter(grads[1], ("wide", "narrow"), scatter_dimension=0, tiled=True),
        lax.psum_scatter(grads[2], ("wide", "narrow"), scatter_dimension=0, tiled=True),
        lax.psum_scatter(grads[3], ("wide", "narrow"), scatter_dimension=0, tiled=True),
        lax.psum_scatter(grads[4], ("wide", "narrow"), scatter_dimension=0, tiled=True),
        lax.psum_scatter(grads[5], ("wide", "narrow"), scatter_dimension=0, tiled=True),
        lax.psum_scatter(grads[6], ("wide", "narrow"), scatter_dimension=0, tiled=True),
        lax.psum_scatter(grads[7], ("wide", "narrow"), scatter_dimension=0, tiled=True),
        lax.psum_scatter(grads[8], ("wide", "narrow"), scatter_dimension=0, tiled=True),
    )
    return (
        activations,
        input_grad,
        shards[0],
        shards[1],
        shards[2],
        shards[3],
        shards[4],
        shards[5],
        shards[6],
        shards[7],
        shards[8],
    )


F32 = jnp.float32
BF16 = jnp.bfloat16
PAIR = 2 * HEAD_DIM
MIB = 1 << 20
TILE = 256


def params(limit=60):
    return pltpu.CompilerParams(vmem_limit_bytes=limit * MIB)


def whole(shape):
    return pl.BlockSpec(shape, lambda *_: (0,) * len(shape), pipeline_mode=pl.Buffered(1))


SCALARS = pl.BlockSpec(memory_space=pltpu.SMEM)
APART = pl.BlockSpec(memory_space=pl.ANY)


def swap(value, mask, size):
    return lax.ppermute(value, "wide", [(i, i ^ mask) for i in range(size)])


def swap_x(value):
    return lax.ppermute(value, "narrow", [(0, 1), (1, 0)])


def by_side(side, first, second):
    return jnp.where(side == 0, first, second)


def after(value, *others):
    return lax.optimization_barrier((value, *others))[0]


def pair_up(piece, give, side):
    other = swap_x(give)
    return jnp.concatenate([by_side(side, piece, other), by_side(side, other, piece)], 0)


def spread_z(unit, size):
    return jnp.stack([unit] + [swap(unit, 4 * k, size) for k in range(1, size // 4)])


def spread_xy(stack, size):
    return swap_x(stack), swap(stack, 2, size)


PIECES = ((0, 0), (1, 0), (0, 1), (1, 1))
DOWN_PIECES = ((0, 0), (0, 1))


def listing(refs, places=PIECES):
    found = []
    for at, ref in enumerate(refs):
        x, y = places[at % len(places)]
        core = at // len(places)
        for k in range(ref.shape[0]):
            found.append((ref, k, x, 4 * k + 2 * y + core))
    return found


def chip_sum(keep, arrived, part, parts=4):
    groups = keep.shape[0] // parts
    at = slice(part * groups, (part + 1) * groups)
    return keep[at].astype(F32) + arrived[at].astype(F32)


def diagonal_of(keep, arrived):
    return chip_sum(keep, arrived, 3).astype(BF16)


def over_y_of(keep, arrived):
    return chip_sum(keep, arrived, 1).astype(BF16)


def over_x_of(keep, arrived, corner):
    return (chip_sum(keep, arrived, 2) + corner.astype(F32)).astype(BF16)


def collect_own(keep, arrived, sides, units):
    return [sum([part[k].astype(F32) for part in (arrived, *sides)], keep[k].astype(F32)) for k in units]


def settle_rows(total, side):
    half = total.shape[0] // 2
    other = swap_x(by_side(side, total[half:], total[:half]).astype(BF16)).astype(F32)
    return by_side(side, total[:half], total[half:]) + other


def settle(total, side):
    half = total.shape[0] // 2
    mine = by_side(side, total[:half], total[half:])
    other = swap_x(by_side(side, total[half:], total[:half]).astype(BF16)).astype(F32)
    return by_side(side, mine, other), by_side(side, other, mine)


def file_rows(keep, send, me, side, half, lanes, source):
    groups = keep.shape[0] // 4
    size = keep.shape[1]
    for rel in range(4 * groups):
        slot = ((half ^ side) * 2 + rel // 2 % 2) * groups + rel // 4
        start = pl.multiple_of((me ^ rel) * size, 8)
        block = source[pl.ds(start, size), :].astype(BF16)
        (send if rel % 2 else keep)[slot, :, lanes] = block


def pack_kernel(place_ref, gain_attn_ref, gain_mlp_ref, *refs):
    qkv_refs, mlp_refs = refs[:3], refs[3:6]
    unit_ref, own_ref, give_ref, wide_s = refs[6:]
    rows, width = qkv_refs[0].shape
    halves = []
    for h, gain_ref in enumerate((gain_attn_ref, gain_mlp_ref)):
        wide_s[...] = jnp.zeros_like(wide_s)
        wide_s[0:1, :rows] = gain_ref[...].astype(F32)
        columns = []
        for pair in range(h * width // PAIR // 2, (h + 1) * width // PAIR // 2):
            columns += [ref[:, pair * PAIR : (pair + 1) * PAIR] for ref in qkv_refs]
        gains = jnp.transpose(wide_s[...])[:rows]
        halves.append(jnp.concatenate([jnp.concatenate(columns, 1).astype(F32), gains], 1))
    unit_ref[...] = jnp.concatenate(halves, 0).astype(BF16)
    side = place_ref[1]
    done = 0
    for ref in mlp_refs:
        half = ref.shape[1] // 2
        lanes = slice(done, done + half)
        first, second = ref[:, :half], ref[:, half:]

        @pl.when(side == 0)
        def _():
            own_ref[:, lanes] = first
            give_ref[:, lanes] = second

        @pl.when(side == 1)
        def _():
            own_ref[:, lanes] = second
            give_ref[:, lanes] = first

        done += half


def pack(place, gains, qkv_weights, mlp_weights):
    rows, width = qkv_weights[0].shape
    cols = sum(w.shape[1] for w in mlp_weights) // 2
    whole_in = pl.BlockSpec(memory_space=pltpu.VMEM)
    return pl.pallas_call(
        pack_kernel,
        in_specs=[SCALARS] + [whole_in] * 8,
        out_specs=[whole_in] * 3,
        out_shape=[
            jax.ShapeDtypeStruct((2 * rows, 3 * width // 2 + 128), BF16),
            jax.ShapeDtypeStruct((rows, cols), BF16),
            jax.ShapeDtypeStruct((rows, cols), BF16),
        ],
        scratch_shapes=[pltpu.VMEM((128, 128), F32)],
        compiler_params=params(),
        cost_estimate=pl.CostEstimate(flops=0, bytes_accessed=MIB, transcendentals=0),
        name="pack",
    )(place, *[gain[None, :] for gain in gains], *qkv_weights, *mlp_weights)


TRIPLE = 3 * PAIR


def project_kernel(place_ref, own_ref, third_ref, fourth_ref, *refs):
    pieces, (qkv_ref, n1_ref, gain_ref, held, staged, sems) = refs[:8], refs[-6:]
    step = pl.program_id(0)
    width = own_ref.shape[1]
    cols = 3 * width // 2

    @pl.when(pl.program_id(0) == 0)
    def _():
        me, side = place_ref[0], place_ref[1]
        pairs, rows = staged.shape[1:3]
        copies = []
        for at, (ref, k, x, rel) in enumerate(listing(pieces)):
            copies.append(pltpu.make_async_copy(ref.at[k], staged.at[side ^ x, me ^ rel], sems.at[at]))
        for copy in copies:
            copy.start()
        for copy in copies:
            copy.wait()
        own = rows // 2
        for pair in range(pairs):
            units = [staged[x, pair].astype(F32) for x in range(2)]
            for h in range(2):
                both_rows = jnp.concatenate([unit[h * own : (h + 1) * own] for unit in units], 0)
                held[h, pair * rows : (pair + 1) * rows, :] = both_rows.astype(BF16)
        for h in range(2):
            gain_ref[h * 8 : h * 8 + 8, :] = jnp.transpose(held[h, :, cols:].astype(F32))[:8]

    short = own_ref.shape[0] - third_ref.shape[0]
    third = jnp.concatenate([third_ref[...], fourth_ref[:short, :]], 0)
    x = jnp.where(step < 2, own_ref[...], jnp.where(step == 2, third, fourth_ref[short:, :])).astype(F32)
    root = lax.rsqrt(jnp.mean(x * x, -1, keepdims=True) + EPS)
    n1 = (x * root * gain_ref[0:1, :]).astype(BF16)
    n1_ref[...] = n1
    is_query = lax.broadcasted_iota(jnp.int32, (1, cols), 1) % TRIPLE < PAIR
    scale = jnp.where(is_query, HEAD_DIM**-0.5, 1.0)
    for h in range(2):
        qkv_ref[:, h * cols : (h + 1) * cols] = (nn(n1, held[h, :, :cols]) * scale).astype(BF16)


def project(place, own, others, pieces, ready=()):
    rows, width = 2 * own.shape[0], own.shape[1]
    tile = rows // 4
    groups, unit_rows, unit_cols = pieces[0].shape
    held = (2, width, unit_cols)
    return pl.pallas_call(
        project_kernel,
        grid=(4,),
        in_specs=[SCALARS, pl.BlockSpec((tile, width), lambda i: (jnp.minimum(i, 1), 0))]
        + [whole(part.shape) for part in others]
        + [APART] * (len(pieces) + len(ready)),
        out_specs=[
            pl.BlockSpec((tile, 3 * width), lambda i: (i, 0)),
            pl.BlockSpec((tile, width), lambda i: (i, 0)),
            whole((16, width)),
            whole(held),
        ],
        out_shape=[
            jax.ShapeDtypeStruct((rows, 3 * width), BF16),
            jax.ShapeDtypeStruct((rows, width), BF16),
            jax.ShapeDtypeStruct((16, width), F32),
            jax.ShapeDtypeStruct(held, BF16),
        ],
        scratch_shapes=[
            pltpu.VMEM((2, 4 * groups, unit_rows, unit_cols), BF16),
            pltpu.SemaphoreType.DMA((len(pieces) * groups,)),
        ],
        compiler_params=params(),
        cost_estimate=pl.CostEstimate(
            flops=18 * rows * width * width, bytes_accessed=16 * rows * width, transcendentals=0
        ),
        name="project",
    )(place, own, *others, *pieces, *ready)


def nt(left, right):
    return lax.dot_general(left, right, (((1,), (1,)), ((), ())), preferred_element_type=F32)


def tn(left, right):
    return lax.dot_general(left, right, (((0,), (0,)), ((), ())), preferred_element_type=F32)


def nn(left, right):
    return jnp.dot(left, right, preferred_element_type=F32)


STRIP = 128


def head_mask(head):
    lanes = lax.broadcasted_iota(jnp.int32, (1, PAIR), 1)
    return (lanes // HEAD_DIM) == head


SAFE = 60.0
QUERIES = 512


def attend_kernel(qkv_ref, *refs):
    o_ref, lse_ref, lse_s = refs[-3:]
    q_ref, keys, value = qkv_ref.at[:, pl.ds(0, PAIR)], qkv_ref[:, PAIR : 2 * PAIR], qkv_ref[:, 2 * PAIR :]
    masks = [head_mask(h) for h in range(2)]
    values = [jnp.where(mask, value, jnp.ones_like(value)) for mask in masks]
    size = min(QUERIES, q_ref.shape[0])

    def blocks(shifted):
        for start in range(0, q_ref.shape[0], size):
            rows = slice(start, start + size)
            queries = q_ref[rows, :]
            mixed, peaks = [], []
            for h in range(2):
                own = jnp.where(masks[h], queries, jnp.zeros_like(queries))
                scores = nt(own, keys)
                expo = []
                peaks.append(jnp.max(scores, -1, keepdims=True) if shifted else 0.0)
                for s in range(0, size, 64):
                    strip = scores[s : s + 64]
                    expo.append(jnp.exp(strip - peaks[h][s : s + 64] if shifted else strip).astype(BF16))
                mixed.append(nn(jnp.concatenate(expo, 0), values[h]))
            summed = pltpu.roll(jnp.where(masks[0], mixed[1], mixed[0]), HEAD_DIM, 1)
            o_ref[rows, :] = (jnp.where(masks[0], mixed[0], mixed[1]) * (1.0 / summed)).astype(BF16)
            peak = jnp.where(masks[0], peaks[0], peaks[1]) if shifted else 0.0
            lse_s[rows, :] = peak + jnp.log(summed)

    longest = []
    for part in (q_ref[...], keys):
        wide = part.astype(F32)
        longest.append(jnp.max(jnp.sum(wide * wide, -1, keepdims=True)))
    safe = longest[0] * longest[1] < SAFE * SAFE
    pl.when(safe)(lambda: blocks(False))
    pl.when(jnp.logical_not(safe))(lambda: blocks(True))
    turned = jnp.transpose(lse_s[...])
    for h in range(2):
        lse_ref[0, h : h + 1, :] = turned[h * HEAD_DIM : h * HEAD_DIM + 1]


def attend_fast(qkv, first, count, ready=()):
    rows = qkv.shape[0]
    return pl.pallas_call(
        attend_kernel,
        grid=(count,),
        in_specs=[pl.BlockSpec((rows, TRIPLE), lambda i: (0, first + i))] + [APART] * len(ready),
        out_specs=[
            pl.BlockSpec((rows, PAIR), lambda i: (0, i)),
            pl.BlockSpec((1, 8, rows), lambda i: (i, 0, 0)),
        ],
        out_shape=[
            jax.ShapeDtypeStruct((rows, count * PAIR), BF16),
            jax.ShapeDtypeStruct((count, 8, rows), F32),
        ],
        scratch_shapes=[pltpu.VMEM((rows, PAIR), F32)],
        compiler_params=params(),
        cost_estimate=pl.CostEstimate(
            flops=32 * rows * rows * count * PAIR, bytes_accessed=8 * rows * count * PAIR, transcendentals=0
        ),
        name="attend",
    )(qkv, *ready)


HIDDEN = 512


def mlp_kernel(place_ref, source_ref, weight_ref, x_ref, own_g_ref, third_g_ref, fourth_g_ref, gain_ref, *refs):
    (act_ref, other_ref, dx1_ref, do_ref, keep_ref, send_ref, keep_down_ref, send_down_ref, dgain_ref,
     held, down, g_ref, x1_s, n2_s, n2t_s, dy_s, acts, dn2, hid_s, dg_s, du_s, part_s, sems, sems_later) = refs[-24:]
    pieces, down_pieces, o_refs = refs[:8], refs[8:12], refs[12:-24]
    me, side = place_ref[0], place_ref[1]
    scale = weight_ref[source_ref[side]]
    step = pl.program_id(0)
    rows, width = x_ref.shape
    hidden_size = down.shape[0]
    blocks = rows // TILE
    half = width // 2
    units = hidden_size // 2
    gain = gain_ref[8:9, :]
    pair_rows = keep_ref.shape[1]
    per_pair = keep_down_ref.shape[1]

    @pl.when(step == 0)
    def _():
        first, later = [], []
        for ref, k, x, rel in listing(pieces):
            pair = me ^ rel
            at_half = side ^ x
            source = ref.at[k]
            at = pl.ds(pl.multiple_of(pair * pair_rows, 16), pair_rows)
            for copies, sem, lanes in ((first, sems, pl.ds(0, half)), (later, sems_later, pl.ds(half, 2 * units))):
                copies.append(
                    pltpu.make_async_copy(source.at[:, lanes], held.at[at_half, at, lanes], sem.at[len(copies)])
                )
        for ref, k, _, rel in listing(down_pieces, DOWN_PIECES):
            at = pl.ds(pl.multiple_of((me ^ rel) * per_pair, 16), per_pair)
            later.append(pltpu.make_async_copy(ref.at[k], down.at[at, :], sems_later.at[len(later)]))
        for copy in first + later:
            copy.start()
        done = 0
        for ref in (own_g_ref, third_g_ref, fourth_g_ref):
            g_ref[done : done + ref.shape[0], :] = ref[...]
            done += ref.shape[0]
        for copy in first:
            copy.wait()

        @pl.loop(0, blocks)
        def _(i):
            at = pl.ds(pl.multiple_of(i * TILE, TILE), TILE)
            heads = jnp.concatenate([ref[at, :] for ref in o_refs], 1)
            mixed = jnp.concatenate([nn(heads, held[h, :, :half]) for h in range(2)], 1)
            x1 = x_ref[at, :].astype(F32) + mixed
            x1_s[at, :] = x1
            acts[at, :] = x1
            root = lax.rsqrt(jnp.mean(x1 * x1, -1, keepdims=True) + EPS)
            n2_s[at, :] = (x1 * root * gain).astype(BF16)
            dy_s[at, :] = (g_ref[at, :].astype(F32) * scale).astype(BF16)
            dn2[at, :] = jnp.zeros((TILE, width), F32)

        for i in range(blocks):
            n2t_s[:, i * TILE : (i + 1) * TILE] = jnp.transpose(n2_s[i * TILE : (i + 1) * TILE, :])
        for copy in later:
            copy.wait()

    in_half = units // HIDDEN
    at_half = step // in_half
    lane = (step % in_half) * HIDDEN
    gate_at = pl.ds(pl.multiple_of(half + lane, 128), HIDDEN)
    up_at = pl.ds(pl.multiple_of(half + units + lane, 128), HIDDEN)
    w_gate = held[at_half, :, gate_at]
    w_up = held[at_half, :, up_at]
    hidden_rows = pl.ds(pl.multiple_of(step * HIDDEN, HIDDEN), HIDDEN)
    w_down = down[hidden_rows, :]
    c_one = math.sqrt(2 / math.pi)
    c_two = 0.044715 * c_one
    half_rows = rows // 2
    for base in range(0, rows, half_rows):
        at = slice(base, base + half_rows)
        gate_all = nn(n2_s[at, :], w_gate)
        up_all = nn(n2_s[at, :], w_up)
        dh_all = nt(dy_s[at, :], w_down)
        for s in range(0, half_rows, STRIP // 2):
            strip = slice(s, s + STRIP // 2)
            out = slice(base + s, base + s + STRIP // 2)
            gate, up, dh = gate_all[strip], up_all[strip], dh_all[strip]
            squared = gate * gate
            bend = jnp.tanh(gate * (c_one + c_two * squared))
            rise = 0.5 + 0.5 * bend
            gelu = gate * rise
            slope = rise + gate * (0.5 * (1.0 - bend * bend)) * (c_one + 3.0 * c_two * squared)
            hid_s[out, :] = (gelu * up).astype(BF16)
            dg_s[out, :] = (dh * up * slope).astype(BF16)
            du_s[out, :] = (dh * gelu).astype(BF16)
        acts[at, :] += nn(hid_s[at, :], w_down)
        dn2[at, :] += nt(dg_s[at, :], w_gate) + nt(du_s[at, :], w_up)

    for values, lanes in ((dg_s, gate_at), (du_s, up_at)):
        part_s[:, :HIDDEN] = nn(n2t_s[...], values[...])
        file_rows(keep_ref, send_ref, me, side, at_half, lanes, part_s.at[:, pl.ds(0, HIDDEN)])

    groups = keep_ref.shape[0] // 4
    step_total = tn(hid_s[...], dy_s[...]).astype(BF16)
    for nth in range(HIDDEN // per_pair):
        rel = (step * (HIDDEN // per_pair) + nth) ^ me
        slot = rel // 2 % 2 * groups + rel // 4
        block = step_total[nth * per_pair : (nth + 1) * per_pair]

        @pl.when(rel % 2 == 0)
        def _():
            keep_down_ref[slot] = block

        @pl.when(rel % 2 == 1)
        def _():
            send_down_ref[slot] = block

    @pl.when(step == pl.num_programs(0) - 1)
    def _():
        dgain_ref[...] = jnp.zeros_like(dgain_ref)

        act_ref[...] = acts[: rows // 2, :].astype(BF16)
        other_ref[...] = acts[rows // 2 :, :].astype(BF16)

        @pl.loop(0, blocks)
        def _(i):
            at = pl.ds(pl.multiple_of(i * TILE, TILE), TILE)
            x1 = x1_s[at, :]
            root = lax.rsqrt(jnp.mean(x1 * x1, -1, keepdims=True) + EPS)
            back = dn2[at, :]
            unit_x1 = x1 * root
            dgain_ref[0:1, :] += jnp.sum(back * unit_x1, 0, keepdims=True)
            lifted = back * gain
            inner = jnp.mean(lifted * unit_x1, -1, keepdims=True)
            d_x1 = g_ref[at, :].astype(F32) * scale + root * (lifted - unit_x1 * inner)
            dx1_ref[at, :] = d_x1
            low = d_x1.astype(BF16)
            n2_s[at, :] = low
            do = nt(low[:, :half], held[0, :, :half]) + nt(low[:, half:], held[1, :, :half])
            do_ref[at, :] = do.astype(BF16)

        done = 0
        for ref in o_refs:
            count = ref.shape[1]
            part_s[done : done + count, :] = tn(ref[...], n2_s[...])
            done += count
        for h in range(2):
            file_rows(keep_ref, send_ref, me, side, h, slice(0, half), part_s.at[:, pl.ds(h * half, half)])


def mlp(place, source, weight, heads, x, grads, gains, pieces, down_pieces):
    rows, width = x.shape
    groups, pair_rows, cols = pieces[0].shape
    per_pair = down_pieces[0].shape[1]
    hidden = 4 * groups * per_pair
    kept = (4 * groups, pair_rows, cols)
    kept_down = (2 * groups, per_pair, width)
    units = sum(piece.shape[0] for piece in pieces)
    return pl.pallas_call(
        mlp_kernel,
        grid=(hidden // HIDDEN,),
        in_specs=[SCALARS] * 3
        + [whole((rows, width))]
        + [whole(part.shape) for part in grads]
        + [whole(gains.shape)]
        + [APART] * (len(pieces) + len(down_pieces))
        + [whole(part.shape) for part in heads],
        out_specs=[whole((rows // 2, width))] * 2
        + [whole((rows, width))] * 2
        + [whole(kept)] * 2
        + [whole(kept_down)] * 2
        + [whole((8, width))],
        out_shape=[
            jax.ShapeDtypeStruct((rows // 2, width), BF16),
            jax.ShapeDtypeStruct((rows // 2, width), BF16),
            jax.ShapeDtypeStruct((rows, width), F32),
            jax.ShapeDtypeStruct((rows, width), BF16),
            jax.ShapeDtypeStruct(kept, BF16),
            jax.ShapeDtypeStruct(kept, BF16),
            jax.ShapeDtypeStruct(kept_down, BF16),
            jax.ShapeDtypeStruct(kept_down, BF16),
            jax.ShapeDtypeStruct((8, width), F32),
        ],
        scratch_shapes=[
            pltpu.VMEM((2, width, width // 2 + hidden), BF16),
            pltpu.VMEM((hidden, width), BF16),
            pltpu.VMEM((rows, width), BF16),
            pltpu.VMEM((rows, width), F32),
            pltpu.VMEM((rows, width), BF16),
            pltpu.VMEM((width, rows), BF16),
            pltpu.VMEM((rows, width), BF16),
            pltpu.VMEM((rows, width), F32),
            pltpu.VMEM((rows, width), F32),
            pltpu.VMEM((rows, HIDDEN), BF16),
            pltpu.VMEM((rows, HIDDEN), BF16),
            pltpu.VMEM((rows, HIDDEN), BF16),
            pltpu.VMEM((width, width), F32),
            pltpu.SemaphoreType.DMA((units,)),
            pltpu.SemaphoreType.DMA((units + 4 * groups,)),
        ],
        compiler_params=params(),
        cost_estimate=pl.CostEstimate(
            flops=4 * rows * width * (3 * width + 9 * hidden),
            bytes_accessed=40 * MIB,
            transcendentals=0,
        ),
        name="mlp",
    )(place, source, weight, x, *grads, gains, *pieces, *down_pieces, *heads)


def attend_back_kernel(qkv_ref, do_ref, o_ref, lse_ref, *refs):
    d_ref, token_ref, dk_s, dv_s = refs[-4:]
    q_ref, keys, values = qkv_ref.at[:, pl.ds(0, PAIR)], qkv_ref[:, PAIR : 2 * PAIR], qkv_ref[:, 2 * PAIR :]
    total = keys.shape[0]
    token_ref[...] = jnp.zeros_like(token_ref)
    scale = HEAD_DIM**-0.5
    k_own = jnp.concatenate([jnp.where(head_mask(h), keys, jnp.zeros_like(keys)) for h in range(2)], 0)
    prod = do_ref[...].astype(F32) * o_ref[...].astype(F32)
    high = prod.astype(BF16)
    low = (prod - high.astype(F32)).astype(BF16)
    chosen = (
        lax.broadcasted_iota(jnp.int32, (8, PAIR), 1) // HEAD_DIM
        == lax.broadcasted_iota(jnp.int32, (8, PAIR), 0)
    ).astype(BF16)
    delta = nt(chosen, high) + nt(chosen, low)
    for block in range(q_ref.shape[0] // TILE):
        rows = slice(block * TILE, (block + 1) * TILE)
        queries, d_out = q_ref[rows, :], do_ref[rows, :]
        q_own, d_own, probs, slopes = [], [], [], []
        for h in range(2):
            mask = head_mask(h)
            q_own.append(jnp.where(mask, queries, jnp.zeros_like(queries)))
            d_own.append(jnp.where(mask, d_out, jnp.zeros_like(d_out)))
            scores = nt(keys, q_own[h])
            d_probs = nt(values, d_own[h])
            lse = lse_ref[0, h : h + 1, rows]
            center = delta[h : h + 1, rows]
            p_strips, s_strips = [], []
            for s in range(total // STRIP):
                strip = slice(s * STRIP, (s + 1) * STRIP)
                p = jnp.exp(scores[strip] - lse)
                p_strips.append(p.astype(BF16))
                s_strips.append((p * (d_probs[strip] - center)).astype(BF16))
            probs.append(jnp.concatenate(p_strips, 0))
            slopes.append(jnp.concatenate(s_strips, 0))
        d_ref[rows, :PAIR] = (tn(jnp.concatenate(slopes, 0), k_own) * scale).astype(BF16)
        d_keys = nn(jnp.concatenate(slopes, 1), jnp.concatenate(q_own, 0))
        d_values = nn(jnp.concatenate(probs, 1), jnp.concatenate(d_own, 0))
        if block == 0:
            dk_s[...] = d_keys
            dv_s[...] = d_values
        else:
            dk_s[...] += d_keys
            dv_s[...] += d_values
    d_ref[:, PAIR : 2 * PAIR] = dk_s[...].astype(BF16)
    d_ref[:, 2 * PAIR :] = dv_s[...].astype(BF16)


def attend_back_fast(qkv, d_out, heads, lse, first, d_qkv, ready=()):
    rows = d_out.shape[0]
    count = lse.shape[0]
    into = [] if d_qkv is None else [d_qkv]
    return pl.pallas_call(
        attend_back_kernel,
        grid=(count,),
        in_specs=[
            pl.BlockSpec((rows, TRIPLE), lambda i: (0, first + i)),
            pl.BlockSpec((rows, PAIR), lambda i: (0, first + i)),
            pl.BlockSpec((rows, PAIR), lambda i: (0, i)),
            pl.BlockSpec((1, 8, rows), lambda i: (i, 0, 0)),
        ]
        + [APART] * (len(into) + len(ready)),
        out_specs=[pl.BlockSpec((rows, TRIPLE), lambda i: (0, first + i)), whole((8, 128))],
        out_shape=[jax.ShapeDtypeStruct(qkv.shape, BF16), jax.ShapeDtypeStruct((8, 128), F32)],
        input_output_aliases={4: 0} if into else {},
        scratch_shapes=[pltpu.VMEM((rows, PAIR), F32)] * 2,
        compiler_params=params(),
        cost_estimate=pl.CostEstimate(
            flops=50 * rows * rows * count * PAIR, bytes_accessed=16 * rows * count * PAIR, transcendentals=0
        ),
        name="attend_back",
    )(qkv, d_out, heads, lse, *into, *ready)


def file_devices(keep, send, me, side, lanes, sources):
    groups = keep.shape[0] // 4
    own = keep.shape[1] // 2
    for rel in range(4 * groups):
        for x in range(2):
            start = pl.multiple_of((me ^ rel) * 2 * own + (side ^ x) * own, 8)
            block = jnp.concatenate([source[pl.ds(start, own), :] for source in sources], 0)
            slot = (x * 2 + rel // 2 % 2) * groups + rel // 4
            (send if rel % 2 else keep)[slot, :, lanes] = block.astype(BF16)


def project_back_kernel(place_ref, first_ref, second_ref, n1_ref, w_ref, x_hbm, dx1_hbm, gain_ref, dgain_ref, *refs):
    (own_ref, other_ref, keep_ref, send_ref,
     first_s, second_s, turned_s, wide_s, back_s, x_ref, dx1_ref, sems) = refs[-12:]
    me, side = place_ref[0], place_ref[1]
    step = pl.program_id(0)
    rows, width = n1_ref.shape
    copies = [
        pltpu.make_async_copy(x_hbm, x_ref, sems.at[0]),
        pltpu.make_async_copy(dx1_hbm, dx1_ref, sems.at[1]),
    ]

    @pl.when(step == 0)
    def _():
        for copy in copies:
            copy.start()
        for i in range(rows // TILE):
            turned_s[:, i * TILE : (i + 1) * TILE] = jnp.transpose(n1_ref[i * TILE : (i + 1) * TILE, :])
        back_s[...] = jnp.zeros_like(back_s)

    back_s[...] += nt(first_ref[...], w_ref[0]) + nt(second_ref[...], w_ref[1])
    first_s[...] = nn(turned_s[...], first_ref[...])
    second_s[...] = nn(turned_s[...], second_ref[...])
    lanes = pl.ds(pl.multiple_of(step * TRIPLE, 128), TRIPLE)
    file_devices(keep_ref, send_ref, me, side, lanes, (first_s, second_s))

    @pl.when(step == pl.num_programs(0) - 1)
    def _():
        for copy in copies:
            copy.wait()
        total = jnp.zeros((1, width), F32)
        for i in range(rows // TILE):
            at = slice(i * TILE, (i + 1) * TILE)
            back = back_s[at, :]
            x = x_ref[at, :].astype(F32)
            root = lax.rsqrt(jnp.mean(x * x, -1, keepdims=True) + EPS)
            unit = x * root
            total += jnp.sum(back * unit, 0, keepdims=True)
            lifted = back * gain_ref[0:1, :]
            inner = jnp.mean(lifted * unit, -1, keepdims=True)
            d_x = dx1_ref[at, :] + root * (lifted - unit * inner)
            start = i * TILE - rows // 2
            if start < 0:
                own_ref[at, :] = d_x
            else:
                other_ref[start : start + TILE, :] = d_x.astype(BF16)
        for row, part in ((total, first_s), (dgain_ref[0:1, :], second_s)):
            wide_s[...] = jnp.zeros_like(wide_s)
            wide_s[0:1, :] = row
            part[:, :128] = jnp.transpose(wide_s[...])
        last = keep_ref.shape[2] - 128
        sources = [part.at[:, pl.ds(0, 128)] for part in (first_s, second_s)]
        file_devices(keep_ref, send_ref, me, side, slice(last, last + 128), sources)


def project_back(place, d_qkv, n1, weights, x, d_x1, gains, d_gain, kept, ready=()):
    rows, width = n1.shape
    steps = width // PAIR // 2
    return pl.pallas_call(
        project_back_kernel,
        grid=(steps,),
        in_specs=[
            SCALARS,
            pl.BlockSpec((rows, TRIPLE), lambda i: (0, i)),
            pl.BlockSpec((rows, TRIPLE), lambda i: (0, steps + i)),
            whole((rows, width)),
            pl.BlockSpec((2, width, TRIPLE), lambda i: (0, 0, i)),
            APART,
            APART,
            whole(gains.shape),
            whole((8, width)),
        ]
        + [APART] * len(ready),
        out_specs=[whole((rows // 2, width))] * 2 + [whole(kept)] * 2,
        out_shape=[
            jax.ShapeDtypeStruct((rows // 2, width), F32),
            jax.ShapeDtypeStruct((rows // 2, width), BF16),
            jax.ShapeDtypeStruct(kept, BF16),
            jax.ShapeDtypeStruct(kept, BF16),
        ],
        scratch_shapes=[
            pltpu.VMEM((width, TRIPLE), F32),
            pltpu.VMEM((width, TRIPLE), F32),
            pltpu.VMEM((width, rows), BF16),
            pltpu.VMEM((128, width), F32),
            pltpu.VMEM((rows, width), F32),
            pltpu.VMEM((rows, width), BF16),
            pltpu.VMEM((rows, width), F32),
            pltpu.SemaphoreType.DMA((2,)),
        ],
        compiler_params=params(),
        cost_estimate=pl.CostEstimate(
            flops=24 * rows * width * width, bytes_accessed=40 * rows * width, transcendentals=0
        ),
        name="project_back",
    )(place, d_qkv, d_qkv, n1, weights, x, d_x1, gains, d_gain, *ready)


def give_half(plots, side):
    own = lax.dynamic_index_in_dim(plots, side, 0, keepdims=False)
    return own, lax.dynamic_index_in_dim(plots, 1 - side, 0, keepdims=False)


def halves_back(own, arrived, side):
    arrived = arrived.astype(own.dtype)
    return jnp.stack([by_side(side, own, arrived), by_side(side, arrived, own)])


CALLS = (3, 2, 1)


def local_fast(size, *arguments):
    (inputs, out_grad, source_id, source_weight, gain_attn, gain_mlp,
     w_query, w_key, w_value, w_attn_out, w_gate, w_up, w_down) = arguments
    half_rows, width = inputs.shape[1:]
    half = width // 2
    hidden = w_gate.shape[1]
    groups = size // 4
    side = lax.axis_index("narrow")
    place = jnp.stack([lax.axis_index("wide"), side]).astype(jnp.int32)

    pairs = width // PAIR
    unit_a, unit_b, give = pack(
        place, (gain_attn, gain_mlp), (w_query, w_key, w_value), (w_attn_out, w_gate, w_up)
    )
    stack_a = spread_z(unit_a, size)
    unit_b = pair_up(unit_b, give, side)
    unit_c = pair_up(w_down, after(w_down, unit_a), side)
    quarter = half_rows // 2
    own_x, give_x = give_half(after(inputs, unit_a), side)
    short = quarter // 2
    others = [swap_x(give_x[:short])]
    stack_a, unit_b, unit_c, others[0] = lax.optimization_barrier((stack_a, unit_b, unit_c, others[0]))
    x_a, y_a = spread_xy(stack_a, size)
    units_b = [unit_b, None, swap(unit_b, 8, size)]
    near_c = swap(unit_c, 4, size)
    x_a, y_a, units_b[2], near_c = lax.optimization_barrier((x_a, y_a, units_b[2], near_c))
    d_a = swap(x_a, 2, size)
    others.append(swap_x(after(give_x[short:], x_a)))
    unit_b = after(unit_b, y_a)
    units_b[1] = swap(unit_b, 4, size)
    units_b += [swap(unit_b, 4 * k, size) for k in range(3, groups)]
    d_a, others[1], units_b[1], *units_b[3:] = lax.optimization_barrier((d_a, others[1], units_b[1], *units_b[3:]))
    pieces_a = [stack_a, x_a, y_a, d_a]
    own_grad, give_grad = give_half(after(out_grad, x_a), side)
    grads = [own_grad, swap_x(give_grad[:quarter]), swap_x(after(give_grad[quarter:], d_a))]
    pieces_a += [swap(piece, 1, size) for piece in pieces_a]

    stack_b = jnp.stack(units_b)
    unit_c = after(unit_c, *pieces_a[4:])
    units_c = [unit_c, near_c] + [swap(unit_c, 4 * k, size) for k in range(2, groups)]
    qkv, n1, gains, weights = project(place, own_x, others, pieces_a, [stack_b])
    x_b, y_b = spread_xy(stack_b, size)
    heads, lses = [], []
    for call, count in enumerate(CALLS):
        ready = [[grads[1]], [*heads, y_b, *units_c], [*heads, grads[2]]][call]
        made = attend_fast(qkv, sum(CALLS[:call]), count, ready)
        heads.append(made[0])
        lses.append(made[1])
        if call == 0:
            y_b, stack_b, *units_c = lax.optimization_barrier((y_b, stack_b, *units_c, heads[-1]))[:-1]
            d_b = swap_x(y_b)
            stack_c = jnp.stack(units_c)
            y_c = swap(stack_c, 2, size)
            twins_b = [swap(stack_b, 1, size), swap(y_b, 1, size)]
            twins_c = [swap(stack_c, 1, size)]
    x = jnp.concatenate(lax.optimization_barrier((own_x, *others, heads[-1]))[:3], 0)
    x_b, d_b, y_c, _ = lax.optimization_barrier((x_b, d_b, y_c, heads[-1]))
    pieces_b = [stack_b, x_b, y_b, d_b]
    pieces_b += [twins_b[0], swap(x_b, 1, size), twins_b[1], swap(d_b, 1, size)]
    pieces_c = [stack_c, y_c, *twins_c, swap(y_c, 1, size)]
    acts, other_acts, d_x1, d_out, keep, send, keep_c, send_c, d_gain = mlp(
        place, source_id, source_weight, heads, x, grads, gains, pieces_b, pieces_c
    )

    twin = swap(send, 1, size)
    twin_c = swap(send_c, 1, size)
    other_acts = swap_x(other_acts)
    d_qkv = None
    ready = []
    for call in reversed(range(len(CALLS))):
        start = sum(CALLS[:call])
        d_qkv, token = attend_back_fast(qkv, d_out, heads[call], lses[call], start, d_qkv, ready)
        if call == 2:
            twin, twin_c = lax.optimization_barrier((twin, twin_c, token))[:2]
            diagonal, over_y = diagonal_of(keep, twin), over_y_of(keep, twin)
            corner = swap(diagonal, 2, size)
            by_y = swap(after(over_y, diagonal), 2, size)
            ready = [diagonal, over_y, token]
        elif call == 1:
            over_y_c = chip_sum(keep_c, after(twin_c, token), 1, 2).astype(BF16)
            twin, other_acts, corner, over_y_c = lax.optimization_barrier((twin, other_acts, corner, over_y_c, token))[:4]
            over_x = over_x_of(keep, twin, corner)
            by_x = swap_x(over_x)
            ready = [over_x, token, other_acts, over_y_c]
    twin, by_x, by_y = lax.optimization_barrier((twin, by_x, by_y, token))[:3]
    sides = (by_x, by_y)
    far = [unit.astype(BF16) for unit in collect_own(keep, twin, sides, range(1, groups))]
    arrived_c = swap(over_y_c, 2, size)
    kept = (4 * groups, *unit_a.shape)
    arrived = [swap(far[k - 1], 4 * k, size) for k in range(1, groups)]
    own, other, keep_a, send_a = project_back(
        place, d_qkv, n1, weights, x, d_x1, gains, d_gain, kept, [*far, arrived_c]
    )
    other = swap_x(other)
    send_a, *arrived = lax.optimization_barrier((send_a, *arrived))
    twin_a = swap(send_a, 1, size)
    diagonal = diagonal_of(keep_a, twin_a)
    corner = swap(diagonal, 2, size)
    keep, twin, by_x, by_y, keep_c, twin_c, arrived_c = lax.optimization_barrier(
        (keep, twin, by_x, by_y, keep_c, twin_c, arrived_c, diagonal)
    )[:7]
    total_c = chip_sum(keep_c, twin_c, 0, 2) + arrived_c.astype(F32)
    far_c = [swap(total_c[k].astype(BF16), 4 * k, size) for k in range(1, groups)]
    total_b = sum([part.astype(F32) for part in arrived], collect_own(keep, twin, (by_x, by_y), [0])[0])
    first_b, second_b = settle(total_b, side)
    twin_a, corner, other, first_b = lax.optimization_barrier((twin_a, corner, other, first_b))
    sides = [swap_x(over_x_of(keep_a, twin_a, corner)), swap(over_y_of(keep_a, twin_a), 2, size)]
    twin_a, *rest = lax.optimization_barrier((twin_a, *sides, *far_c))
    sides, far_c = rest[:2], rest[2:]
    units = collect_own(keep_a, twin_a, sides, range(groups))
    arrived = [swap(units[k].astype(BF16), 4 * k, size) for k in range(1, groups)]
    far_c[-1] = after(far_c[-1], units[0])
    other, other_acts, _ = lax.optimization_barrier((other, other_acts, units[0]))
    activations = halves_back(acts, other_acts, side)
    input_grad = halves_back(own, other, side)
    grad_down = settle_rows(sum([part.astype(F32) for part in far_c], total_c[0]), side)
    arrived[0], grad_down = lax.optimization_barrier((arrived[0], grad_down))
    total_a = sum([part.astype(F32) for part in arrived], units[0])
    own_rows = unit_a.shape[0] // 2
    first_a, second_a = total_a[:own_rows], total_a[own_rows:]

    def in_order(part):
        return jnp.concatenate(
            [
                piece[:, pair * TRIPLE + part * PAIR : pair * TRIPLE + (part + 1) * PAIR]
                for piece in (first_a, second_a)
                for pair in range(pairs // 2)
            ],
            1,
        )

    def joined(first, second, start, count):
        return jnp.concatenate([first[:, start : start + count], second[:, start : start + count]], 1)

    units = hidden // 2
    return (
        activations,
        input_grad,
        first_a[:, 3 * half],
        second_a[:, 3 * half],
        in_order(0),
        in_order(1),
        in_order(2),
        joined(first_b, second_b, 0, half),
        joined(first_b, second_b, half, units),
        joined(first_b, second_b, half + units, units),
        grad_down,
    )


def solution(mesh):
    size = mesh.shape["wide"]
    fits = mesh.shape["narrow"] == 2 and size == 16
    body = functools.partial(local_fast, size) if fits else local
    placed = (
        P("wide", "narrow", None),
        P("wide", "narrow", None),
        P("wide"),
        P(),
        P(("wide", "narrow")),
        P(("wide", "narrow")),
        P(("wide", "narrow"), None),
        P(("wide", "narrow"), None),
        P(("wide", "narrow"), None),
        P(("wide", "narrow"), None),
        P(("wide", "narrow"), None),
        P(("wide", "narrow"), None),
        P(("wide", "narrow"), None),
    )
    return jax.shard_map(
        body,
        mesh=mesh,
        in_specs=placed,
        out_specs=(
            P("wide", "narrow", None),
            P("wide", "narrow", None),
            P(("wide", "narrow")),
            P(("wide", "narrow")),
            P(("wide", "narrow"), None),
            P(("wide", "narrow"), None),
            P(("wide", "narrow"), None),
            P(("wide", "narrow"), None),
            P(("wide", "narrow"), None),
            P(("wide", "narrow"), None),
            P(("wide", "narrow"), None),
        ),
        check_vma=False,
    )
```

```python
import functools
import math

import jax
import jax.numpy as jnp
from jax import lax
from jax.experimental import pallas as pl
from jax.experimental.pallas import tpu as pltpu
from jax.sharding import PartitionSpec as P

HEADS = 12
HEAD_DIM = 64


EPS = 1e-06
HIGH = lax.Precision.HIGHEST


def rms(value, gain):
    return value * lax.rsqrt(jnp.mean(value * value, -1, keepdims=True) + EPS) * gain


def matmul(left, right):
    return jnp.dot(left, right, preferred_element_type=jnp.float32)


def matmul_tn(left, right):
    return lax.dot_general(
        left, right, (((0,), (0,)), ((), ())), preferred_element_type=jnp.float32
    )


def matmul_nt(left, right):
    return lax.dot_general(
        left, right, (((1,), (1,)), ((), ())), preferred_element_type=jnp.float32
    )


def attend(items):
    query, keys, values = items
    rows = query.shape[0]
    total = keys.shape[0]
    scale = HEAD_DIM ** (-0.5)
    q_heads = query.reshape(rows, HEADS, HEAD_DIM)
    k_heads = keys.reshape(total, HEADS, HEAD_DIM)
    v_heads = values.reshape(total, HEADS, HEAD_DIM)
    scores = (
        jnp.einsum("rhd,shd->hrs", q_heads, k_heads, preferred_element_type=jnp.float32) * scale
    )
    peak = jnp.max(scores, -1, keepdims=True)
    expo = jnp.exp(scores - peak)
    summed = jnp.sum(expo, -1, keepdims=True)
    probs_full = expo / summed
    probs = probs_full.astype(jnp.bfloat16)
    heads_out = jnp.einsum("hrs,shd->rhd", probs, v_heads, preferred_element_type=jnp.float32)
    exact_out = jnp.einsum("hrs,shd->rhd", probs_full, v_heads.astype(jnp.float32), precision=HIGH)
    log_total = (peak + jnp.log(summed))[:, :, 0]
    return (heads_out.reshape(rows, HEADS * HEAD_DIM), log_total, exact_out)


def attend_back(items):
    query, keys, values, log_total, d_out = items
    rows = query.shape[0]
    total = keys.shape[0]
    width = HEADS * HEAD_DIM
    scale = HEAD_DIM ** (-0.5)
    q_heads = query.reshape(rows, HEADS, HEAD_DIM)
    k_heads = keys.reshape(total, HEADS, HEAD_DIM)
    v_heads = values.reshape(total, HEADS, HEAD_DIM)
    d_heads = d_out.reshape(rows, HEADS, HEAD_DIM)
    scores = (
        jnp.einsum("rhd,shd->hrs", q_heads, k_heads, preferred_element_type=jnp.float32) * scale
    )
    probs = jnp.exp(scores - log_total[:, :, None])
    probs_low = probs.astype(jnp.bfloat16)
    d_probs = jnp.einsum("rhd,shd->hrs", d_heads, v_heads, preferred_element_type=jnp.float32)
    center = jnp.sum(d_probs * probs, -1, keepdims=True)
    d_scores = (probs * (d_probs - center)).astype(jnp.bfloat16)
    d_query = (
        jnp.einsum("hrs,shd->rhd", d_scores, k_heads, preferred_element_type=jnp.float32) * scale
    )
    d_keys = (
        jnp.einsum("hrs,rhd->shd", d_scores, q_heads, preferred_element_type=jnp.float32) * scale
    )
    d_values = jnp.einsum("hrs,rhd->shd", probs_low, d_heads, preferred_element_type=jnp.float32)
    return (
        d_query.reshape(rows, width),
        d_keys.reshape(total, width),
        d_values.reshape(total, width),
    )


def local(
    inputs,
    out_grad,
    source_id,
    source_weight,
    gain_attn,
    gain_mlp,
    w_query,
    w_key,
    w_value,
    w_attn_out,
    w_gate,
    w_up,
    w_down,
):
    plots, rows, width = inputs.shape
    gathered = (
        lax.all_gather(gain_attn, ("wide", "narrow"), axis=0, tiled=True),
        lax.all_gather(gain_mlp, ("wide", "narrow"), axis=0, tiled=True),
        lax.all_gather(w_query, ("wide", "narrow"), axis=0, tiled=True),
        lax.all_gather(w_key, ("wide", "narrow"), axis=0, tiled=True),
        lax.all_gather(w_value, ("wide", "narrow"), axis=0, tiled=True),
        lax.all_gather(w_attn_out, ("wide", "narrow"), axis=0, tiled=True),
        lax.all_gather(w_gate, ("wide", "narrow"), axis=0, tiled=True),
        lax.all_gather(w_up, ("wide", "narrow"), axis=0, tiled=True),
        lax.all_gather(w_down, ("wide", "narrow"), axis=0, tiled=True),
    )
    gain_one, gain_two, wq, wk, wv, wo, wg, wu, wd = gathered
    gain_one = gain_one.astype(jnp.float32)
    gain_two = gain_two.astype(jnp.float32)
    x_rows = inputs.astype(jnp.float32).reshape(plots * rows, width)
    n1 = rms(x_rows, gain_one).astype(jnp.bfloat16)
    query = matmul(n1, wq).astype(jnp.bfloat16)
    keys_own = matmul(n1, wk).astype(jnp.bfloat16).reshape(plots, rows, width)
    values_own = matmul(n1, wv).astype(jnp.bfloat16).reshape(plots, rows, width)
    keys_all, values_all = (
        lax.all_gather(keys_own, "narrow", axis=1, tiled=True),
        lax.all_gather(values_own, "narrow", axis=1, tiled=True),
    )
    query_plots = query.reshape(plots, rows, width)
    heads_out, log_total, exact_out = lax.map(attend, (query_plots, keys_all, values_all))
    attn = heads_out.reshape(plots * rows, width).astype(jnp.bfloat16)
    x1 = x_rows + matmul(attn, wo)
    n2 = rms(x1, gain_two).astype(jnp.bfloat16)
    gate = matmul(n2, wg)
    up = matmul(n2, wu)
    gate_act, gelu_back = jax.vjp(lambda u: jax.nn.gelu(u, approximate=True), gate)
    hidden = (gate_act * up).astype(jnp.bfloat16)
    activations = (x1 + matmul(hidden, wd)).astype(jnp.bfloat16).reshape(plots, rows, width)
    onehot = (
        source_id[:, None] == jnp.arange(source_weight.shape[0], dtype=jnp.int32)[None, :]
    ).astype(jnp.float32)
    plot_scale = jnp.sum(onehot * source_weight[None, :], -1)
    cotangent = (out_grad.astype(jnp.float32) * plot_scale[:, None, None]).reshape(
        plots * rows, width
    )
    again = (
        lax.all_gather(gain_attn, ("wide", "narrow"), axis=0, tiled=True),
        lax.all_gather(gain_mlp, ("wide", "narrow"), axis=0, tiled=True),
        lax.all_gather(w_query, ("wide", "narrow"), axis=0, tiled=True),
        lax.all_gather(w_key, ("wide", "narrow"), axis=0, tiled=True),
        lax.all_gather(w_value, ("wide", "narrow"), axis=0, tiled=True),
        lax.all_gather(w_attn_out, ("wide", "narrow"), axis=0, tiled=True),
        lax.all_gather(w_gate, ("wide", "narrow"), axis=0, tiled=True),
        lax.all_gather(w_up, ("wide", "narrow"), axis=0, tiled=True),
        lax.all_gather(w_down, ("wide", "narrow"), axis=0, tiled=True),
    )
    gain_one, gain_two, wq, wk, wv, wo, wg, wu, wd = again
    gain_one = gain_one.astype(jnp.float32)
    gain_two = gain_two.astype(jnp.float32)
    d_y = cotangent.astype(jnp.bfloat16)
    d_hidden = matmul_nt(d_y, wd)
    grad_down = matmul_tn(hidden, d_y)
    d_gate = gelu_back(d_hidden * up)[0].astype(jnp.bfloat16)
    d_up = (d_hidden * gate_act).astype(jnp.bfloat16)
    grad_gate = matmul_tn(n2, d_gate)
    grad_up = matmul_tn(n2, d_up)
    d_n2 = matmul_nt(d_gate, wg) + matmul_nt(d_up, wu)
    _, norm_two_back = jax.vjp(rms, x1, gain_two)
    d_x1_norm, grad_gain_mlp = norm_two_back(d_n2)
    d_x1 = cotangent + d_x1_norm
    d_attn = d_x1.astype(jnp.bfloat16)
    grad_attn_out = matmul_tn(attn, d_attn)
    d_out = matmul_nt(d_attn, wo).astype(jnp.bfloat16).reshape(plots, rows, width)
    keys_all, values_all = (
        lax.all_gather(keys_own, "narrow", axis=1, tiled=True),
        lax.all_gather(values_own, "narrow", axis=1, tiled=True),
    )
    d_query, d_keys_part, d_values_part = lax.map(
        attend_back, (query_plots, keys_all, values_all, log_total, d_out)
    )
    d_keys, d_values = (
        lax.psum_scatter(
            d_keys_part.astype(jnp.bfloat16), "narrow", scatter_dimension=1, tiled=True
        ).astype(jnp.float32),
        lax.psum_scatter(
            d_values_part.astype(jnp.bfloat16), "narrow", scatter_dimension=1, tiled=True
        ).astype(jnp.float32),
    )
    dq_low = d_query.reshape(plots * rows, width).astype(jnp.bfloat16)
    dk_low = d_keys.reshape(plots * rows, width).astype(jnp.bfloat16)
    dv_low = d_values.reshape(plots * rows, width).astype(jnp.bfloat16)
    grad_query = matmul_tn(n1, dq_low)
    grad_key = matmul_tn(n1, dk_low)
    grad_value = matmul_tn(n1, dv_low)
    d_n1 = matmul_nt(dq_low, wq) + matmul_nt(dk_low, wk) + matmul_nt(dv_low, wv)
    _, norm_one_back = jax.vjp(rms, x_rows, gain_one)
    d_x_norm, grad_gain_attn = norm_one_back(d_n1)
    input_grad = (d_x1 + d_x_norm).reshape(plots, rows, width)
    grads = (
        grad_gain_attn,
        grad_gain_mlp,
        grad_query,
        grad_key,
        grad_value,
        grad_attn_out,
        grad_gate,
        grad_up,
        grad_down,
    )
    shards = (
        lax.psum_scatter(grads[0], ("wide", "narrow"), scatter_dimension=0, tiled=True),
        lax.psum_scatter(grads[1], ("wide", "narrow"), scatter_dimension=0, tiled=True),
        lax.psum_scatter(grads[2], ("wide", "narrow"), scatter_dimension=0, tiled=True),
        lax.psum_scatter(grads[3], ("wide", "narrow"), scatter_dimension=0, tiled=True),
        lax.psum_scatter(grads[4], ("wide", "narrow"), scatter_dimension=0, tiled=True),
        lax.psum_scatter(grads[5], ("wide", "narrow"), scatter_dimension=0, tiled=True),
        lax.psum_scatter(grads[6], ("wide", "narrow"), scatter_dimension=0, tiled=True),
        lax.psum_scatter(grads[7], ("wide", "narrow"), scatter_dimension=0, tiled=True),
        lax.psum_scatter(grads[8], ("wide", "narrow"), scatter_dimension=0, tiled=True),
    )
    return (
        activations,
        input_grad,
        shards[0],
        shards[1],
        shards[2],
        shards[3],
        shards[4],
        shards[5],
        shards[6],
        shards[7],
        shards[8],
    )


F32 = jnp.float32
BF16 = jnp.bfloat16
PAIR = 2 * HEAD_DIM
MIB = 1 << 20
TILE = 256


def params(limit=60):
    return pltpu.CompilerParams(vmem_limit_bytes=limit * MIB)


def whole(shape):
    return pl.BlockSpec(shape, lambda *_: (0,) * len(shape), pipeline_mode=pl.Buffered(1))


SCALARS = pl.BlockSpec(memory_space=pltpu.SMEM)
APART = pl.BlockSpec(memory_space=pl.ANY)


def swap(value, mask, size):
    return lax.ppermute(value, "wide", [(i, i ^ mask) for i in range(size)])


def swap_x(value):
    return lax.ppermute(value, "narrow", [(0, 1), (1, 0)])


def by_side(side, first, second):
    return jnp.where(side == 0, first, second)


def after(value, *others):
    return lax.optimization_barrier((value, *others))[0]


def pair_up(piece, give, side):
    other = swap_x(give)
    return jnp.concatenate([by_side(side, piece, other), by_side(side, other, piece)], 0)


def spread_z(unit, size):
    return jnp.stack([unit] + [swap(unit, 4 * k, size) for k in range(1, size // 4)])


def spread_xy(stack, size):
    return swap_x(stack), swap(stack, 2, size)


PIECES = ((0, 0), (1, 0), (0, 1), (1, 1))
DOWN_PIECES = ((0, 0), (0, 1))


def listing(refs, places=PIECES):
    found = []
    for at, ref in enumerate(refs):
        x, y = places[at % len(places)]
        core = at // len(places)
        for k in range(ref.shape[0]):
            found.append((ref, k, x, 4 * k + 2 * y + core))
    return found


def chip_sum(keep, arrived, part, parts=4):
    groups = keep.shape[0] // parts
    at = slice(part * groups, (part + 1) * groups)
    return keep[at].astype(F32) + arrived[at].astype(F32)


def diagonal_of(keep, arrived):
    return chip_sum(keep, arrived, 3).astype(BF16)


def over_y_of(keep, arrived):
    return chip_sum(keep, arrived, 1).astype(BF16)


def over_x_of(keep, arrived, corner):
    return (chip_sum(keep, arrived, 2) + corner.astype(F32)).astype(BF16)


def collect_own(keep, arrived, sides, units):
    return [sum([part[k].astype(F32) for part in (arrived, *sides)], keep[k].astype(F32)) for k in units]


def settle_rows(total, side):
    half = total.shape[0] // 2
    other = swap_x(by_side(side, total[half:], total[:half]).astype(BF16)).astype(F32)
    return by_side(side, total[:half], total[half:]) + other


def settle(total, side):
    half = total.shape[0] // 2
    mine = by_side(side, total[:half], total[half:])
    other = swap_x(by_side(side, total[half:], total[:half]).astype(BF16)).astype(F32)
    return by_side(side, mine, other), by_side(side, other, mine)


def file_rows(keep, send, me, side, half, lanes, source):
    groups = keep.shape[0] // 4
    size = keep.shape[1]
    for rel in range(4 * groups):
        slot = ((half ^ side) * 2 + rel // 2 % 2) * groups + rel // 4
        start = pl.multiple_of((me ^ rel) * size, 8)
        block = source[pl.ds(start, size), :].astype(BF16)
        (send if rel % 2 else keep)[slot, :, lanes] = block


def pack_kernel(place_ref, gain_attn_ref, gain_mlp_ref, *refs):
    qkv_refs, mlp_refs = refs[:3], refs[3:6]
    unit_ref, own_ref, give_ref, wide_s = refs[6:]
    rows, width = qkv_refs[0].shape
    halves = []
    for h, gain_ref in enumerate((gain_attn_ref, gain_mlp_ref)):
        wide_s[...] = jnp.zeros_like(wide_s)
        wide_s[0:1, :rows] = gain_ref[...].astype(F32)
        columns = []
        for pair in range(h * width // PAIR // 2, (h + 1) * width // PAIR // 2):
            columns += [ref[:, pair * PAIR : (pair + 1) * PAIR] for ref in qkv_refs]
        gains = jnp.transpose(wide_s[...])[:rows]
        halves.append(jnp.concatenate([jnp.concatenate(columns, 1).astype(F32), gains], 1))
    unit_ref[...] = jnp.concatenate(halves, 0).astype(BF16)
    side = place_ref[1]
    done = 0
    for ref in mlp_refs:
        half = ref.shape[1] // 2
        lanes = slice(done, done + half)
        first, second = ref[:, :half], ref[:, half:]

        @pl.when(side == 0)
        def _():
            own_ref[:, lanes] = first
            give_ref[:, lanes] = second

        @pl.when(side == 1)
        def _():
            own_ref[:, lanes] = second
            give_ref[:, lanes] = first

        done += half


def pack(place, gains, qkv_weights, mlp_weights):
    rows, width = qkv_weights[0].shape
    cols = sum(w.shape[1] for w in mlp_weights) // 2
    whole_in = pl.BlockSpec(memory_space=pltpu.VMEM)
    return pl.pallas_call(
        pack_kernel,
        in_specs=[SCALARS] + [whole_in] * 8,
        out_specs=[whole_in] * 3,
        out_shape=[
            jax.ShapeDtypeStruct((2 * rows, 3 * width // 2 + 128), BF16),
            jax.ShapeDtypeStruct((rows, cols), BF16),
            jax.ShapeDtypeStruct((rows, cols), BF16),
        ],
        scratch_shapes=[pltpu.VMEM((128, 128), F32)],
        compiler_params=params(),
        cost_estimate=pl.CostEstimate(flops=0, bytes_accessed=MIB, transcendentals=0),
        name="pack",
    )(place, *[gain[None, :] for gain in gains], *qkv_weights, *mlp_weights)


TRIPLE = 3 * PAIR


def project_kernel(place_ref, own_ref, third_ref, fourth_ref, *refs):
    pieces, (qkv_ref, n1_ref, gain_ref, held, staged, sems) = refs[:8], refs[-6:]
    step = pl.program_id(0)
    width = own_ref.shape[1]
    cols = 3 * width // 2

    @pl.when(pl.program_id(0) == 0)
    def _():
        me, side = place_ref[0], place_ref[1]
        pairs, rows = staged.shape[1:3]
        copies = []
        for at, (ref, k, x, rel) in enumerate(listing(pieces)):
            copies.append(pltpu.make_async_copy(ref.at[k], staged.at[side ^ x, me ^ rel], sems.at[at]))
        for copy in copies:
            copy.start()
        for copy in copies:
            copy.wait()
        own = rows // 2
        for pair in range(pairs):
            units = [staged[x, pair].astype(F32) for x in range(2)]
            for h in range(2):
                both_rows = jnp.concatenate([unit[h * own : (h + 1) * own] for unit in units], 0)
                held[h, pair * rows : (pair + 1) * rows, :] = both_rows.astype(BF16)
        for h in range(2):
            gain_ref[h * 8 : h * 8 + 8, :] = jnp.transpose(held[h, :, cols:].astype(F32))[:8]

    short = own_ref.shape[0] - third_ref.shape[0]
    third = jnp.concatenate([third_ref[...], fourth_ref[:short, :]], 0)
    x = jnp.where(step < 2, own_ref[...], jnp.where(step == 2, third, fourth_ref[short:, :])).astype(F32)
    root = lax.rsqrt(jnp.mean(x * x, -1, keepdims=True) + EPS)
    n1 = (x * root * gain_ref[0:1, :]).astype(BF16)
    n1_ref[...] = n1
    is_query = lax.broadcasted_iota(jnp.int32, (1, cols), 1) % TRIPLE < PAIR
    scale = jnp.where(is_query, HEAD_DIM**-0.5, 1.0)
    for h in range(2):
        qkv_ref[:, h * cols : (h + 1) * cols] = (nn(n1, held[h, :, :cols]) * scale).astype(BF16)


def project(place, own, others, pieces, ready=()):
    rows, width = 2 * own.shape[0], own.shape[1]
    tile = rows // 4
    groups, unit_rows, unit_cols = pieces[0].shape
    held = (2, width, unit_cols)
    return pl.pallas_call(
        project_kernel,
        grid=(4,),
        in_specs=[SCALARS, pl.BlockSpec((tile, width), lambda i: (jnp.minimum(i, 1), 0))]
        + [whole(part.shape) for part in others]
        + [APART] * (len(pieces) + len(ready)),
        out_specs=[
            pl.BlockSpec((tile, 3 * width), lambda i: (i, 0)),
            pl.BlockSpec((tile, width), lambda i: (i, 0)),
            whole((16, width)),
            whole(held),
        ],
        out_shape=[
            jax.ShapeDtypeStruct((rows, 3 * width), BF16),
            jax.ShapeDtypeStruct((rows, width), BF16),
            jax.ShapeDtypeStruct((16, width), F32),
            jax.ShapeDtypeStruct(held, BF16),
        ],
        scratch_shapes=[
            pltpu.VMEM((2, 4 * groups, unit_rows, unit_cols), BF16),
            pltpu.SemaphoreType.DMA((len(pieces) * groups,)),
        ],
        compiler_params=params(),
        cost_estimate=pl.CostEstimate(
            flops=18 * rows * width * width, bytes_accessed=16 * rows * width, transcendentals=0
        ),
        name="project",
    )(place, own, *others, *pieces, *ready)


def nt(left, right):
    return lax.dot_general(left, right, (((1,), (1,)), ((), ())), preferred_element_type=F32)


def tn(left, right):
    return lax.dot_general(left, right, (((0,), (0,)), ((), ())), preferred_element_type=F32)


def nn(left, right):
    return jnp.dot(left, right, preferred_element_type=F32)


STRIP = 128


def head_mask(head):
    lanes = lax.broadcasted_iota(jnp.int32, (1, PAIR), 1)
    return (lanes // HEAD_DIM) == head


SAFE = 60.0
QUERIES = 512


def attend_kernel(qkv_ref, *refs):
    o_ref, lse_ref, lse_s = refs[-3:]
    q_ref, keys, value = qkv_ref.at[:, pl.ds(0, PAIR)], qkv_ref[:, PAIR : 2 * PAIR], qkv_ref[:, 2 * PAIR :]
    masks = [head_mask(h) for h in range(2)]
    values = [jnp.where(mask, value, jnp.ones_like(value)) for mask in masks]
    size = min(QUERIES, q_ref.shape[0])

    def blocks(shifted):
        for start in range(0, q_ref.shape[0], size):
            rows = slice(start, start + size)
            queries = q_ref[rows, :]
            mixed, peaks = [], []
            for h in range(2):
                own = jnp.where(masks[h], queries, jnp.zeros_like(queries))
                scores = nt(own, keys)
                expo = []
                peaks.append(jnp.max(scores, -1, keepdims=True) if shifted else 0.0)
                for s in range(0, size, 64):
                    strip = scores[s : s + 64]
                    expo.append(jnp.exp(strip - peaks[h][s : s + 64] if shifted else strip).astype(BF16))
                mixed.append(nn(jnp.concatenate(expo, 0), values[h]))
            summed = pltpu.roll(jnp.where(masks[0], mixed[1], mixed[0]), HEAD_DIM, 1)
            o_ref[rows, :] = (jnp.where(masks[0], mixed[0], mixed[1]) * (1.0 / summed)).astype(BF16)
            peak = jnp.where(masks[0], peaks[0], peaks[1]) if shifted else 0.0
            lse_s[rows, :] = peak + jnp.log(summed)

    longest = []
    for part in (q_ref[...], keys):
        wide = part.astype(F32)
        longest.append(jnp.max(jnp.sum(wide * wide, -1, keepdims=True)))
    safe = longest[0] * longest[1] < SAFE * SAFE
    pl.when(safe)(lambda: blocks(False))
    pl.when(jnp.logical_not(safe))(lambda: blocks(True))
    turned = jnp.transpose(lse_s[...])
    for h in range(2):
        lse_ref[0, h : h + 1, :] = turned[h * HEAD_DIM : h * HEAD_DIM + 1]


def attend_fast(qkv, first, count, ready=()):
    rows = qkv.shape[0]
    return pl.pallas_call(
        attend_kernel,
        grid=(count,),
        in_specs=[pl.BlockSpec((rows, TRIPLE), lambda i: (0, first + i))] + [APART] * len(ready),
        out_specs=[
            pl.BlockSpec((rows, PAIR), lambda i: (0, i)),
            pl.BlockSpec((1, 8, rows), lambda i: (i, 0, 0)),
        ],
        out_shape=[
            jax.ShapeDtypeStruct((rows, count * PAIR), BF16),
            jax.ShapeDtypeStruct((count, 8, rows), F32),
        ],
        scratch_shapes=[pltpu.VMEM((rows, PAIR), F32)],
        compiler_params=params(),
        cost_estimate=pl.CostEstimate(
            flops=32 * rows * rows * count * PAIR, bytes_accessed=8 * rows * count * PAIR, transcendentals=0
        ),
        name="attend",
    )(qkv, *ready)


HIDDEN = 512


def mlp_kernel(place_ref, source_ref, weight_ref, x_ref, own_g_ref, third_g_ref, fourth_g_ref, gain_ref, *refs):
    (act_ref, other_ref, dx1_ref, do_ref, keep_ref, send_ref, keep_down_ref, send_down_ref, dgain_ref,
     held, down, g_ref, x1_s, n2_s, n2t_s, dy_s, acts, dn2, hid_s, dg_s, du_s, part_s, sems, sems_later) = refs[-24:]
    pieces, down_pieces, o_refs = refs[:8], refs[8:12], refs[12:-24]
    me, side = place_ref[0], place_ref[1]
    scale = weight_ref[source_ref[side]]
    step = pl.program_id(0)
    rows, width = x_ref.shape
    hidden_size = down.shape[0]
    blocks = rows // TILE
    half = width // 2
    units = hidden_size // 2
    gain = gain_ref[8:9, :]
    pair_rows = keep_ref.shape[1]
    per_pair = keep_down_ref.shape[1]

    @pl.when(step == 0)
    def _():
        first, later = [], []
        for ref, k, x, rel in listing(pieces):
            pair = me ^ rel
            at_half = side ^ x
            source = ref.at[k]
            at = pl.ds(pl.multiple_of(pair * pair_rows, 16), pair_rows)
            for copies, sem, lanes in ((first, sems, pl.ds(0, half)), (later, sems_later, pl.ds(half, 2 * units))):
                copies.append(
                    pltpu.make_async_copy(source.at[:, lanes], held.at[at_half, at, lanes], sem.at[len(copies)])
                )
        for ref, k, _, rel in listing(down_pieces, DOWN_PIECES):
            at = pl.ds(pl.multiple_of((me ^ rel) * per_pair, 16), per_pair)
            later.append(pltpu.make_async_copy(ref.at[k], down.at[at, :], sems_later.at[len(later)]))
        for copy in first + later:
            copy.start()
        done = 0
        for ref in (own_g_ref, third_g_ref, fourth_g_ref):
            g_ref[done : done + ref.shape[0], :] = ref[...]
            done += ref.shape[0]
        for copy in first:
            copy.wait()

        @pl.loop(0, blocks)
        def _(i):
            at = pl.ds(pl.multiple_of(i * TILE, TILE), TILE)
            heads = jnp.concatenate([ref[at, :] for ref in o_refs], 1)
            mixed = jnp.concatenate([nn(heads, held[h, :, :half]) for h in range(2)], 1)
            x1 = x_ref[at, :].astype(F32) + mixed
            x1_s[at, :] = x1
            acts[at, :] = x1
            root = lax.rsqrt(jnp.mean(x1 * x1, -1, keepdims=True) + EPS)
            n2_s[at, :] = (x1 * root * gain).astype(BF16)
            dy_s[at, :] = (g_ref[at, :].astype(F32) * scale).astype(BF16)
            dn2[at, :] = jnp.zeros((TILE, width), F32)

        for i in range(blocks):
            n2t_s[:, i * TILE : (i + 1) * TILE] = jnp.transpose(n2_s[i * TILE : (i + 1) * TILE, :])
        for copy in later:
            copy.wait()

    in_half = units // HIDDEN
    at_half = step // in_half
    lane = (step % in_half) * HIDDEN
    gate_at = pl.ds(pl.multiple_of(half + lane, 128), HIDDEN)
    up_at = pl.ds(pl.multiple_of(half + units + lane, 128), HIDDEN)
    w_gate = held[at_half, :, gate_at]
    w_up = held[at_half, :, up_at]
    hidden_rows = pl.ds(pl.multiple_of(step * HIDDEN, HIDDEN), HIDDEN)
    w_down = down[hidden_rows, :]
    c_one = math.sqrt(2 / math.pi)
    c_two = 0.044715 * c_one
    half_rows = rows // 2
    for base in range(0, rows, half_rows):
        at = slice(base, base + half_rows)
        gate_all = nn(n2_s[at, :], w_gate)
        up_all = nn(n2_s[at, :], w_up)
        dh_all = nt(dy_s[at, :], w_down)
        for s in range(0, half_rows, STRIP // 2):
            strip = slice(s, s + STRIP // 2)
            out = slice(base + s, base + s + STRIP // 2)
            gate, up, dh = gate_all[strip], up_all[strip], dh_all[strip]
            squared = gate * gate
            bend = jnp.tanh(gate * (c_one + c_two * squared))
            rise = 0.5 + 0.5 * bend
            gelu = gate * rise
            slope = rise + gate * (0.5 * (1.0 - bend * bend)) * (c_one + 3.0 * c_two * squared)
            hid_s[out, :] = (gelu * up).astype(BF16)
            dg_s[out, :] = (dh * up * slope).astype(BF16)
            du_s[out, :] = (dh * gelu).astype(BF16)
        acts[at, :] += nn(hid_s[at, :], w_down)
        dn2[at, :] += nt(dg_s[at, :], w_gate) + nt(du_s[at, :], w_up)

    for values, lanes in ((dg_s, gate_at), (du_s, up_at)):
        part_s[:, :HIDDEN] = nn(n2t_s[...], values[...])
        file_rows(keep_ref, send_ref, me, side, at_half, lanes, part_s.at[:, pl.ds(0, HIDDEN)])

    groups = keep_ref.shape[0] // 4
    step_total = tn(hid_s[...], dy_s[...]).astype(BF16)
    for nth in range(HIDDEN // per_pair):
        rel = (step * (HIDDEN // per_pair) + nth) ^ me
        slot = rel // 2 % 2 * groups + rel // 4
        block = step_total[nth * per_pair : (nth + 1) * per_pair]

        @pl.when(rel % 2 == 0)
        def _():
            keep_down_ref[slot] = block

        @pl.when(rel % 2 == 1)
        def _():
            send_down_ref[slot] = block

    @pl.when(step == pl.num_programs(0) - 1)
    def _():
        dgain_ref[...] = jnp.zeros_like(dgain_ref)

        act_ref[...] = acts[: rows // 2, :].astype(BF16)
        other_ref[...] = acts[rows // 2 :, :].astype(BF16)

        @pl.loop(0, blocks)
        def _(i):
            at = pl.ds(pl.multiple_of(i * TILE, TILE), TILE)
            x1 = x1_s[at, :]
            root = lax.rsqrt(jnp.mean(x1 * x1, -1, keepdims=True) + EPS)
            back = dn2[at, :]
            unit_x1 = x1 * root
            dgain_ref[0:1, :] += jnp.sum(back * unit_x1, 0, keepdims=True)
            lifted = back * gain
            inner = jnp.mean(lifted * unit_x1, -1, keepdims=True)
            d_x1 = g_ref[at, :].astype(F32) * scale + root * (lifted - unit_x1 * inner)
            dx1_ref[at, :] = d_x1
            low = d_x1.astype(BF16)
            n2_s[at, :] = low
            do = nt(low[:, :half], held[0, :, :half]) + nt(low[:, half:], held[1, :, :half])
            do_ref[at, :] = do.astype(BF16)

        done = 0
        for ref in o_refs:
            count = ref.shape[1]
            part_s[done : done + count, :] = tn(ref[...], n2_s[...])
            done += count
        for h in range(2):
            file_rows(keep_ref, send_ref, me, side, h, slice(0, half), part_s.at[:, pl.ds(h * half, half)])


def mlp(place, source, weight, heads, x, grads, gains, pieces, down_pieces):
    rows, width = x.shape
    groups, pair_rows, cols = pieces[0].shape
    per_pair = down_pieces[0].shape[1]
    hidden = 4 * groups * per_pair
    kept = (4 * groups, pair_rows, cols)
    kept_down = (2 * groups, per_pair, width)
    units = sum(piece.shape[0] for piece in pieces)
    return pl.pallas_call(
        mlp_kernel,
        grid=(hidden // HIDDEN,),
        in_specs=[SCALARS] * 3
        + [whole((rows, width))]
        + [whole(part.shape) for part in grads]
        + [whole(gains.shape)]
        + [APART] * (len(pieces) + len(down_pieces))
        + [whole(part.shape) for part in heads],
        out_specs=[whole((rows // 2, width))] * 2
        + [whole((rows, width))] * 2
        + [whole(kept)] * 2
        + [whole(kept_down)] * 2
        + [whole((8, width))],
        out_shape=[
            jax.ShapeDtypeStruct((rows // 2, width), BF16),
            jax.ShapeDtypeStruct((rows // 2, width), BF16),
            jax.ShapeDtypeStruct((rows, width), F32),
            jax.ShapeDtypeStruct((rows, width), BF16),
            jax.ShapeDtypeStruct(kept, BF16),
            jax.ShapeDtypeStruct(kept, BF16),
            jax.ShapeDtypeStruct(kept_down, BF16),
            jax.ShapeDtypeStruct(kept_down, BF16),
            jax.ShapeDtypeStruct((8, width), F32),
        ],
        scratch_shapes=[
            pltpu.VMEM((2, width, width // 2 + hidden), BF16),
            pltpu.VMEM((hidden, width), BF16),
            pltpu.VMEM((rows, width), BF16),
            pltpu.VMEM((rows, width), F32),
            pltpu.VMEM((rows, width), BF16),
            pltpu.VMEM((width, rows), BF16),
            pltpu.VMEM((rows, width), BF16),
            pltpu.VMEM((rows, width), F32),
            pltpu.VMEM((rows, width), F32),
            pltpu.VMEM((rows, HIDDEN), BF16),
            pltpu.VMEM((rows, HIDDEN), BF16),
            pltpu.VMEM((rows, HIDDEN), BF16),
            pltpu.VMEM((width, width), F32),
            pltpu.SemaphoreType.DMA((units,)),
            pltpu.SemaphoreType.DMA((units + 4 * groups,)),
        ],
        compiler_params=params(),
        cost_estimate=pl.CostEstimate(
            flops=4 * rows * width * (3 * width + 9 * hidden),
            bytes_accessed=40 * MIB,
            transcendentals=0,
        ),
        name="mlp",
    )(place, source, weight, x, *grads, gains, *pieces, *down_pieces, *heads)


def attend_back_kernel(qkv_ref, do_ref, o_ref, lse_ref, *refs):
    d_ref, token_ref, dk_s, dv_s = refs[-4:]
    q_ref, keys, values = qkv_ref.at[:, pl.ds(0, PAIR)], qkv_ref[:, PAIR : 2 * PAIR], qkv_ref[:, 2 * PAIR :]
    total = keys.shape[0]
    token_ref[...] = jnp.zeros_like(token_ref)
    scale = HEAD_DIM**-0.5
    k_own = jnp.concatenate([jnp.where(head_mask(h), keys, jnp.zeros_like(keys)) for h in range(2)], 0)
    prod = do_ref[...].astype(F32) * o_ref[...].astype(F32)
    high = prod.astype(BF16)
    low = (prod - high.astype(F32)).astype(BF16)
    chosen = (
        lax.broadcasted_iota(jnp.int32, (8, PAIR), 1) // HEAD_DIM
        == lax.broadcasted_iota(jnp.int32, (8, PAIR), 0)
    ).astype(BF16)
    delta = nt(chosen, high) + nt(chosen, low)
    for block in range(q_ref.shape[0] // TILE):
        rows = slice(block * TILE, (block + 1) * TILE)
        queries, d_out = q_ref[rows, :], do_ref[rows, :]
        q_own, d_own, probs, slopes = [], [], [], []
        for h in range(2):
            mask = head_mask(h)
            q_own.append(jnp.where(mask, queries, jnp.zeros_like(queries)))
            d_own.append(jnp.where(mask, d_out, jnp.zeros_like(d_out)))
            scores = nt(keys, q_own[h])
            d_probs = nt(values, d_own[h])
            lse = lse_ref[0, h : h + 1, rows]
            center = delta[h : h + 1, rows]
            p_strips, s_strips = [], []
            for s in range(total // STRIP):
                strip = slice(s * STRIP, (s + 1) * STRIP)
                p = jnp.exp(scores[strip] - lse)
                p_strips.append(p.astype(BF16))
                s_strips.append((p * (d_probs[strip] - center)).astype(BF16))
            probs.append(jnp.concatenate(p_strips, 0))
            slopes.append(jnp.concatenate(s_strips, 0))
        d_ref[rows, :PAIR] = (tn(jnp.concatenate(slopes, 0), k_own) * scale).astype(BF16)
        d_keys = nn(jnp.concatenate(slopes, 1), jnp.concatenate(q_own, 0))
        d_values = nn(jnp.concatenate(probs, 1), jnp.concatenate(d_own, 0))
        if block == 0:
            dk_s[...] = d_keys
            dv_s[...] = d_values
        else:
            dk_s[...] += d_keys
            dv_s[...] += d_values
    d_ref[:, PAIR : 2 * PAIR] = dk_s[...].astype(BF16)
    d_ref[:, 2 * PAIR :] = dv_s[...].astype(BF16)


def attend_back_fast(qkv, d_out, heads, lse, first, d_qkv, ready=()):
    rows = d_out.shape[0]
    count = lse.shape[0]
    into = [] if d_qkv is None else [d_qkv]
    return pl.pallas_call(
        attend_back_kernel,
        grid=(count,),
        in_specs=[
            pl.BlockSpec((rows, TRIPLE), lambda i: (0, first + i)),
            pl.BlockSpec((rows, PAIR), lambda i: (0, first + i)),
            pl.BlockSpec((rows, PAIR), lambda i: (0, i)),
            pl.BlockSpec((1, 8, rows), lambda i: (i, 0, 0)),
        ]
        + [APART] * (len(into) + len(ready)),
        out_specs=[pl.BlockSpec((rows, TRIPLE), lambda i: (0, first + i)), whole((8, 128))],
        out_shape=[jax.ShapeDtypeStruct(qkv.shape, BF16), jax.ShapeDtypeStruct((8, 128), F32)],
        input_output_aliases={4: 0} if into else {},
        scratch_shapes=[pltpu.VMEM((rows, PAIR), F32)] * 2,
        compiler_params=params(),
        cost_estimate=pl.CostEstimate(
            flops=50 * rows * rows * count * PAIR, bytes_accessed=16 * rows * count * PAIR, transcendentals=0
        ),
        name="attend_back",
    )(qkv, d_out, heads, lse, *into, *ready)


def file_devices(keep, send, me, side, lanes, sources):
    groups = keep.shape[0] // 4
    own = keep.shape[1] // 2
    for rel in range(4 * groups):
        for x in range(2):
            start = pl.multiple_of((me ^ rel) * 2 * own + (side ^ x) * own, 8)
            block = jnp.concatenate([source[pl.ds(start, own), :] for source in sources], 0)
            slot = (x * 2 + rel // 2 % 2) * groups + rel // 4
            (send if rel % 2 else keep)[slot, :, lanes] = block.astype(BF16)


def project_back_kernel(place_ref, first_ref, second_ref, n1_ref, w_ref, x_hbm, dx1_hbm, gain_ref, dgain_ref, *refs):
    (own_ref, *other_refs, keep_ref, send_ref,
     first_s, second_s, turned_s, wide_s, back_s, x_ref, dx1_ref, sems) = refs[-13:]
    me, side = place_ref[0], place_ref[1]
    step = pl.program_id(0)
    rows, width = n1_ref.shape
    copies = [
        pltpu.make_async_copy(x_hbm, x_ref, sems.at[0]),
        pltpu.make_async_copy(dx1_hbm, dx1_ref, sems.at[1]),
    ]

    @pl.when(step == 0)
    def _():
        for copy in copies:
            copy.start()
        for i in range(rows // TILE):
            turned_s[:, i * TILE : (i + 1) * TILE] = jnp.transpose(n1_ref[i * TILE : (i + 1) * TILE, :])
        back_s[...] = jnp.zeros_like(back_s)

    back_s[...] += nt(first_ref[...], w_ref[0]) + nt(second_ref[...], w_ref[1])
    first_s[...] = nn(turned_s[...], first_ref[...])
    second_s[...] = nn(turned_s[...], second_ref[...])
    lanes = pl.ds(pl.multiple_of(step * TRIPLE, 128), TRIPLE)
    file_devices(keep_ref, send_ref, me, side, lanes, (first_s, second_s))

    @pl.when(step == pl.num_programs(0) - 1)
    def _():
        for copy in copies:
            copy.wait()
        total = jnp.zeros((1, width), F32)
        for i in range(rows // TILE):
            at = slice(i * TILE, (i + 1) * TILE)
            back = back_s[at, :]
            x = x_ref[at, :].astype(F32)
            root = lax.rsqrt(jnp.mean(x * x, -1, keepdims=True) + EPS)
            unit = x * root
            total += jnp.sum(back * unit, 0, keepdims=True)
            lifted = back * gain_ref[0:1, :]
            inner = jnp.mean(lifted * unit, -1, keepdims=True)
            d_x = dx1_ref[at, :] + root * (lifted - unit * inner)
            start = i * TILE - rows // 2
            if start < 0:
                own_ref[at, :] = d_x
            else:
                other_refs[start // TILE][...] = d_x.astype(BF16)
        for row, part in ((total, first_s), (dgain_ref[0:1, :], second_s)):
            wide_s[...] = jnp.zeros_like(wide_s)
            wide_s[0:1, :] = row
            part[:, :128] = jnp.transpose(wide_s[...])
        last = keep_ref.shape[2] - 128
        sources = [part.at[:, pl.ds(0, 128)] for part in (first_s, second_s)]
        file_devices(keep_ref, send_ref, me, side, slice(last, last + 128), sources)


def project_back(place, d_qkv, n1, weights, x, d_x1, gains, d_gain, kept, ready=()):
    rows, width = n1.shape
    steps = width // PAIR // 2
    return pl.pallas_call(
        project_back_kernel,
        grid=(steps,),
        in_specs=[
            SCALARS,
            pl.BlockSpec((rows, TRIPLE), lambda i: (0, i)),
            pl.BlockSpec((rows, TRIPLE), lambda i: (0, steps + i)),
            whole((rows, width)),
            pl.BlockSpec((2, width, TRIPLE), lambda i: (0, 0, i)),
            APART,
            APART,
            whole(gains.shape),
            whole((8, width)),
        ]
        + [APART] * len(ready),
        out_specs=[whole((rows // 2, width))] + [whole((TILE, width))] * 2 + [whole(kept)] * 2,
        out_shape=[
            jax.ShapeDtypeStruct((rows // 2, width), F32),
            jax.ShapeDtypeStruct((TILE, width), BF16),
            jax.ShapeDtypeStruct((TILE, width), BF16),
            jax.ShapeDtypeStruct(kept, BF16),
            jax.ShapeDtypeStruct(kept, BF16),
        ],
        scratch_shapes=[
            pltpu.VMEM((width, TRIPLE), F32),
            pltpu.VMEM((width, TRIPLE), F32),
            pltpu.VMEM((width, rows), BF16),
            pltpu.VMEM((128, width), F32),
            pltpu.VMEM((rows, width), F32),
            pltpu.VMEM((rows, width), BF16),
            pltpu.VMEM((rows, width), F32),
            pltpu.SemaphoreType.DMA((2,)),
        ],
        compiler_params=params(),
        cost_estimate=pl.CostEstimate(
            flops=24 * rows * width * width, bytes_accessed=40 * rows * width, transcendentals=0
        ),
        name="project_back",
    )(place, d_qkv, d_qkv, n1, weights, x, d_x1, gains, d_gain, *ready)


def give_half(plots, side):
    own = lax.dynamic_index_in_dim(plots, side, 0, keepdims=False)
    return own, lax.dynamic_index_in_dim(plots, 1 - side, 0, keepdims=False)


def halves_back(own, arrived, side):
    arrived = arrived.astype(own.dtype)
    return jnp.stack([by_side(side, own, arrived), by_side(side, arrived, own)])


CALLS = (3, 2, 1)


def local_fast(size, *arguments):
    (inputs, out_grad, source_id, source_weight, gain_attn, gain_mlp,
     w_query, w_key, w_value, w_attn_out, w_gate, w_up, w_down) = arguments
    half_rows, width = inputs.shape[1:]
    half = width // 2
    hidden = w_gate.shape[1]
    groups = size // 4
    side = lax.axis_index("narrow")
    place = jnp.stack([lax.axis_index("wide"), side]).astype(jnp.int32)

    pairs = width // PAIR
    unit_a, unit_b, give = pack(
        place, (gain_attn, gain_mlp), (w_query, w_key, w_value), (w_attn_out, w_gate, w_up)
    )
    stack_a = spread_z(unit_a, size)
    unit_b = pair_up(unit_b, give, side)
    unit_c = pair_up(w_down, after(w_down, unit_a), side)
    quarter = half_rows // 2
    own_x, give_x = give_half(after(inputs, unit_a), side)
    short = quarter // 2
    others = [swap_x(give_x[:short])]
    stack_a, unit_b, unit_c, others[0] = lax.optimization_barrier((stack_a, unit_b, unit_c, others[0]))
    x_a, y_a = spread_xy(stack_a, size)
    units_b = [unit_b, None, swap(unit_b, 8, size)]
    near_c = swap(unit_c, 4, size)
    x_a, y_a, units_b[2], near_c = lax.optimization_barrier((x_a, y_a, units_b[2], near_c))
    d_a = swap(x_a, 2, size)
    others.append(swap_x(after(give_x[short:], x_a)))
    unit_b = after(unit_b, y_a)
    units_b[1] = swap(unit_b, 4, size)
    units_b += [swap(unit_b, 4 * k, size) for k in range(3, groups)]
    d_a, others[1], units_b[1], *units_b[3:] = lax.optimization_barrier((d_a, others[1], units_b[1], *units_b[3:]))
    pieces_a = [stack_a, x_a, y_a, d_a]
    own_grad, give_grad = give_half(after(out_grad, x_a), side)
    grads = [own_grad, swap_x(give_grad[:quarter]), swap_x(after(give_grad[quarter:], d_a))]
    pieces_a += [swap(piece, 1, size) for piece in pieces_a]

    stack_b = jnp.stack(units_b)
    unit_c = after(unit_c, *pieces_a[4:])
    units_c = [unit_c, near_c] + [swap(unit_c, 4 * k, size) for k in range(2, groups)]
    qkv, n1, gains, weights = project(place, own_x, others, pieces_a, [stack_b])
    x_b, y_b = spread_xy(stack_b, size)
    heads, lses = [], []
    for call, count in enumerate(CALLS):
        ready = [[grads[1]], [*heads, y_b, *units_c], [*heads, grads[2]]][call]
        made = attend_fast(qkv, sum(CALLS[:call]), count, ready)
        heads.append(made[0])
        lses.append(made[1])
        if call == 0:
            y_b, stack_b, *units_c = lax.optimization_barrier((y_b, stack_b, *units_c, heads[-1]))[:-1]
            d_b = swap_x(y_b)
            stack_c = jnp.stack(units_c)
            y_c = swap(stack_c, 2, size)
            twins_b = [swap(stack_b, 1, size), swap(y_b, 1, size)]
            twins_c = [swap(stack_c, 1, size)]
    x = jnp.concatenate(lax.optimization_barrier((own_x, *others, heads[-1]))[:3], 0)
    x_b, d_b, y_c, _ = lax.optimization_barrier((x_b, d_b, y_c, heads[-1]))
    pieces_b = [stack_b, x_b, y_b, d_b]
    pieces_b += [twins_b[0], swap(x_b, 1, size), twins_b[1], swap(d_b, 1, size)]
    pieces_c = [stack_c, y_c, *twins_c, swap(y_c, 1, size)]
    acts, other_acts, d_x1, d_out, keep, send, keep_c, send_c, d_gain = mlp(
        place, source_id, source_weight, heads, x, grads, gains, pieces_b, pieces_c
    )

    twin = swap(send, 1, size)
    twin_c = swap(send_c, 1, size)
    other_acts = swap_x(other_acts)
    d_qkv = None
    ready = []
    for call in reversed(range(len(CALLS))):
        start = sum(CALLS[:call])
        d_qkv, token = attend_back_fast(qkv, d_out, heads[call], lses[call], start, d_qkv, ready)
        if call == 2:
            twin, twin_c = lax.optimization_barrier((twin, twin_c, token))[:2]
            diagonal, over_y = diagonal_of(keep, twin), over_y_of(keep, twin)
            corner = swap(diagonal, 2, size)
            by_y = swap(after(over_y, diagonal), 2, size)
            ready = [diagonal, over_y, token]
        elif call == 1:
            over_y_c = chip_sum(keep_c, after(twin_c, token), 1, 2).astype(BF16)
            twin, other_acts, corner, over_y_c = lax.optimization_barrier((twin, other_acts, corner, over_y_c, token))[:4]
            over_x = over_x_of(keep, twin, corner)
            by_x = swap_x(over_x)
            ready = [over_x, token, other_acts, over_y_c]
    twin, by_x, by_y = lax.optimization_barrier((twin, by_x, by_y, token))[:3]
    sides = (by_x, by_y)
    far = [unit.astype(BF16) for unit in collect_own(keep, twin, sides, range(1, groups))]
    arrived_c = swap(after(over_y_c, by_y), 2, size)
    kept = (4 * groups, *unit_a.shape)
    arrived = [swap(far[k - 1], 4 * k, size) for k in range(1, groups)]
    own, *other, keep_a, send_a = project_back(
        place, d_qkv, n1, weights, x, d_x1, gains, d_gain, kept, [*far, over_y_c]
    )
    others = [swap_x(other[0])]
    send_a, arrived_c, *arrived = lax.optimization_barrier((send_a, arrived_c, *arrived))
    twin_a = swap(send_a, 1, size)
    diagonal = diagonal_of(keep_a, twin_a)
    corner = swap(diagonal, 2, size)
    keep, twin, by_x, by_y, keep_c, twin_c, arrived_c = lax.optimization_barrier(
        (keep, twin, by_x, by_y, keep_c, twin_c, arrived_c, diagonal)
    )[:7]
    total_c = chip_sum(keep_c, twin_c, 0, 2) + arrived_c.astype(F32)
    far_c = [swap(total_c[k].astype(BF16), 4 * k, size) for k in range(1, groups)]
    total_b = sum([part.astype(F32) for part in arrived], collect_own(keep, twin, (by_x, by_y), [0])[0])
    others.append(swap_x(after(other[1], total_b)))
    first_b, second_b = settle(total_b, side)
    twin_a, corner, first_b, others[0] = lax.optimization_barrier((twin_a, corner, first_b, others[0]))
    sides = [swap_x(over_x_of(keep_a, twin_a, corner)), swap(over_y_of(keep_a, twin_a), 2, size)]
    twin_a, *rest = lax.optimization_barrier((twin_a, *sides, *far_c))
    sides, far_c = rest[:2], rest[2:]
    units = collect_own(keep_a, twin_a, sides, range(groups))
    arrived = [swap(units[k].astype(BF16), 4 * k, size) for k in range(1, groups)]
    far_c[-1] = after(far_c[-1], units[0])
    other_acts = after(other_acts, units[0])
    activations = halves_back(acts, other_acts, side)
    grad_down = settle_rows(sum([part.astype(F32) for part in far_c], total_c[0]), side)
    others[1] = after(others[1], grad_down)
    input_grad = halves_back(own, jnp.concatenate(others, 0), side)
    arrived[0], grad_down = lax.optimization_barrier((arrived[0], grad_down))
    total_a = sum([part.astype(F32) for part in arrived], units[0])
    own_rows = unit_a.shape[0] // 2
    first_a, second_a = total_a[:own_rows], total_a[own_rows:]

    def in_order(part):
        return jnp.concatenate(
            [
                piece[:, pair * TRIPLE + part * PAIR : pair * TRIPLE + (part + 1) * PAIR]
                for piece in (first_a, second_a)
                for pair in range(pairs // 2)
            ],
            1,
        )

    def joined(first, second, start, count):
        return jnp.concatenate([first[:, start : start + count], second[:, start : start + count]], 1)

    units = hidden // 2
    return (
        activations,
        input_grad,
        first_a[:, 3 * half],
        second_a[:, 3 * half],
        in_order(0),
        in_order(1),
        in_order(2),
        joined(first_b, second_b, 0, half),
        joined(first_b, second_b, half, units),
        joined(first_b, second_b, half + units, units),
        grad_down,
    )


def solution(mesh):
    size = mesh.shape["wide"]
    fits = mesh.shape["narrow"] == 2 and size == 16
    body = functools.partial(local_fast, size) if fits else local
    placed = (
        P("wide", "narrow", None),
        P("wide", "narrow", None),
        P("wide"),
        P(),
        P(("wide", "narrow")),
        P(("wide", "narrow")),
        P(("wide", "narrow"), None),
        P(("wide", "narrow"), None),
        P(("wide", "narrow"), None),
        P(("wide", "narrow"), None),
        P(("wide", "narrow"), None),
        P(("wide", "narrow"), None),
        P(("wide", "narrow"), None),
    )
    return jax.shard_map(
        body,
        mesh=mesh,
        in_specs=placed,
        out_specs=(
            P("wide", "narrow", None),
            P("wide", "narrow", None),
            P(("wide", "narrow")),
            P(("wide", "narrow")),
            P(("wide", "narrow"), None),
            P(("wide", "narrow"), None),
            P(("wide", "narrow"), None),
            P(("wide", "narrow"), None),
            P(("wide", "narrow"), None),
            P(("wide", "narrow"), None),
            P(("wide", "narrow"), None),
        ),
        check_vma=False,
    )
```
